128 devices in a mesh: wide: 16 (over x, z), mid: 8 (over y, core).
Axes of the slice: x: 4, y: 4, z: 4, core: 2. Of those that a mesh axis runs over, the one named last changes fastest.
Arguments:
- noise: float32 [512, 256, 512], P('wide', 'mid'), may hold values from -6 to 6
- spectrum: float32 [512], replicated, may hold values from 0.3 to 1.2
- send_core: int32 [16, 8, 16], P('wide', 'mid'), may hold values from -1 to 127, as said below
- recv_source: int32 [16, 8, 8], P('wide', 'mid'), may hold values from 0 to 15, as said below
Outputs:
- coefficient: float32 [512, 256, 512], P('wide', 'mid')
- corrector: float32 [16, 8, 8, 48, 2304], P('wide', 'mid')
The draws below stay inside these ranges and needn't reach their ends.
Inputs may be any that keep to these rules, and one draw needn't show every extreme that they name: Every owner has exactly 8 patches, whose sources are distinct devices of its own mid row; device (s, m) sends a core to owner (d, m) exactly when s is among recv_source[d, m], never the same core to two owners, and send_core is -1 otherwise. `recv_source`: listed in no particular order.
All inputs are finite; a program needn't handle non-finite values.
Results may differ from the reference program's by a relative error of at most 0.0003.
Values sent between devices are 32-bit elements; how exact they have to be, the bound alone decides.
No kernel may reach another device: no remote copies, remote signals or barrier semaphores. Data moves between devices by JAX's collectives and lax.ppermute only.
A program may use at most 256 MiB of HBM per device.

```python
import math
import jax
import jax.numpy as jnp
from jax import lax

NX = 512
CY = 32
NZ = 512
CORE = 16
LAYER = 16
PATCH_DEV = 8
ITERS = 2
NY = 256
EDGE = 48
NCORE = 128
N_WIDE = 16
N_MID = 8


def routing_tables(key):
    base = jax.random.fold_in(key, 7)
    first_key, second_key, third_key = jax.random.split(base, 3)
    source_ids = jnp.arange(N_WIDE, dtype=jnp.int32)
    random_part = jax.random.randint(first_key, (N_WIDE, N_MID, N_WIDE), 0, 64)
    source_bias = jax.random.randint(second_key, (1, N_MID, N_WIDE), 0, 4) * 32
    score = (random_part + source_bias) * N_WIDE + source_ids[None, None, :]
    ignored, chosen = lax.top_k(score, PATCH_DEV)
    chosen = chosen.astype(jnp.int32)
    core_ids = jnp.arange(NCORE, dtype=jnp.int32)
    core_score = jax.random.randint(third_key, (N_WIDE, N_MID, NCORE), 0, 1 << 20) * NCORE + core_ids[None, None, :]
    ordering = jnp.argsort(core_score, axis=-1)[:, :, :N_WIDE].astype(jnp.int32)
    picked = jnp.any(chosen[:, :, :, None] == source_ids[None, None, None, :], axis=2)
    sending = jnp.where(jnp.transpose(picked, (2, 1, 0)), ordering, -1).astype(jnp.int32)
    return (sending, chosen)


def draw_send_core(key, part):
    return routing_tables(key)[0]


def draw_recv_source(key, part):
    return routing_tables(key)[1]


def levels(rng, shape, cuts, low, top_value):
    gain = 1.0
    for dim, blocks in cuts:
        draws = jax.random.uniform(jax.random.fold_in(jax.random.fold_in(rng, 6), dim), (blocks,), jnp.float32, low / len(cuts), top_value / len(cuts))
        gain = gain * jnp.repeat(jnp.exp(draws), shape[dim] // blocks).reshape((-1,) + (1,) * (len(shape) - 1 - dim))
    return gain


def normal_values(own_key, shape, spread, reach, cuts=(), held_as=jnp.bfloat16):
    loudness = levels(own_key, shape, cuts, -0.22, 0.18) if cuts else 1.0
    result = jax.random.normal(own_key, shape, jnp.float32) * spread * loudness
    return jnp.minimum(jnp.maximum(result, -reach), reach).astype(held_as)


def setup_inputs(seed: int = 0) -> dict:
    key_list = jax.random.split(jax.random.key(seed), 5)
    noise = normal_values(key_list[0], (NX, NY, NZ), 1.0, 6.0, ((0, 16), (1, 8)), jnp.float32)
    spectrum = jnp.clip(jnp.exp(jax.random.uniform(key_list[1], (NX,), jnp.float32, math.log(0.3), math.log(1.2))), 0.3, 1.2)
    send_core = draw_send_core(jax.random.fold_in(key_list[4], 71), 0)
    recv_source = draw_recv_source(jax.random.fold_in(key_list[4], 71), 0)
    return {"noise": noise, "spectrum": spectrum, "send_core": send_core, "recv_source": recv_source}


REACTION = 1.0
TINY = 1e-6


def face_set(conduct):
    padded = jnp.pad(conduct, 1)
    return (0.5 * (conduct + padded[2:, 1:-1, 1:-1]), 0.5 * (conduct + padded[:-2, 1:-1, 1:-1]),
            0.5 * (conduct + padded[1:-1, 2:, 1:-1]), 0.5 * (conduct + padded[1:-1, :-2, 1:-1]),
            0.5 * (conduct + padded[1:-1, 1:-1, 2:]), 0.5 * (conduct + padded[1:-1, 1:-1, :-2]))


def apply_operator(field, faces):
    padded = jnp.pad(field, 1)
    nearby = (padded[2:, 1:-1, 1:-1], padded[:-2, 1:-1, 1:-1], padded[1:-1, 2:, 1:-1],
              padded[1:-1, :-2, 1:-1], padded[1:-1, 1:-1, 2:], padded[1:-1, 1:-1, :-2])
    diagonal = REACTION + faces[0] + faces[1] + faces[2] + faces[3] + faces[4] + faces[5]
    couple = faces[0] * nearby[0] + faces[1] * nearby[1] + faces[2] * nearby[2]
    couple = couple + faces[3] * nearby[3] + faces[4] * nearby[4] + faces[5] * nearby[5]
    return diagonal * field - couple


def solve_patch(conduct):
    faces = face_set(conduct)
    residual = faces[0] - faces[1]
    direction = residual
    solution = jnp.zeros_like(conduct)
    norm_now = jnp.sum(residual * residual)
    for sweep_index in range(ITERS):
        image = apply_operator(direction, faces)
        alpha = norm_now / (jnp.sum(direction * image) + TINY)
        solution = solution + alpha * direction
        residual = residual - alpha * image
        norm_next = jnp.sum(residual * residual)
        direction = residual + (norm_next / (norm_now + TINY)) * direction
        norm_now = norm_next
    return solution


def reference(noise, spectrum, send_core, recv_source):
    spectral = jnp.fft.fft(noise, axis=0)
    logfield = jnp.real(jnp.fft.ifft(spectrum[:, None, None] * spectral, axis=0)).astype(jnp.float32)
    coefficient = jnp.exp(logfield)
    padded = jnp.pad(coefficient, LAYER)
    cells_x = NX // N_WIDE
    cores_y = CY // CORE
    cores_z = NZ // CORE
    owner_w = jnp.broadcast_to(jnp.arange(N_WIDE, dtype=jnp.int32)[:, None, None], recv_source.shape)
    owner_m = jnp.broadcast_to(jnp.arange(N_MID, dtype=jnp.int32)[None, :, None], recv_source.shape)
    core_id = send_core[recv_source, owner_m, owner_w]
    index_x = core_id // (cores_y * cores_z)
    index_y = (core_id // cores_z) % cores_y
    index_z = core_id % cores_z
    start_x = (recv_source * cells_x + index_x * CORE).astype(jnp.int32).reshape(-1)
    start_y = (owner_m * CY + index_y * CORE).astype(jnp.int32).reshape(-1)
    start_z = (index_z * CORE).astype(jnp.int32).reshape(-1)

    def one_patch(starts):
        block = lax.dynamic_slice(padded, (starts[0], starts[1], starts[2]), (EDGE, EDGE, EDGE))
        return solve_patch(block).reshape(EDGE, EDGE * EDGE)

    solved = lax.map(one_patch, (start_x, start_y, start_z))
    return coefficient, solved.reshape(N_WIDE, N_MID, PATCH_DEV, EDGE, EDGE * EDGE)
```

```python
import math

import jax
import jax.numpy as jnp
import numpy as np
from jax import lax
from jax.experimental import pallas as pl
from jax.experimental.pallas import tpu as pltpu
from jax.sharding import PartitionSpec as P

NX = 512
NZ = 512
CY = 32
CX = 32
CORE = 16
LAYER = 16
WIDE = 16
PATCH_DEV = 8
EDGE = 48
TAPS = 3
LANES = PATCH_DEV * EDGE
SIDE = 128
TINY = 1e-06
F32 = jnp.float32
VMEM_LIMIT = 56 * 1024 * 1024


def params():
    return pltpu.CompilerParams(vmem_limit_bytes=VMEM_LIMIT)


def full(shape):
    return jax.ShapeDtypeStruct(shape, F32)


def split_kernel(in_ref, low_ref, high_ref):
    for w in range(WIDE):
        for t, out_ref in enumerate((low_ref, high_ref)):
            out_ref[w * CX:(w + 1) * CX, :] = in_ref[pl.ds(t * WIDE + w, CX, stride=CY), :]


def split_rows(block):
    return pl.pallas_call(
        split_kernel,
        grid=(NZ // SIDE,),
        in_specs=[pl.BlockSpec((CX * CY, SIDE), lambda j: (0, j))],
        out_specs=[pl.BlockSpec((NX, SIDE), lambda j: (0, j))] * 2,
        out_shape=[full((NX, NZ))] * 2,
        compiler_params=params(),
        cost_estimate=pl.CostEstimate(flops=0, bytes_accessed=8 << 20, transcendentals=0),
        name="split_rows",
    )(block.reshape(CX * CY, NZ))


def join_kernel(low_ref, high_ref, out_ref):
    for w in range(WIDE):
        for t, in_ref in enumerate((low_ref, high_ref)):
            out_ref[pl.ds(t * WIDE + w, CX, stride=CY), :] = in_ref[w * CX:(w + 1) * CX, :]


def join_rows(low, high):
    joined = pl.pallas_call(
        join_kernel,
        grid=(NZ // SIDE,),
        in_specs=[pl.BlockSpec((NX, SIDE), lambda j: (0, j))] * 2,
        out_specs=pl.BlockSpec((CX * CY, SIDE), lambda j: (0, j)),
        out_shape=full((CX * CY, NZ)),
        compiler_params=params(),
        cost_estimate=pl.CostEstimate(flops=0, bytes_accessed=8 << 20, transcendentals=0),
        name="join_rows",
    )(low, high)
    return joined.reshape(CX, CY, NZ)


def filter_kernel(matrix_ref, in_ref, out_ref):
    out_ref[...] = jnp.exp(
        jnp.dot(
            matrix_ref[...],
            in_ref[...],
            precision=lax.Precision.HIGHEST,
            preferred_element_type=F32,
        )
    )


def filter_exp(matrix, lines):
    half = NZ // 2
    return pl.pallas_call(
        filter_kernel,
        grid=(2,),
        in_specs=[
            pl.BlockSpec((NX, NX), lambda j: (0, 0)),
            pl.BlockSpec((NX, half), lambda j: (0, j)),
        ],
        out_specs=pl.BlockSpec((NX, half), lambda j: (0, j)),
        out_shape=full((NX, NZ)),
        compiler_params=params(),
        cost_estimate=pl.CostEstimate(
            flops=12 * NX * NX * NZ, bytes_accessed=3 << 20, transcendentals=NX * NZ
        ),
        name="filter_exp",
    )(matrix, lines)


def window_kernel(table_ref, p0_ref, p1_ref, p2_ref, p3_ref, out_ref, held, sems):
    owner = pl.program_id(0)

    @pl.when(owner == 0)
    def _():
        copies = [
            pltpu.make_async_copy(
                src, held.at[t, pl.ds(LAYER, NX), pl.ds(SIDE, NZ)], sems.at[t]
            )
            for t, src in enumerate((p0_ref, p1_ref, p2_ref, p3_ref))
        ]
        for copy in copies:
            copy.start()
        for t in range(4):
            held[t, 0:LAYER, :] = jnp.zeros((LAYER, NZ + 2 * SIDE), F32)
            held[t, LAYER + NX:, :] = jnp.zeros((LAYER, NZ + 2 * SIDE), F32)
            held[t, LAYER:LAYER + NX, 0:SIDE] = jnp.zeros((NX, SIDE), F32)
            held[t, LAYER:LAYER + NX, SIDE + NZ:] = jnp.zeros((NX, SIDE), F32)
        for copy in copies:
            copy.wait()

    places = []
    for p in range(PATCH_DEV):
        source = table_ref[owner, WIDE + p]
        core = jnp.maximum(table_ref[source, owner], 0)
        x_at = source * CX + (core >> 6) * CORE
        t_at = (core >> 5) & 1
        z_at = (core & 31) * CORE + (SIDE - LAYER)
        tile = pl.multiple_of((z_at >> 7) * SIDE, SIDE)
        offset = z_at & (SIDE - 1)
        turn = ((p * EDGE) % SIDE - offset) & (SIDE - 1)
        places.append((pl.multiple_of(x_at, CORE), t_at, tile, offset, turn))
    lane = lax.broadcasted_iota(jnp.int32, (EDGE, SIDE), 1)
    for t in range(TAPS):
        tiles = [None] * 3
        for p, (x_at, t_at, tile, offset, turn) in enumerate(places):
            rows = pl.ds(x_at, EDGE)
            first = held[t_at + t, rows, pl.ds(tile, SIDE)]
            second = held[t_at + t, rows, pl.ds(pl.multiple_of(tile + SIDE, SIDE), SIDE)]
            moved = pltpu.roll(jnp.where(lane >= offset, first, second), turn, 1)
            at = (p * EDGE) % SIDE
            q = (p * EDGE) // SIDE
            tiles[q] = moved if at == 0 else jnp.where(lane >= at, moved, tiles[q])
            if at + EDGE > SIDE:
                tiles[q + 1] = moved
        for q in range(3):
            out_ref[t * EDGE:(t + 1) * EDGE, q * SIDE:(q + 1) * SIDE] = tiles[q]


def windows(table, planes):
    rows = TAPS * EDGE
    return pl.pallas_call(
        window_kernel,
        grid_spec=pltpu.PrefetchScalarGridSpec(
            num_scalar_prefetch=1,
            grid=(WIDE,),
            in_specs=[pl.BlockSpec(memory_space=pl.ANY)] * 4,
            out_specs=pl.BlockSpec((None, rows, LANES), lambda d, table: (d, 0, 0)),
            scratch_shapes=[
                pltpu.VMEM((4, NX + 2 * LAYER, NZ + 2 * SIDE), F32),
                pltpu.SemaphoreType.DMA((4,)),
            ],
        ),
        out_shape=full((WIDE, rows, LANES)),
        compiler_params=params(),
        cost_estimate=pl.CostEstimate(flops=0, bytes_accessed=16 << 20, transcendentals=0),
        name="patch_windows",
    )(table, *planes)


def solve_kernel(kappa_ref, out_ref, first, image):
    row = lax.broadcasted_iota(jnp.int32, (EDGE, LANES), 0)
    lane = lax.broadcasted_iota(jnp.int32, (EDGE, LANES), 1)
    depth = lane - ((lane * 1366) >> 16) * EDGE
    x_low, x_high = row == 0, row == EDGE - 1
    z_low, z_high = depth == 0, depth == EDGE - 1
    zero = jnp.zeros((EDGE, LANES), F32)

    def above_x(v):
        return jnp.where(x_high, 0.0, pltpu.roll(v, EDGE - 1, 0))

    def above_z(v):
        return jnp.where(z_high, 0.0, pltpu.roll(v, LANES - 1, 1))

    def half_kappa(y):
        t, w = y >> 4, y & 15
        rows = pl.ds(pl.multiple_of(t * EDGE, EDGE), EDGE)
        return 0.5 * kappa_ref[w, rows, :]

    def upper(y):
        above = half_kappa(jnp.minimum(y + 1, EDGE - 1))
        return jnp.where(y + 1 < EDGE, above, 0.0)

    def rhs_of(h):
        below = jnp.where(x_low, 0.0, pltpu.roll(h, 1, 0))
        return above_x(h) - below

    def fold(v):
        return jnp.sum(v.reshape(EDGE // 8, 8, LANES), axis=0)

    seg_a = (lax.broadcasted_iota(jnp.int32, (LANES, LANES), 0) * 1366) >> 16
    seg_b = (lax.broadcasted_iota(jnp.int32, (LANES, LANES), 1) * 1366) >> 16
    same = jnp.where(seg_a == seg_b, 1.0, 0.0).astype(F32)

    def patch_total(part):
        spread = jnp.dot(part, same, precision=lax.Precision.HIGHEST, preferred_element_type=F32)
        return jnp.sum(spread, axis=0, keepdims=True)

    none = jnp.zeros((8, LANES), F32)

    def first_pass(y, carry):
        flux_low, h, v, rr, dq = carry
        h_up = upper(y)
        v_up = rhs_of(h_up)
        flux_y = (h + h_up) * (v_up - v)
        flux_x = (h + above_x(h)) * (above_x(v) - v)
        flux_z = (h + above_z(h)) * (above_z(v) - v)
        edge = h * v
        low_x = jnp.where(x_low, edge, pltpu.roll(flux_x, 1, 0))
        low_z = jnp.where(z_low, edge, pltpu.roll(flux_z, 1, 1))
        q = v - (flux_x - low_x) - (flux_y - flux_low) - (flux_z - low_z)
        first[y] = v
        image[y] = q
        return flux_y, h_up, v_up, rr + fold(v * v), dq + fold(v * q)

    h0 = half_kappa(0)
    v0 = rhs_of(h0)
    carry = lax.fori_loop(0, EDGE, first_pass, (h0 * v0, h0, v0, none, none))
    rr = patch_total(carry[3])
    alpha = rr / (patch_total(carry[4]) + TINY)

    def second_pass(y, total):
        left = first[y] - alpha * image[y]
        return total + fold(left * left)

    new = patch_total(lax.fori_loop(0, EDGE, second_pass, none))
    beta = new / (rr + TINY)

    def direction(y):
        return (first[y] - alpha * image[y]) + beta * first[y]

    def third_pass(y, carry):
        h, v, total = carry
        h_up = upper(y)
        v_up = jnp.where(y + 1 < EDGE, direction(jnp.minimum(y + 1, EDGE - 1)), 0.0)
        step_x = above_x(v) - v
        step_y = v_up - v
        step_z = above_z(v) - v
        edges = jnp.where(x_low, h, 0.0) + jnp.where(z_low, h, 0.0) + jnp.where(y == 0, h, 0.0)
        energy = (1.0 + edges) * (v * v)
        energy = energy + (h + above_x(h)) * (step_x * step_x)
        energy = energy + (h + h_up) * (step_y * step_y)
        energy = energy + (h + above_z(h)) * (step_z * step_z)
        return h_up, v_up, total + fold(energy)

    carry = lax.fori_loop(0, EDGE, third_pass, (h0, direction(0), none))
    alpha_next = new / (patch_total(carry[2]) + TINY)
    on_first = alpha + alpha_next * (1.0 + beta)
    on_image = -(alpha_next * alpha)

    chunk = (lax.broadcasted_iota(jnp.int32, (8, LANES), 1) * 1366) >> 16
    bits = [(chunk & (1 << b)) != 0 for b in range(3)]

    def last_pass(step, _):
        group, tile = step // 6, step % 6
        rows = pl.ds(pl.multiple_of(tile * 8, 8), 8)
        lines = []
        for j in range(8):
            y = group * 8 + j
            lines.append(on_first * first[y, rows, :] + on_image * image[y, rows, :])
        for b in range(3):
            hop = EDGE << b
            fresh = [None] * 8
            for j in range(8):
                if j & (1 << b):
                    continue
                k = j | (1 << b)
                fresh[j] = jnp.where(bits[b], pltpu.roll(lines[k], hop, 1), lines[j])
                fresh[k] = jnp.where(bits[b], lines[k], pltpu.roll(lines[j], LANES - hop, 1))
            lines = fresh
        columns = pl.ds(pl.multiple_of(group * LANES, LANES), LANES)
        for p in range(8):
            out_ref[p, rows, columns] = lines[p]
        return 0

    lax.fori_loop(0, 36, last_pass, 0)


def solve(kappa):
    return pl.pallas_call(
        solve_kernel,
        in_specs=[pl.BlockSpec(memory_space=pltpu.VMEM)],
        out_specs=pl.BlockSpec(memory_space=pltpu.VMEM),
        out_shape=full((PATCH_DEV, EDGE, EDGE * EDGE)),
        scratch_shapes=[pltpu.VMEM((EDGE, EDGE, LANES), F32)] * 2,
        compiler_params=params(),
        cost_estimate=pl.CostEstimate(
            flops=60 * EDGE**3 * PATCH_DEV, bytes_accessed=32 << 20, transcendentals=0
        ),
        name="solve_patches",
    )(kappa)


def wave_tables():
    index = np.arange(NX, dtype=np.int64)
    angle = (index[:, None] * index[None, :] % NX) * (2.0 * math.pi / NX)
    waves = np.concatenate([np.cos(angle), np.sin(angle)], axis=0)
    return waves.astype(np.float32)


def on_device(noise, spectrum, send_core, recv_source):
    swap = lambda v: lax.all_to_all(
        v.reshape(WIDE, v.shape[0] // WIDE, v.shape[1]), "wide", split_axis=0, concat_axis=0
    ).reshape(v.shape)
    mine = jnp.concatenate([send_core.reshape(1, WIDE), recv_source.reshape(1, PATCH_DEV)], axis=1)
    table = lax.all_gather(mine, "wide", axis=0, tiled=True)
    low, high = split_rows(noise)
    low, high = swap(low), swap(high)
    waves = jnp.asarray(wave_tables())
    weights = jnp.concatenate([spectrum, spectrum])[:, None] / NX
    matrix = lax.dot_general(
        waves,
        waves * weights,
        (((0,), (0,)), ((), ())),
        precision=lax.Precision.HIGHEST,
        preferred_element_type=F32,
    )
    count = lax.axis_size("mid")
    forward = [(i, i + 1) for i in range(count - 1)]
    backward = [(i + 1, i) for i in range(count - 1)]
    low = filter_exp(matrix, low)
    above = lax.ppermute(low, "mid", backward)
    high = filter_exp(matrix, high)
    below = lax.ppermute(high, "mid", forward)
    out_low, out_high = swap(low), swap(high)
    outgoing = windows(table, (below, low, high, above))
    incoming = lax.all_to_all(outgoing, "wide", split_axis=0, concat_axis=0)
    coefficient = join_rows(out_low, out_high)
    solved = solve(incoming)
    return coefficient, solved.reshape(1, 1, PATCH_DEV, EDGE, EDGE * EDGE)


def solution(mesh):
    in_specs = (P("wide", "mid", None), P(), P("wide", "mid", None), P("wide", "mid", None))
    out_specs = (P("wide", "mid", None), P("wide", "mid", None, None, None))
    return jax.shard_map(
        on_device, mesh=mesh, in_specs=in_specs, out_specs=out_specs, check_vma=False
    )
```

```python
import math

import jax
import jax.numpy as jnp
import numpy as np
from jax import lax
from jax.experimental import pallas as pl
from jax.experimental.pallas import tpu as pltpu
from jax.sharding import PartitionSpec as P

NX = 512
NZ = 512
CY = 32
CX = 32
CORE = 16
LAYER = 16
WIDE = 16
PATCH_DEV = 8
EDGE = 48
TAPS = 3
LANES = PATCH_DEV * EDGE
SIDE = 128
TILES = NZ // SIDE
ROWS = 2 * TILES * CX
TINY = 1e-06
F32 = jnp.float32
VMEM_LIMIT = 56 * 1024 * 1024


def params():
    return pltpu.CompilerParams(vmem_limit_bytes=VMEM_LIMIT)


def full(shape):
    return jax.ShapeDtypeStruct(shape, F32)


def part_rows(t):
    return pl.ds(pl.multiple_of((t * TILES + pl.program_id(0)) * CX, CX), CX)


def split_kernel(in_ref, table_ref, out_ref):
    for w in range(WIDE):
        for t in range(2):
            out_ref[w, part_rows(t), :] = in_ref[pl.ds(t * WIDE + w, CX, stride=CY), :]
        out_ref[w, ROWS:, :] = table_ref[...]


def split_rows(block, table):
    return pl.pallas_call(
        split_kernel,
        grid=(TILES,),
        in_specs=[
            pl.BlockSpec((CX * CY, SIDE), lambda j: (0, j)),
            pl.BlockSpec((8, SIDE), lambda j: (0, 0)),
        ],
        out_specs=pl.BlockSpec((WIDE, ROWS + 8, SIDE), lambda j: (0, 0, 0)),
        out_shape=full((WIDE, ROWS + 8, SIDE)),
        compiler_params=params(),
        cost_estimate=pl.CostEstimate(flops=0, bytes_accessed=8 << 20, transcendentals=0),
        name="split_rows",
    )(block.reshape(CX * CY, NZ), table)


def join_kernel(in_ref, out_ref):
    for w in range(WIDE):
        for t in range(2):
            out_ref[pl.ds(t * WIDE + w, CX, stride=CY), :] = in_ref[w, part_rows(t), :]


def join_rows(parts):
    joined = pl.pallas_call(
        join_kernel,
        grid=(TILES,),
        in_specs=[pl.BlockSpec((WIDE, ROWS, SIDE), lambda j: (0, 0, 0))],
        out_specs=pl.BlockSpec((CX * CY, SIDE), lambda j: (0, j)),
        out_shape=full((CX * CY, NZ)),
        compiler_params=params(),
        cost_estimate=pl.CostEstimate(flops=0, bytes_accessed=8 << 20, transcendentals=0),
        name="join_rows",
    )(parts)
    return joined.reshape(CX, CY, NZ)


def filter_kernel(matrix_ref, in_ref, parts_ref, low_ref, high_ref):
    step = pl.program_id(0)
    lines = jnp.concatenate(
        [in_ref[:, 0:CX, :].reshape(NX, SIDE), in_ref[:, CX:, :].reshape(NX, SIDE)], axis=1
    )
    value = jnp.exp(
        jnp.dot(
            matrix_ref[...],
            lines,
            precision=lax.Precision.HIGHEST,
            preferred_element_type=F32,
        )
    )
    left, right = value[:, :SIDE], value[:, SIDE:]
    parts_ref[:, 0:CX, :] = left.reshape(WIDE, CX, SIDE)
    parts_ref[:, CX:, :] = right.reshape(WIDE, CX, SIDE)

    @pl.when(step < 2)
    def _():
        low_ref[0] = left
        low_ref[1] = right

    @pl.when(step >= 2)
    def _():
        high_ref[0] = left
        high_ref[1] = right


def filter_exp(matrix, lines):
    block = pl.BlockSpec((WIDE, 2 * CX, SIDE), lambda i: (0, i, 0))
    return pl.pallas_call(
        filter_kernel,
        grid=(4,),
        in_specs=[pl.BlockSpec((NX, NX), lambda i: (0, 0)), block],
        out_specs=[
            block,
            pl.BlockSpec((2, NX, SIDE), lambda i: (jnp.minimum(i, 1), 0, 0)),
            pl.BlockSpec((2, NX, SIDE), lambda i: (jnp.maximum(i - 2, 0), 0, 0)),
        ],
        out_shape=[full((WIDE, ROWS, SIDE)), full((TILES, NX, SIDE)), full((TILES, NX, SIDE))],
        compiler_params=params(),
        cost_estimate=pl.CostEstimate(
            flops=24 * NX * NX * NZ, bytes_accessed=7 << 20, transcendentals=2 * NX * NZ
        ),
        name="filter_exp",
    )(matrix, lines)


def window_kernel(table_ref, p0_ref, p1_ref, p2_ref, p3_ref, out_ref, held, sems):
    owner = pl.program_id(0)

    @pl.when(owner == 0)
    def _():
        copies = [
            pltpu.make_async_copy(
                src, held.at[t, pl.ds(1, TILES), pl.ds(LAYER, NX), :], sems.at[t]
            )
            for t, src in enumerate((p0_ref, p1_ref, p2_ref, p3_ref))
        ]
        for copy in copies:
            copy.start()
        side = jnp.zeros((NX + 2 * LAYER, SIDE), F32)
        for t in range(4):
            held[t, 0] = side
            held[t, TILES + 1] = side
            for j in range(TILES):
                held[t, 1 + j, 0:LAYER, :] = side[:LAYER]
                held[t, 1 + j, LAYER + NX:, :] = side[:LAYER]
        for copy in copies:
            copy.wait()

    places = []
    for p in range(PATCH_DEV):
        source = table_ref[owner, WIDE + p]
        core = jnp.maximum(table_ref[source, owner], 0)
        x_at = source * CX + (core >> 6) * CORE
        t_at = (core >> 5) & 1
        z_at = (core & 31) * CORE + (SIDE - LAYER)
        tile = z_at >> 7
        offset = z_at & (SIDE - 1)
        turn = ((p * EDGE) % SIDE - offset) & (SIDE - 1)
        places.append((pl.multiple_of(x_at, CORE), t_at, tile, offset, turn))
    lane = lax.broadcasted_iota(jnp.int32, (EDGE, SIDE), 1)
    for t in range(TAPS):
        tiles = [None] * 3
        for p, (x_at, t_at, tile, offset, turn) in enumerate(places):
            rows = pl.ds(x_at, EDGE)
            first = held[t_at + t, tile, rows, :]
            second = held[t_at + t, tile + 1, rows, :]
            moved = pltpu.roll(jnp.where(lane >= offset, first, second), turn, 1)
            at = (p * EDGE) % SIDE
            q = (p * EDGE) // SIDE
            tiles[q] = moved if at == 0 else jnp.where(lane >= at, moved, tiles[q])
            if at + EDGE > SIDE:
                tiles[q + 1] = moved
        for q in range(3):
            out_ref[t * EDGE:(t + 1) * EDGE, q * SIDE:(q + 1) * SIDE] = tiles[q]


def windows(table, planes):
    rows = TAPS * EDGE
    return pl.pallas_call(
        window_kernel,
        grid_spec=pltpu.PrefetchScalarGridSpec(
            num_scalar_prefetch=1,
            grid=(WIDE,),
            in_specs=[pl.BlockSpec(memory_space=pl.ANY)] * 4,
            out_specs=pl.BlockSpec((None, rows, LANES), lambda d, table: (d, 0, 0)),
            scratch_shapes=[
                pltpu.VMEM((4, TILES + 2, NX + 2 * LAYER, SIDE), F32),
                pltpu.SemaphoreType.DMA((4,)),
            ],
        ),
        out_shape=full((WIDE, rows, LANES)),
        compiler_params=params(),
        cost_estimate=pl.CostEstimate(flops=0, bytes_accessed=16 << 20, transcendentals=0),
        name="patch_windows",
    )(table, *planes)


def solve_kernel(kappa_ref, out_ref, first, image):
    row = lax.broadcasted_iota(jnp.int32, (EDGE, LANES), 0)
    lane = lax.broadcasted_iota(jnp.int32, (EDGE, LANES), 1)
    depth = lane - ((lane * 1366) >> 16) * EDGE
    x_low, x_high = row == 0, row == EDGE - 1
    z_low, z_high = depth == 0, depth == EDGE - 1
    zero = jnp.zeros((EDGE, LANES), F32)

    def above_x(v):
        return jnp.where(x_high, 0.0, pltpu.roll(v, EDGE - 1, 0))

    def above_z(v):
        return jnp.where(z_high, 0.0, pltpu.roll(v, LANES - 1, 1))

    def half_kappa(y):
        t, w = y >> 4, y & 15
        rows = pl.ds(pl.multiple_of(t * EDGE, EDGE), EDGE)
        return 0.5 * kappa_ref[w, rows, :]

    def upper(y):
        above = half_kappa(jnp.minimum(y + 1, EDGE - 1))
        return jnp.where(y + 1 < EDGE, above, 0.0)

    def rhs_of(h):
        below = jnp.where(x_low, 0.0, pltpu.roll(h, 1, 0))
        return above_x(h) - below

    def fold(v):
        return jnp.sum(v.reshape(EDGE // 8, 8, LANES), axis=0)

    seg_a = (lax.broadcasted_iota(jnp.int32, (LANES, LANES), 0) * 1366) >> 16
    seg_b = (lax.broadcasted_iota(jnp.int32, (LANES, LANES), 1) * 1366) >> 16
    same = jnp.where(seg_a == seg_b, 1.0, 0.0).astype(F32)

    def patch_total(part):
        spread = jnp.dot(part, same, precision=lax.Precision.HIGHEST, preferred_element_type=F32)
        return jnp.sum(spread, axis=0, keepdims=True)

    none = jnp.zeros((8, LANES), F32)

    def first_pass(y, carry):
        flux_low, h, v, rr, dq = carry
        h_up = upper(y)
        v_up = rhs_of(h_up)
        flux_y = (h + h_up) * (v_up - v)
        flux_x = (h + above_x(h)) * (above_x(v) - v)
        flux_z = (h + above_z(h)) * (above_z(v) - v)
        edge = h * v
        low_x = jnp.where(x_low, edge, pltpu.roll(flux_x, 1, 0))
        low_z = jnp.where(z_low, edge, pltpu.roll(flux_z, 1, 1))
        q = v - (flux_x - low_x) - (flux_y - flux_low) - (flux_z - low_z)
        first[y] = v
        image[y] = q
        return flux_y, h_up, v_up, rr + fold(v * v), dq + fold(v * q)

    h0 = half_kappa(0)
    v0 = rhs_of(h0)
    carry = lax.fori_loop(0, EDGE, first_pass, (h0 * v0, h0, v0, none, none))
    rr = patch_total(carry[3])
    alpha = rr / (patch_total(carry[4]) + TINY)

    def second_pass(y, total):
        left = first[y] - alpha * image[y]
        return total + fold(left * left)

    new = patch_total(lax.fori_loop(0, EDGE, second_pass, none))
    beta = new / (rr + TINY)

    def direction(y):
        return (first[y] - alpha * image[y]) + beta * first[y]

    def third_pass(y, carry):
        h, v, total = carry
        h_up = upper(y)
        v_up = jnp.where(y + 1 < EDGE, direction(jnp.minimum(y + 1, EDGE - 1)), 0.0)
        step_x = above_x(v) - v
        step_y = v_up - v
        step_z = above_z(v) - v
        edges = jnp.where(x_low, h, 0.0) + jnp.where(z_low, h, 0.0) + jnp.where(y == 0, h, 0.0)
        energy = (1.0 + edges) * (v * v)
        energy = energy + (h + above_x(h)) * (step_x * step_x)
        energy = energy + (h + h_up) * (step_y * step_y)
        energy = energy + (h + above_z(h)) * (step_z * step_z)
        return h_up, v_up, total + fold(energy)

    carry = lax.fori_loop(0, EDGE, third_pass, (h0, direction(0), none))
    alpha_next = new / (patch_total(carry[2]) + TINY)
    on_first = alpha + alpha_next * (1.0 + beta)
    on_image = -(alpha_next * alpha)

    chunk = (lax.broadcasted_iota(jnp.int32, (8, LANES), 1) * 1366) >> 16
    bits = [(chunk & (1 << b)) != 0 for b in range(3)]

    def last_pass(step, _):
        group, tile = step // 6, step % 6
        rows = pl.ds(pl.multiple_of(tile * 8, 8), 8)
        lines = []
        for j in range(8):
            y = group * 8 + j
            lines.append(on_first * first[y, rows, :] + on_image * image[y, rows, :])
        for b in range(3):
            hop = EDGE << b
            fresh = [None] * 8
            for j in range(8):
                if j & (1 << b):
                    continue
                k = j | (1 << b)
                fresh[j] = jnp.where(bits[b], pltpu.roll(lines[k], hop, 1), lines[j])
                fresh[k] = jnp.where(bits[b], lines[k], pltpu.roll(lines[j], LANES - hop, 1))
            lines = fresh
        columns = pl.ds(pl.multiple_of(group * LANES, LANES), LANES)
        for p in range(8):
            out_ref[p, rows, columns] = lines[p]
        return 0

    lax.fori_loop(0, 36, last_pass, 0)


def solve(kappa):
    return pl.pallas_call(
        solve_kernel,
        in_specs=[pl.BlockSpec(memory_space=pltpu.VMEM)],
        out_specs=pl.BlockSpec(memory_space=pltpu.VMEM),
        out_shape=full((PATCH_DEV, EDGE, EDGE * EDGE)),
        scratch_shapes=[pltpu.VMEM((EDGE, EDGE, LANES), F32)] * 2,
        compiler_params=params(),
        cost_estimate=pl.CostEstimate(
            flops=60 * EDGE**3 * PATCH_DEV, bytes_accessed=32 << 20, transcendentals=0
        ),
        name="solve_patches",
    )(kappa)


def wave_tables():
    index = np.arange(NX, dtype=np.int64)
    angle = (index[:, None] * index[None, :] % NX) * (2.0 * math.pi / NX)
    waves = np.concatenate([np.cos(angle), np.sin(angle)], axis=0)
    return waves.astype(np.float32)


def on_device(noise, spectrum, send_core, recv_source):
    swap = lambda v: lax.all_to_all(v, "wide", split_axis=0, concat_axis=0)
    mine = jnp.concatenate([send_core.reshape(1, WIDE), recv_source.reshape(1, PATCH_DEV)], axis=1)
    mine = jnp.pad(mine.astype(F32), ((0, 7), (0, SIDE - mine.shape[1])))
    lines = swap(split_rows(noise, mine))
    table = lines[:, ROWS, :WIDE + PATCH_DEV].astype(jnp.int32)
    waves = jnp.asarray(wave_tables())
    weights = jnp.concatenate([spectrum, spectrum])[:, None] / NX
    matrix = lax.dot_general(
        waves,
        waves * weights,
        (((0,), (0,)), ((), ())),
        precision=lax.Precision.HIGHEST,
        preferred_element_type=F32,
    )
    count = lax.axis_size("mid")
    forward = [(i, i + 1) for i in range(count - 1)]
    backward = [(i + 1, i) for i in range(count - 1)]
    parts, low, high = filter_exp(matrix, lines)
    above = lax.ppermute(low, "mid", backward)
    below = lax.ppermute(high, "mid", forward)
    coefficient = join_rows(swap(parts))
    outgoing = windows(table, (below, low, high, above))
    incoming = swap(outgoing)
    solved = solve(incoming)
    return coefficient, solved.reshape(1, 1, PATCH_DEV, EDGE, EDGE * EDGE)


def solution(mesh):
    in_specs = (P("wide", "mid", None), P(), P("wide", "mid", None), P("wide", "mid", None))
    out_specs = (P("wide", "mid", None), P("wide", "mid", None, None, None))
    return jax.shard_map(
        on_device, mesh=mesh, in_specs=in_specs, out_specs=out_specs, check_vma=False
    )
```

```python
import math

import jax
import jax.numpy as jnp
import numpy as np
from jax import lax
from jax.experimental import pallas as pl
from jax.experimental.pallas import tpu as pltpu
from jax.sharding import PartitionSpec as P

NX = 512
NZ = 512
CY = 32
CX = 32
CORE = 16
LAYER = 16
WIDE = 16
PATCH_DEV = 8
EDGE = 48
TAPS = 3
LANES = PATCH_DEV * EDGE
SIDE = 128
TILES = NZ // SIDE
ROWS = 2 * TILES * CX
TINY = 1e-06
F32 = jnp.float32
VMEM_LIMIT = 56 * 1024 * 1024


def params():
    return pltpu.CompilerParams(vmem_limit_bytes=VMEM_LIMIT)


def full(shape):
    return jax.ShapeDtypeStruct(shape, F32)


def exchange(pieces):
    row = lax.broadcasted_iota(jnp.int32, pieces[0].shape, 0)
    pieces = list(pieces)
    for bit in (4, 2, 1):
        upper = (row & bit) != 0
        for i in range(8):
            k = i | bit
            if i == k:
                continue
            pieces[i], pieces[k] = (
                jnp.where(upper, pltpu.roll(pieces[k], bit, 0), pieces[i]),
                jnp.where(upper, pieces[k], pltpu.roll(pieces[i], 8 - bit, 0)),
            )
    return pieces


def split_kernel(in_ref, send_ref, source_ref, out_ref, held, sems):
    j = pl.program_id(0)

    def leave(t, tile):
        rows = pl.ds(pl.multiple_of((t * TILES + tile) * CX, CX), CX)
        return pltpu.make_async_copy(held.at[:, rows, :], out_ref.at[:, rows, :], sems.at[t, tile])

    def leave_tables():
        rows = pl.ds(ROWS, 8)
        return pltpu.make_async_copy(held.at[:, rows, :], out_ref.at[:, rows, :], sems.at[2, 0])

    @pl.when(j == 0)
    def _():
        for w in range(WIDE):
            held[w, ROWS:ROWS + 1, 0:WIDE] = send_ref[...].astype(F32)
            held[w, ROWS + 1:ROWS + 2, 0:PATCH_DEV] = source_ref[...].astype(F32)
        leave_tables().start()

    for t in range(2):
        first = pl.multiple_of((t * TILES + j) * CX, CX)
        for x in range(0, CX, 8):
            for y in range(0, WIDE, 8):
                at = t * WIDE + y
                pieces = exchange([in_ref[x + i, at:at + 8, :] for i in range(8)])
                for i in range(8):
                    held[y + i, pl.ds(first + x, 8), :] = pieces[i]
        leave(t, j).start()

    @pl.when(j == TILES - 1)
    def _():
        leave_tables().wait()
        for t in range(2):
            for tile in range(TILES):
                leave(t, tile).wait()


def split_rows(block, send, source):
    return pl.pallas_call(
        split_kernel,
        grid=(TILES,),
        in_specs=[
            pl.BlockSpec((CX, CY, SIDE), lambda j: (0, 0, j)),
            pl.BlockSpec((1, WIDE), lambda j: (0, 0)),
            pl.BlockSpec((1, PATCH_DEV), lambda j: (0, 0)),
        ],
        out_specs=pl.BlockSpec(memory_space=pl.ANY),
        out_shape=full((WIDE, ROWS + 8, SIDE)),
        scratch_shapes=[
            pltpu.VMEM((WIDE, ROWS + 8, SIDE), F32),
            pltpu.SemaphoreType.DMA((3, TILES)),
        ],
        compiler_params=params(),
        cost_estimate=pl.CostEstimate(flops=0, bytes_accessed=8 << 20, transcendentals=0),
        name="split_rows",
    )(block, send, source)


def join_kernel(in_ref, *refs):
    out_ref = refs[-1]
    for x in range(0, CX, 8):
        for y in range(0, WIDE, 8):
            pieces = exchange([in_ref[y + i, x:x + 8, :] for i in range(8)])
            for i in range(8):
                out_ref[x + i, y:y + 8, :] = pieces[i]


def join_rows(t, parts, *others):
    return pl.pallas_call(
        join_kernel,
        grid=(TILES,),
        in_specs=[pl.BlockSpec((WIDE, CX, SIDE), lambda j: (0, j, 0))]
        + [pl.BlockSpec(memory_space=pl.ANY)] * len(others),
        out_specs=pl.BlockSpec((CX, WIDE, SIDE), lambda j: (0, t, j)),
        out_shape=full((CX, CY, NZ)),
        input_output_aliases={1: 0} if others else {},
        compiler_params=params(),
        cost_estimate=pl.CostEstimate(flops=0, bytes_accessed=4 << 20, transcendentals=0),
        name="join_rows",
    )(parts, *others)


def pair_kernel(in_ref, high_ref, low_ref):
    value = in_ref[...]
    high = value.astype(jnp.bfloat16)
    high_ref[...] = high
    low_ref[...] = (value - high.astype(F32)).astype(jnp.bfloat16)


def bf16_pair(matrix):
    return pl.pallas_call(
        pair_kernel,
        out_shape=[jax.ShapeDtypeStruct((NX, NX), jnp.bfloat16)] * 2,
        compiler_params=params(),
        cost_estimate=pl.CostEstimate(flops=0, bytes_accessed=2 << 20, transcendentals=0),
        name="bf16_pair",
    )(matrix)


def filter_kernel(high_ref, low_ref, in_ref, parts_ref, plane_ref):
    lines = jnp.concatenate(
        [in_ref[:, 0:CX, :].reshape(NX, SIDE), in_ref[:, CX:, :].reshape(NX, SIDE)], axis=1
    )
    high = lines.astype(jnp.bfloat16)
    low = (lines - high.astype(F32)).astype(jnp.bfloat16)
    dot = lambda a, b: jnp.dot(a, b, preferred_element_type=F32)
    small = dot(high_ref[...], low) + dot(low_ref[...], high)
    value = jnp.exp(dot(high_ref[...], high) + small)
    for k in range(2):
        side = value[:, k * SIDE:(k + 1) * SIDE]
        parts_ref[:, k * CX:(k + 1) * CX, :] = side.reshape(WIDE, CX, SIDE)
        plane_ref[k] = 0.5 * side


def filter_exp(t, pair, lines):
    whole = pl.BlockSpec((NX, NX), lambda i: (0, 0))
    return pl.pallas_call(
        filter_kernel,
        grid=(2,),
        in_specs=[whole, whole, pl.BlockSpec((WIDE, 2 * CX, SIDE), lambda i: (0, 2 * t + i, 0))],
        out_specs=[
            pl.BlockSpec((WIDE, 2 * CX, SIDE), lambda i: (0, i, 0)),
            pl.BlockSpec((2, NX, SIDE), lambda i: (i, 0, 0)),
        ],
        out_shape=[full((WIDE, TILES * CX, SIDE)), full((TILES, NX, SIDE))],
        compiler_params=params(),
        cost_estimate=pl.CostEstimate(
            flops=6 * NX * NX * NZ, bytes_accessed=4 << 20, transcendentals=NX * NZ
        ),
        name="filter_exp",
    )(*pair, lines)


def window_kernel(table_ref, p0_ref, p1_ref, p2_ref, p3_ref, out_ref, held, sems):
    owner = pl.program_id(0)

    @pl.when(owner == 0)
    def _():
        copies = [
            pltpu.make_async_copy(
                src, held.at[t, pl.ds(1, TILES), pl.ds(LAYER, NX), :], sems.at[t]
            )
            for t, src in enumerate((p0_ref, p1_ref, p2_ref, p3_ref))
        ]
        for copy in copies:
            copy.start()
        side = jnp.zeros((NX + 2 * LAYER, SIDE), F32)
        for t in range(4):
            held[t, 0] = side
            held[t, TILES + 1] = side
            for j in range(TILES):
                held[t, 1 + j, 0:LAYER, :] = side[:LAYER]
                held[t, 1 + j, LAYER + NX:, :] = side[:LAYER]
        for copy in copies:
            copy.wait()

    places = []
    for p in range(PATCH_DEV):
        source = table_ref[owner, WIDE + p]
        core = jnp.maximum(table_ref[source, owner], 0)
        x_at = source * CX + (core >> 6) * CORE
        t_at = (core >> 5) & 1
        z_at = (core & 31) * CORE + (SIDE - LAYER)
        tile = z_at >> 7
        offset = z_at & (SIDE - 1)
        turn = ((p * EDGE) % SIDE - offset) & (SIDE - 1)
        places.append((pl.multiple_of(x_at, CORE), t_at, tile, offset, turn))
    lane = lax.broadcasted_iota(jnp.int32, (EDGE, SIDE), 1)
    for t in range(TAPS):
        tiles = [None] * 3
        for p, (x_at, t_at, tile, offset, turn) in enumerate(places):
            rows = pl.ds(x_at, EDGE)
            first = held[t_at + t, tile, rows, :]
            second = held[t_at + t, tile + 1, rows, :]
            moved = pltpu.roll(jnp.where(lane >= offset, first, second), turn, 1)
            at = (p * EDGE) % SIDE
            q = (p * EDGE) // SIDE
            tiles[q] = moved if at == 0 else jnp.where(lane >= at, moved, tiles[q])
            if at + EDGE > SIDE:
                tiles[q + 1] = moved
        for q in range(3):
            out_ref[t * EDGE:(t + 1) * EDGE, q * SIDE:(q + 1) * SIDE] = tiles[q]


def windows(table, planes):
    rows = TAPS * EDGE
    return pl.pallas_call(
        window_kernel,
        grid_spec=pltpu.PrefetchScalarGridSpec(
            num_scalar_prefetch=1,
            grid=(WIDE,),
            in_specs=[pl.BlockSpec(memory_space=pl.ANY)] * 4,
            out_specs=pl.BlockSpec((None, rows, LANES), lambda d, table: (d, 0, 0)),
            scratch_shapes=[
                pltpu.VMEM((4, TILES + 2, NX + 2 * LAYER, SIDE), F32),
                pltpu.SemaphoreType.DMA((4,)),
            ],
        ),
        out_shape=full((WIDE, rows, LANES)),
        compiler_params=params(),
        cost_estimate=pl.CostEstimate(flops=0, bytes_accessed=16 << 20, transcendentals=0),
        name="patch_windows",
    )(table, *planes)


STRIPS = EDGE // 8
GROUPS = EDGE // 8
PIECES = [(i, q) for i in range(STRIPS) for q in range(3)]


def piece(i, q):
    return (pl.ds(8 * i, 8), pl.ds(SIDE * q, SIDE))


def solve_kernel(half_ref, out_ref, half, first, image, heavy, face_x, face_y, face_z, ready, arrive, leave):
    arrivals = [
        pltpu.make_async_copy(
            half_ref.at[:, pl.ds(t * EDGE, EDGE), :], half.at[pl.ds(1 + t * WIDE, WIDE)], arrive.at[t]
        )
        for t in range(TAPS)
    ]
    for copy in arrivals:
        copy.start()
    none = jnp.zeros((8, SIDE), F32)
    for at in PIECES:
        half[0, *piece(*at)] = none
        half[EDGE + 1, *piece(*at)] = none
        first[EDGE, *piece(*at)] = none
        image[EDGE, *piece(*at)] = none

    row = lax.broadcasted_iota(jnp.int32, (8, SIDE), 0)
    lane = lax.broadcasted_iota(jnp.int32, (8, SIDE), 1)
    row_low, row_high = row == 0, row == 7
    lane_low, lane_high = lane == 0, lane == SIDE - 1
    depth = []
    for q in range(3):
        place = lane + q * SIDE
        depth.append(place - ((place * 1366) >> 16) * EDGE)
    z_low = [d == 0 for d in depth]
    z_high = [d == EDGE - 1 for d in depth]

    def above_x(slab):
        turned = {at: pltpu.roll(slab[at], 7, 0) for at in PIECES}
        return {
            (i, q): jnp.where(row_high, turned[i + 1, q] if i < STRIPS - 1 else 0.0, turned[i, q])
            for i, q in PIECES
        }

    def below_x(slab):
        turned = {at: pltpu.roll(slab[at], 1, 0) for at in PIECES}
        return {
            (i, q): jnp.where(row_low, turned[i - 1, q] if i else 0.0, turned[i, q])
            for i, q in PIECES
        }

    def above_z(strip):
        turned = [pltpu.roll(v, SIDE - 1, 1) for v in strip]
        return [
            jnp.where(lane_high, turned[1], turned[0]),
            jnp.where(lane_high, turned[2], turned[1]),
            turned[2],
        ]

    def below_z(strip):
        turned = [pltpu.roll(v, 1, 1) for v in strip]
        return [
            jnp.where(lane_low, 0.0, turned[0]),
            jnp.where(lane_low, turned[0], turned[1]),
            jnp.where(lane_low, turned[1], turned[2]),
        ]

    def load(ref, y):
        return {at: ref[y, *piece(*at)] for at in PIECES}

    def strip(slab, i):
        return [slab[i, q] for q in range(3)]

    same = jnp.where(
        ((lax.broadcasted_iota(jnp.int32, (LANES, LANES), 0) * 1366) >> 16)
        == ((lax.broadcasted_iota(jnp.int32, (LANES, LANES), 1) * 1366) >> 16),
        1.0,
        0.0,
    ).astype(jnp.bfloat16)

    def patch_total(parts):
        part = jnp.concatenate(parts, axis=1)
        high = part.astype(jnp.bfloat16).astype(F32)
        middle = (part - high).astype(jnp.bfloat16).astype(F32)
        low = part - high - middle
        stack = jnp.concatenate([high, middle, low, jnp.zeros_like(low)], axis=0)
        spread = jnp.dot(stack.astype(jnp.bfloat16), same, preferred_element_type=F32)
        total = jnp.sum(spread, axis=0, keepdims=True)
        return [
            jnp.broadcast_to(total[:, SIDE * q:SIDE * (q + 1)], (8, SIDE)) for q in range(3)
        ]

    def divide(top, bottom):
        return [t / (b + TINY) for t, b in zip(top, bottom)]

    nothing = (none, none, none)

    def faces_of(y, rr):
        rr = list(rr)
        h = load(half, y + 1)
        h_up = above_x(h)
        h_down = below_x(h)
        for i in range(STRIPS):
            ups, downs = above_z(strip(h, i)), below_z(strip(h, i))
            for q in range(3):
                here, to = h[i, q], piece(i, q)
                v = h_up[i, q] - h_down[i, q]
                z_up = jnp.where(z_high[q], 0.0, ups[q])
                z_down = jnp.where(z_low[q], 0.0, downs[q])
                y_up = half[y + 2, *to]
                y_down = half[y, *to]
                across = here + h_up[i, q]
                if i == STRIPS - 1:
                    across = jnp.where(row_high, 0.0, across)
                heavy[y, *to] = (
                    (1.0 + 6.0 * here) + (h_up[i, q] + h_down[i, q])
                    + ((y_up + y_down) + (z_up + z_down))
                )
                face_x[y, *to] = across
                face_y[y, *to] = here + y_up
                face_z[y, *to] = jnp.where(z_high[q], 0.0, here + z_up)
                first[y, *to] = v
                rr[q] = rr[q] + v * v
        return tuple(rr)

    rr = nothing
    for t in range(TAPS):
        arrivals[t].wait()
        start = 0 if t == 0 else t * WIDE - 1
        stop = EDGE if t == TAPS - 1 else (t + 1) * WIDE - 1
        rr = lax.fori_loop(start, stop, faces_of, rr)
    for at in PIECES:
        face_y[EDGE - 1, *piece(*at)] = none
        ready[0, *piece(*at)] = none
    rr = patch_total(rr)

    def image_of(y, total):
        total = list(total)
        v = load(first, y)
        v_up = above_x(v)
        across = load(face_x, y)
        from_x = below_x({at: across[at] * v[at] for at in PIECES})
        for i in range(STRIPS):
            deep = [face_z[y, *piece(i, q)] for q in range(3)]
            ups = above_z(strip(v, i))
            downs = below_z([deep[q] * v[i, q] for q in range(3)])
            for q in range(3):
                to = piece(i, q)
                along = face_y[y, *to]
                couple = across[i, q] * v_up[i, q] + from_x[i, q]
                couple = couple + (along * first[y + 1, *to] + ready[0, *to])
                couple = couple + (deep[q] * ups[q] + downs[q])
                result = heavy[y, *to] * v[i, q] - couple
                ready[0, *to] = along * v[i, q]
                image[y, *to] = result
                total[q] = total[q] + v[i, q] * result
        return tuple(total)

    alpha = divide(rr, patch_total(lax.fori_loop(0, EDGE, image_of, nothing)))

    def residual_of(y, total):
        total = list(total)
        for i, q in PIECES:
            left = first[y, *piece(i, q)] - alpha[q] * image[y, *piece(i, q)]
            total[q] = total[q] + left * left
        return tuple(total)

    new = patch_total(lax.fori_loop(0, EDGE, residual_of, nothing))
    beta = divide(new, rr)

    def direction(y, i, q):
        v = first[y, *piece(i, q)]
        return (v - alpha[q] * image[y, *piece(i, q)]) + beta[q] * v

    for at in PIECES:
        ready[0, *piece(*at)] = direction(0, *at)

    def energy_of(y, total):
        total = list(total)
        v = load(ready, 0)
        v_up = above_x(v)
        for i in range(STRIPS):
            ups = above_z(strip(v, i))
            for q in range(3):
                to = piece(i, q)
                y_up = direction(y + 1, i, q)
                ready[0, *to] = y_up
                couple = face_x[y, *to] * v_up[i, q]
                couple = couple + face_y[y, *to] * y_up
                couple = couple + face_z[y, *to] * ups[q]
                total[q] = total[q] + v[i, q] * (heavy[y, *to] * v[i, q] - 2.0 * couple)
        return tuple(total)

    alpha_next = divide(new, patch_total(lax.fori_loop(0, EDGE, energy_of, nothing)))
    on_first = [alpha[q] + alpha_next[q] * (1.0 + beta[q]) for q in range(3)]
    on_image = [-(alpha_next[q] * alpha[q]) for q in range(3)]

    ends = [lane < end for end in (48, 96, 16, 64, 112, 32, 80)]
    departures = []
    for group in range(GROUPS):

        def correct(i, _):
            rows = pl.ds(8*i,8)
            chunks = []
            for j in range(8):
                line = []
                for q in range(3):
                    at = (8 * group + j, rows, pl.ds(SIDE * q, SIDE))
                    line.append(on_first[q] * first[*at] + on_image[q] * image[*at])
                a, b, c = line
                cut = [a, a, jnp.where(ends[1], b, a), b, b, jnp.where(ends[4], c, b), c, c]
                chunks.append(cut)
            for p in range(PATCH_DEV):
                c = []
                for j in range(8):
                    turn = (EDGE * (j - p)) % SIDE
                    c.append(pltpu.roll(chunks[j][p], turn, 1) if turn else chunks[j][p])
                tiles = (
                    jnp.where(ends[0], c[0], jnp.where(ends[1], c[1], c[2])),
                    jnp.where(ends[2], c[2], jnp.where(ends[3], c[3], jnp.where(ends[4], c[4], c[5]))),
                    jnp.where(ends[5], c[5], jnp.where(ends[6], c[6], c[7])),
                )
                for q in range(3):
                    heavy[8 * group + p, rows, pl.ds(SIDE * q, SIDE)] = tiles[q]
            return 0

        [correct(i,0) for i in range(STRIPS)]
        departures.append(
            pltpu.make_async_copy(
                heavy.at[pl.ds(8 * group, PATCH_DEV)],
                out_ref.at[:, :, pl.ds(group * LANES, LANES)],
                leave.at[group],
            )
        )
        departures[-1].start()
    for copy in departures:
        copy.wait()


def solve(half):
    cube = pltpu.VMEM((EDGE, EDGE, LANES), F32)
    longer = pltpu.VMEM((EDGE + 1, EDGE, LANES), F32)
    return pl.pallas_call(
        solve_kernel,
        in_specs=[pl.BlockSpec(memory_space=pl.ANY)],
        out_specs=pl.BlockSpec(memory_space=pl.ANY),
        out_shape=full((PATCH_DEV, EDGE, EDGE * EDGE)),
        scratch_shapes=[
            pltpu.VMEM((EDGE + 2, EDGE, LANES), F32),
            longer,
            longer,
            cube,
            cube,
            cube,
            cube,
            pltpu.VMEM((1, EDGE, LANES), F32),
            pltpu.SemaphoreType.DMA((TAPS,)),
            pltpu.SemaphoreType.DMA((GROUPS,)),
        ],
        compiler_params=params(),
        cost_estimate=pl.CostEstimate(
            flops=60 * EDGE**3 * PATCH_DEV, bytes_accessed=32 << 20, transcendentals=0
        ),
        name="solve_patches",
    )(half)


def wave_tables():
    index = np.arange(NX, dtype=np.int64)
    angle = (index[:, None] * index[None, :] % NX) * (2.0 * math.pi / NX)
    waves = np.concatenate([np.cos(angle), np.sin(angle)], axis=0)
    return waves.astype(np.float32)


def on_device(noise, spectrum, send_core, recv_source):
    swap = lambda v: lax.all_to_all(v, "wide", split_axis=0, concat_axis=0)
    lines = swap(
        split_rows(noise, send_core.reshape(1, WIDE), recv_source.reshape(1, PATCH_DEV))
    )
    table = jnp.concatenate(
        [lines[:, ROWS, :WIDE], lines[:, ROWS + 1, :PATCH_DEV]], axis=1
    ).astype(jnp.int32)
    waves = jnp.asarray(wave_tables())
    weights = jnp.concatenate([spectrum, spectrum])[:, None] / NX
    matrix = lax.dot_general(
        waves,
        waves * weights,
        (((0,), (0,)), ((), ())),
        precision=lax.Precision.HIGHEST,
        preferred_element_type=F32,
    )
    count = lax.axis_size("mid")
    forward = [(i, i + 1) for i in range(count - 1)]
    backward = [(i + 1, i) for i in range(count - 1)]
    pair = bf16_pair(matrix)
    parts_low, low = filter_exp(0, pair, lines)
    parts_high, high = filter_exp(1, pair, lines)
    above = lax.ppermute(low, "mid", backward)
    below = lax.ppermute(high, "mid", forward)
    back_low = swap(parts_low)
    outgoing = windows(table, (below, low, high, above))
    incoming = swap(outgoing)
    coefficient = join_rows(0, back_low)
    incoming, parts_high = lax.optimization_barrier((incoming, parts_high))
    back_high = swap(parts_high)
    solved = solve(incoming)
    coefficient = join_rows(1, back_high, coefficient)
    return coefficient, solved.reshape(1, 1, PATCH_DEV, EDGE, EDGE * EDGE)


def solution(mesh):
    in_specs = (P("wide", "mid", None), P(), P("wide", "mid", None), P("wide", "mid", None))
    out_specs = (P("wide", "mid", None), P("wide", "mid", None, None, None))
    return jax.shard_map(
        on_device, mesh=mesh, in_specs=in_specs, out_specs=out_specs, check_vma=False
    )
```

```python
import functools
import math

import jax
import jax.numpy as jnp
import numpy as np
from jax import lax
from jax.experimental import pallas as pl
from jax.experimental.pallas import tpu as pltpu
from jax.sharding import PartitionSpec as P

NX = 512
NZ = 512
CY = 32
CX = 32
CORE = 16
LAYER = 16
WIDE = 16
PATCH_DEV = 8
EDGE = 48
TAPS = 3
LANES = PATCH_DEV * EDGE
SIDE = 128
TILES = NZ // SIDE
ROWS = 2 * TILES * CX
OWNERS = 4
TINY = 1e-06
F32 = jnp.float32
VMEM_LIMIT = 56 * 1024 * 1024


def params():
    return pltpu.CompilerParams(vmem_limit_bytes=VMEM_LIMIT)


def full(shape):
    return jax.ShapeDtypeStruct(shape, F32)


def exchange(pieces):
    row = lax.broadcasted_iota(jnp.int32, pieces[0].shape, 0)
    pieces = list(pieces)
    for bit in (4, 2, 1):
        upper = (row & bit) != 0
        for i in range(8):
            k = i | bit
            if i == k:
                continue
            pieces[i], pieces[k] = (
                jnp.where(upper, pltpu.roll(pieces[k], bit, 0), pieces[i]),
                jnp.where(upper, pieces[k], pltpu.roll(pieces[i], 8 - bit, 0)),
            )
    return pieces


def split_kernel(in_ref, send_ref, source_ref, out_ref, held, sems):
    j = pl.program_id(0)

    def leave(t, tile):
        rows = pl.ds(pl.multiple_of((t * TILES + tile) * CX, CX), CX)
        return pltpu.make_async_copy(held.at[:, rows, :], out_ref.at[:, rows, :], sems.at[t, tile])

    def leave_tables():
        rows = pl.ds(ROWS, 8)
        return pltpu.make_async_copy(held.at[:, rows, :], out_ref.at[:, rows, :], sems.at[2, 0])

    @pl.when(j == 0)
    def _():
        for w in range(WIDE):
            held[w, ROWS:ROWS + 1, 0:WIDE] = send_ref[...].astype(F32)
            held[w, ROWS + 1:ROWS + 2, 0:PATCH_DEV] = source_ref[...].astype(F32)
        leave_tables().start()

    for t in range(2):
        first = pl.multiple_of((t * TILES + j) * CX, CX)
        for x in range(0, CX, 8):
            for y in range(0, WIDE, 8):
                at = t * WIDE + y
                pieces = exchange([in_ref[x + i, at:at + 8, :] for i in range(8)])
                for i in range(8):
                    held[y + i, pl.ds(first + x, 8), :] = pieces[i]
        leave(t, j).start()

    @pl.when(j == TILES - 1)
    def _():
        leave_tables().wait()
        for t in range(2):
            for tile in range(TILES):
                leave(t, tile).wait()


def split_rows(block, send, source):
    return pl.pallas_call(
        split_kernel,
        grid=(TILES,),
        in_specs=[
            pl.BlockSpec((CX, CY, SIDE), lambda j: (0, 0, j)),
            pl.BlockSpec((1, WIDE), lambda j: (0, 0)),
            pl.BlockSpec((1, PATCH_DEV), lambda j: (0, 0)),
        ],
        out_specs=pl.BlockSpec(memory_space=pl.ANY),
        out_shape=full((WIDE, ROWS + 8, SIDE)),
        scratch_shapes=[
            pltpu.VMEM((WIDE, ROWS + 8, SIDE), F32),
            pltpu.SemaphoreType.DMA((3, TILES)),
        ],
        compiler_params=params(),
        cost_estimate=pl.CostEstimate(flops=0, bytes_accessed=8 << 20, transcendentals=0),
        name="split_rows",
    )(block, send, source)


def join_kernel(low_ref, high_ref, out_ref):
    for t, in_ref in enumerate((low_ref, high_ref)):
        for x in range(0, CX, 8):
            for y in range(0, WIDE, 8):
                pieces = exchange([in_ref[y + i, x:x + 8, :] for i in range(8)])
                for i in range(8):
                    out_ref[x + i, t * WIDE + y:t * WIDE + y + 8, :] = pieces[i]


def join_rows(parts):
    return pl.pallas_call(
        join_kernel,
        grid=(TILES,),
        in_specs=[
            pl.BlockSpec((WIDE, CX, SIDE), lambda j: (0, j, 0)),
            pl.BlockSpec((WIDE, CX, SIDE), lambda j: (0, TILES + j, 0)),
        ],
        out_specs=pl.BlockSpec((CX, CY, SIDE), lambda j: (0, 0, j)),
        out_shape=full((CX, CY, NZ)),
        compiler_params=params(),
        cost_estimate=pl.CostEstimate(flops=0, bytes_accessed=8 << 20, transcendentals=0),
        name="join_rows",
    )(parts, parts)


def pair_kernel(in_ref, high_ref, low_ref):
    value = in_ref[...]
    high = value.astype(jnp.bfloat16)
    high_ref[...] = high
    low_ref[...] = (value - high.astype(F32)).astype(jnp.bfloat16)


def bf16_pair(matrix):
    return pl.pallas_call(
        pair_kernel,
        out_shape=[jax.ShapeDtypeStruct((NX, NX), jnp.bfloat16)] * 2,
        compiler_params=params(),
        cost_estimate=pl.CostEstimate(flops=0, bytes_accessed=2 << 20, transcendentals=0),
        name="bf16_pair",
    )(matrix)


def filter_kernel(high_ref, low_ref, in_ref, *refs):
    parts_ref, plane_ref = refs[-2:]
    lines = jnp.concatenate(
        [in_ref[:, 0:CX, :].reshape(NX, SIDE), in_ref[:, CX:, :].reshape(NX, SIDE)], axis=1
    )
    high = lines.astype(jnp.bfloat16)
    low = (lines - high.astype(F32)).astype(jnp.bfloat16)
    dot = lambda a, b: jnp.dot(a, b, preferred_element_type=F32)
    small = dot(high_ref[...], low) + dot(low_ref[...], high)
    value = jnp.exp(dot(high_ref[...], high) + small)
    for k in range(2):
        side = value[:, k * SIDE:(k + 1) * SIDE]
        parts_ref[:, k * CX:(k + 1) * CX, :] = side.reshape(WIDE, CX, SIDE)
        plane_ref[k] = 0.5 * side


def filter_exp(t, pair, lines, *others):
    whole = pl.BlockSpec((NX, NX), lambda i: (0, 0))
    return pl.pallas_call(
        filter_kernel,
        grid=(2,),
        in_specs=[whole, whole, pl.BlockSpec((WIDE, 2 * CX, SIDE), lambda i: (0, 2 * t + i, 0))]
        + [pl.BlockSpec(memory_space=pl.ANY)] * len(others),
        out_specs=[
            pl.BlockSpec((WIDE, 2 * CX, SIDE), lambda i: (0, 2 * t + i, 0)),
            pl.BlockSpec((2, NX, SIDE), lambda i: (i, 0, 0)),
        ],
        out_shape=[full((WIDE, ROWS, SIDE)), full((TILES, NX, SIDE))],
        input_output_aliases={3: 0} if others else {},
        compiler_params=params(),
        cost_estimate=pl.CostEstimate(
            flops=6 * NX * NX * NZ, bytes_accessed=4 << 20, transcendentals=NX * NZ
        ),
        name="filter_exp",
    )(*pair, lines, *others)


def window_kernel(slots, table_ref, *refs):
    low_ref, high_ref = refs[:2]
    out_ref, held, sems = refs[-3:]
    step = pl.program_id(0)

    @pl.when(step == 0)
    def _():
        copies = [
            pltpu.make_async_copy(
                src, held.at[t, pl.ds(1, TILES), pl.ds(LAYER, NX), :], sems.at[t]
            )
            for t, src in enumerate((low_ref, high_ref))
        ]
        for copy in copies:
            copy.start()
        side = jnp.zeros((NX + 2 * LAYER, SIDE), F32)
        for t in range(2):
            held[t, 0] = side
            held[t, TILES + 1] = side
            for j in range(TILES):
                held[t, 1 + j, 0:LAYER, :] = side[:LAYER]
                held[t, 1 + j, LAYER + NX:, :] = side[:LAYER]
        for copy in copies:
            copy.wait()

    lane = lax.broadcasted_iota(jnp.int32, (EDGE, SIDE), 1)

    def one_owner(k, _):
        owner = step * OWNERS + k
        places = []
        for p in range(PATCH_DEV):
            source = table_ref[owner, WIDE + p]
            core = jnp.maximum(table_ref[source, owner], 0)
            x_at = source * CX + (core >> 6) * CORE
            z_at = (core & 31) * CORE + (SIDE - LAYER)
            offset = z_at & (SIDE - 1)
            turn = ((p * EDGE) % SIDE - offset) & (SIDE - 1)
            places.append((pl.multiple_of(x_at, CORE), (core >> 5) & 1, z_at >> 7, offset, turn))
        for t in range(slots):
            tiles = [None] * 3
            for p, (x_at, t_at, tile, offset, turn) in enumerate(places):
                plane = t if slots == 2 else t_at
                rows = pl.ds(x_at, EDGE)
                near = held[plane, tile, rows, :]
                far = held[plane, tile + 1, rows, :]
                moved = pltpu.roll(jnp.where(lane >= offset, near, far), turn, 1)
                at = (p * EDGE) % SIDE
                q = (p * EDGE) // SIDE
                tiles[q] = moved if at == 0 else jnp.where(lane >= at, moved, tiles[q])
                if at + EDGE > SIDE:
                    tiles[q + 1] = moved
            for q in range(3):
                out_ref[k, t * EDGE:(t + 1) * EDGE, q * SIDE:(q + 1) * SIDE] = tiles[q]
        return 0

    lax.fori_loop(0, OWNERS, one_owner, 0)


def windows(table, planes, *others):
    slots = 1 if others else 2
    at = 2 if others else 0
    return pl.pallas_call(
        functools.partial(window_kernel, slots),
        grid_spec=pltpu.PrefetchScalarGridSpec(
            num_scalar_prefetch=1,
            grid=(WIDE // OWNERS,),
            in_specs=[pl.BlockSpec(memory_space=pl.ANY)] * (2 + len(others)),
            out_specs=pl.BlockSpec((OWNERS, slots * EDGE, LANES), lambda d, table: (d, at, 0)),
            scratch_shapes=[
                pltpu.VMEM((2, TILES + 2, NX + 2 * LAYER, SIDE), F32),
                pltpu.SemaphoreType.DMA((2,)),
            ],
        ),
        out_shape=full((WIDE, TAPS * EDGE, LANES)),
        input_output_aliases={3: 0} if others else {},
        compiler_params=params(),
        cost_estimate=pl.CostEstimate(
            flops=0, bytes_accessed=slots * (6 << 20), transcendentals=0
        ),
        name="patch_windows",
    )(table, *planes, *others)


STRIPS = EDGE // 8
GROUPS = EDGE // 8
PIECES = [(i, q) for i in range(STRIPS) for q in range(3)]


def piece(i, q):
    return (pl.ds(8 * i, 8), pl.ds(SIDE * q, SIDE))


def solve_kernel(
    half_ref, later_ref, out_ref, half, first, image, heavy, face_x, face_y, face_z, ready, arrive, leave
):
    arrivals = [
        pltpu.make_async_copy(
            half_ref.at[:, pl.ds(t * EDGE, EDGE), :], (heavy, face_x, face_y)[t].at[pl.ds(0, WIDE)], arrive.at[t]
        )
        for t in range(TAPS)
    ]
    for copy in arrivals:
        copy.start()
    none = jnp.zeros((8, SIDE), F32)
    for at in PIECES:
        half[0, *piece(*at)] = none
        half[EDGE + 1, *piece(*at)] = none
        first[EDGE, *piece(*at)] = none
        image[EDGE, *piece(*at)] = none

    row = lax.broadcasted_iota(jnp.int32, (8, SIDE), 0)
    lane = lax.broadcasted_iota(jnp.int32, (8, SIDE), 1)
    row_low, row_high = row == 0, row == 7
    lane_low, lane_high = lane == 0, lane == SIDE - 1
    depth = []
    for q in range(3):
        place = lane + q * SIDE
        depth.append(place - ((place * 1366) >> 16) * EDGE)
    z_low = [d == 0 for d in depth]
    z_high = [d == EDGE - 1 for d in depth]

    def above_x(slab):
        turned = {at: pltpu.roll(slab[at], 7, 0) for at in PIECES}
        return {
            (i, q): jnp.where(row_high, turned[i + 1, q] if i < STRIPS - 1 else 0.0, turned[i, q])
            for i, q in PIECES
        }

    def below_x(slab):
        turned = {at: pltpu.roll(slab[at], 1, 0) for at in PIECES}
        return {
            (i, q): jnp.where(row_low, turned[i - 1, q] if i else 0.0, turned[i, q])
            for i, q in PIECES
        }

    def above_z(strip):
        turned = [pltpu.roll(v, SIDE - 1, 1) for v in strip]
        return [
            jnp.where(lane_high, turned[1], turned[0]),
            jnp.where(lane_high, turned[2], turned[1]),
            turned[2],
        ]

    def below_z(strip):
        turned = [pltpu.roll(v, 1, 1) for v in strip]
        return [
            jnp.where(lane_low, 0.0, turned[0]),
            jnp.where(lane_low, turned[0], turned[1]),
            jnp.where(lane_low, turned[1], turned[2]),
        ]

    def load(ref, y):
        return {at: ref[y, *piece(*at)] for at in PIECES}

    def strip(slab, i):
        return [slab[i, q] for q in range(3)]

    same = jnp.where(
        ((lax.broadcasted_iota(jnp.int32, (LANES, LANES), 0) * 1366) >> 16)
        == ((lax.broadcasted_iota(jnp.int32, (LANES, LANES), 1) * 1366) >> 16),
        1.0,
        0.0,
    ).astype(jnp.bfloat16)

    def patch_total(parts):
        part = jnp.concatenate(parts, axis=1)
        high = part.astype(jnp.bfloat16).astype(F32)
        middle = (part - high).astype(jnp.bfloat16).astype(F32)
        low = part - high - middle
        stack = jnp.concatenate([high, middle, low, jnp.zeros_like(low)], axis=0)
        spread = jnp.dot(stack.astype(jnp.bfloat16), same, preferred_element_type=F32)
        total = jnp.sum(spread, axis=0, keepdims=True)
        return [
            jnp.broadcast_to(total[:, SIDE * q:SIDE * (q + 1)], (8, SIDE)) for q in range(3)
        ]

    def divide(top, bottom):
        return [t / (b + TINY) for t, b in zip(top, bottom)]

    nothing = (none, none, none)

    for copy in arrivals:
        copy.wait()
    in_order = [
        jnp.broadcast_to(later_ref[:, SIDE * q:SIDE * (q + 1)], (8, SIDE)) != 0 for q in range(3)
    ]

    def arrange(w, _):
        for i, q in PIECES:
            at = piece(i, q)
            a, b, c = heavy[w, *at], face_x[w, *at], face_y[w, *at]
            half[1 + w, *at] = jnp.where(in_order[q], a, c)
            half[1 + WIDE + w, *at] = jnp.where(in_order[q], b, a)
            half[1 + 2 * WIDE + w, *at] = jnp.where(in_order[q], c, b)
        return 0

    lax.fori_loop(0, WIDE, arrange, 0)

    def faces_of(y, rr):
        rr = list(rr)
        h = load(half, y + 1)
        h_up = above_x(h)
        h_down = below_x(h)
        deep_up, deep_down = {}, {}
        for i in range(STRIPS):
            ups, downs = above_z(strip(h, i)), below_z(strip(h, i))
            for q in range(3):
                deep_up[i, q] = jnp.where(z_high[q], 0.0, ups[q])
                deep_down[i, q] = jnp.where(z_low[q], 0.0, downs[q])
        up_up, up_down = above_x(deep_up), below_x(deep_up)
        down_up, down_down = above_x(deep_down), below_x(deep_down)
        for i, q in PIECES:
            here, to = h[i, q], piece(i, q)
            z_up, z_down = deep_up[i, q], deep_down[i, q]
            v = h_up[i, q] - h_down[i, q]
            y_up = half[y + 2, *to]
            y_down = half[y, *to]
            across = here + h_up[i, q]
            if i == STRIPS - 1:
                across = jnp.where(row_high, 0.0, across)
            deep = here + z_up
            heavy[y, *to] = (
                (1.0 + 6.0 * here) + (h_up[i, q] + h_down[i, q])
                + ((y_up + y_down) + (z_up + z_down))
            )
            face_x[y, *to] = across
            face_y[y, *to] = here + y_up
            face_z[y, *to] = jnp.where(z_high[q], 0.0, deep)
            first[y, *to] = v
            image[y, *to] = deep * (up_up[i, q] - up_down[i, q]) + (here + z_down) * (
                down_up[i, q] - down_down[i, q]
            )
            rr[q] = rr[q] + v * v
        return tuple(rr)

    rr = lax.fori_loop(0, EDGE, faces_of, nothing)
    for at in PIECES:
        face_y[EDGE - 1, *piece(*at)] = none
        ready[0, *piece(*at)] = none
    rr = patch_total(rr)

    def image_of(y, total):
        total = list(total)
        v = load(first, y)
        v_up = above_x(v)
        across = load(face_x, y)
        from_x = below_x({at: across[at] * v[at] for at in PIECES})
        for i, q in PIECES:
            to = piece(i, q)
            along = face_y[y, *to]
            couple = across[i, q] * v_up[i, q] + from_x[i, q]
            couple = couple + (along * first[y + 1, *to] + ready[0, *to])
            result = heavy[y, *to] * v[i, q] - (couple + image[y, *to])
            ready[0, *to] = along * v[i, q]
            image[y, *to] = result
            total[q] = total[q] + v[i, q] * result
        return tuple(total)

    alpha = divide(rr, patch_total(lax.fori_loop(0, EDGE, image_of, nothing)))

    def residual_of(y, total):
        total = list(total)
        for i, q in PIECES:
            left = first[y, *piece(i, q)] - alpha[q] * image[y, *piece(i, q)]
            total[q] = total[q] + left * left
        return tuple(total)

    new = patch_total(lax.fori_loop(0, EDGE, residual_of, nothing))
    beta = divide(new, rr)

    def direction(y, i, q):
        v = first[y, *piece(i, q)]
        return (v - alpha[q] * image[y, *piece(i, q)]) + beta[q] * v

    for at in PIECES:
        ready[0, *piece(*at)] = direction(0, *at)

    def energy_of(y, total):
        total = list(total)
        v = load(ready, 0)
        v_up = above_x(v)
        for i in range(STRIPS):
            ups = above_z(strip(v, i))
            for q in range(3):
                to = piece(i, q)
                y_up = direction(y + 1, i, q)
                ready[0, *to] = y_up
                couple = face_x[y, *to] * v_up[i, q]
                couple = couple + face_y[y, *to] * y_up
                couple = couple + face_z[y, *to] * ups[q]
                total[q] = total[q] + v[i, q] * (heavy[y, *to] * v[i, q] - 2.0 * couple)
        return tuple(total)

    alpha_next = divide(new, patch_total(lax.fori_loop(0, EDGE, energy_of, nothing)))
    on_first = [alpha[q] + alpha_next[q] * (1.0 + beta[q]) for q in range(3)]
    on_image = [-(alpha_next[q] * alpha[q]) for q in range(3)]

    ends = [lane < end for end in (48, 96, 16, 64, 112, 32, 80)]
    departures = []
    for group in range(GROUPS):

        def correct(i, _):
            rows = pl.ds(8*i,8)
            chunks = []
            for j in range(8):
                line = []
                for q in range(3):
                    at = (8 * group + j, rows, pl.ds(SIDE * q, SIDE))
                    line.append(on_first[q] * first[*at] + on_image[q] * image[*at])
                a, b, c = line
                cut = [a, a, jnp.where(ends[1], b, a), b, b, jnp.where(ends[4], c, b), c, c]
                chunks.append(cut)
            for p in range(PATCH_DEV):
                c = []
                for j in range(8):
                    turn = (EDGE * (j - p)) % SIDE
                    c.append(pltpu.roll(chunks[j][p], turn, 1) if turn else chunks[j][p])
                tiles = (
                    jnp.where(ends[0], c[0], jnp.where(ends[1], c[1], c[2])),
                    jnp.where(ends[2], c[2], jnp.where(ends[3], c[3], jnp.where(ends[4], c[4], c[5]))),
                    jnp.where(ends[5], c[5], jnp.where(ends[6], c[6], c[7])),
                )
                for q in range(3):
                    heavy[8 * group + p, rows, pl.ds(SIDE * q, SIDE)] = tiles[q]
            return 0

        [correct(i,0) for i in range(STRIPS)]
        departures.append(
            pltpu.make_async_copy(
                heavy.at[pl.ds(8 * group, PATCH_DEV)],
                out_ref.at[:, :, pl.ds(group * LANES, LANES)],
                leave.at[group],
            )
        )
        departures[-1].start()
    for copy in departures:
        copy.wait()


def solve(half, later):
    cube = pltpu.VMEM((EDGE, EDGE, LANES), F32)
    longer = pltpu.VMEM((EDGE + 1, EDGE, LANES), F32)
    return pl.pallas_call(
        solve_kernel,
        in_specs=[pl.BlockSpec(memory_space=pl.ANY), pl.BlockSpec(memory_space=pltpu.VMEM)],
        out_specs=pl.BlockSpec(memory_space=pl.ANY),
        out_shape=full((PATCH_DEV, EDGE, EDGE * EDGE)),
        scratch_shapes=[
            pltpu.VMEM((EDGE + 2, EDGE, LANES), F32),
            longer,
            longer,
            cube,
            cube,
            cube,
            cube,
            pltpu.VMEM((1, EDGE, LANES), F32),
            pltpu.SemaphoreType.DMA((TAPS,)),
            pltpu.SemaphoreType.DMA((GROUPS,)),
        ],
        compiler_params=params(),
        cost_estimate=pl.CostEstimate(
            flops=60 * EDGE**3 * PATCH_DEV, bytes_accessed=32 << 20, transcendentals=0
        ),
        name="solve_patches",
    )(half, later)


def wave_tables():
    index = np.arange(NX, dtype=np.int64)
    angle = (index[:, None] * index[None, :] % NX) * (2.0 * math.pi / NX)
    waves = np.concatenate([np.cos(angle), np.sin(angle)], axis=0)
    return waves.astype(np.float32)


def on_device(noise, spectrum, send_core, recv_source):
    swap = lambda v: lax.all_to_all(v, "wide", split_axis=0, concat_axis=0)
    lines = swap(
        split_rows(noise, send_core.reshape(1, WIDE), recv_source.reshape(1, PATCH_DEV))
    )
    table = jnp.concatenate(
        [lines[:, ROWS, :WIDE], lines[:, ROWS + 1, :PATCH_DEV]], axis=1
    ).astype(jnp.int32)
    waves = jnp.asarray(wave_tables())
    weights = jnp.concatenate([spectrum, spectrum])[:, None] / NX
    matrix = lax.dot_general(
        waves,
        waves * weights,
        (((0,), (0,)), ((), ())),
        precision=lax.Precision.HIGHEST,
        preferred_element_type=F32,
    )
    count = lax.axis_size("mid")
    forward = [(i, i + 1) for i in range(count - 1)]
    backward = [(i + 1, i) for i in range(count - 1)]
    pair = bf16_pair(matrix)
    parts, low = filter_exp(0, pair, lines)
    above = lax.ppermute(low, "mid", backward)
    parts, high = filter_exp(1, pair, lines, parts)
    below = lax.ppermute(high, "mid", forward)
    back = swap(parts)
    outgoing = windows(table, (low, high))
    outgoing = windows(table, (below, above), outgoing)
    outgoing, back = lax.optimization_barrier((outgoing, back))
    incoming = swap(outgoing)
    coefficient = join_rows(back)
    cores = table[recv_source.reshape(-1), lax.axis_index("wide")]
    later = jnp.repeat((cores >> 5) & 1, EDGE).reshape(1, LANES)
    solved = solve(incoming, later)
    return coefficient, solved.reshape(1, 1, PATCH_DEV, EDGE, EDGE * EDGE)


def solution(mesh):
    in_specs = (P("wide", "mid", None), P(), P("wide", "mid", None), P("wide", "mid", None))
    out_specs = (P("wide", "mid", None), P("wide", "mid", None, None, None))
    return jax.shard_map(
        on_device, mesh=mesh, in_specs=in_specs, out_specs=out_specs, check_vma=False
    )
```

```python
import functools
import math

import jax
import jax.numpy as jnp
import numpy as np
from jax import lax
from jax.experimental import pallas as pl
from jax.experimental.pallas import tpu as pltpu
from jax.sharding import PartitionSpec as P

NX = 512
NZ = 512
CY = 32
CX = 32
CORE = 16
LAYER = 16
WIDE = 16
PATCH_DEV = 8
EDGE = 48
TAPS = 3
LANES = PATCH_DEV * EDGE
SIDE = 128
TILES = NZ // SIDE
ROWS = 2 * TILES * CX
OWNERS = 4
UNROLL = 2
TINY = 1e-06
F32 = jnp.float32


def params(mebibytes):
    return pltpu.CompilerParams(vmem_limit_bytes=mebibytes * 1024 * 1024)


def full(shape):
    return jax.ShapeDtypeStruct(shape, F32)


def exchange(pieces):
    row = lax.broadcasted_iota(jnp.int32, pieces[0].shape, 0)
    pieces = list(pieces)
    for bit in (4, 2, 1):
        upper = (row & bit) != 0
        for i in range(8):
            k = i | bit
            if i == k:
                continue
            pieces[i], pieces[k] = (
                jnp.where(upper, pltpu.roll(pieces[k], bit, 0), pieces[i]),
                jnp.where(upper, pieces[k], pltpu.roll(pieces[i], 8 - bit, 0)),
            )
    return pieces


def split_kernel(in_ref, send_ref, source_ref, out_ref, held, sems):
    j = pl.program_id(0)

    def leave(t, tile):
        rows = pl.ds(pl.multiple_of((t * TILES + tile) * CX, CX), CX)
        return pltpu.make_async_copy(held.at[:, rows, :], out_ref.at[:, rows, :], sems.at[t, tile])

    def leave_tables():
        rows = pl.ds(ROWS, 8)
        return pltpu.make_async_copy(held.at[:, rows, :], out_ref.at[:, rows, :], sems.at[2, 0])

    @pl.when(j == 0)
    def _():
        for w in range(WIDE):
            held[w, ROWS:ROWS + 1, 0:WIDE] = send_ref[...].astype(F32)
            held[w, ROWS + 1:ROWS + 2, 0:PATCH_DEV] = source_ref[...].astype(F32)
        leave_tables().start()

    for t in range(2):
        first = pl.multiple_of((t * TILES + j) * CX, CX)
        for x in range(0, CX, 8):
            for y in range(0, WIDE, 8):
                at = t * WIDE + y
                pieces = exchange([in_ref[x + i, at:at + 8, :] for i in range(8)])
                for i in range(8):
                    held[y + i, pl.ds(first + x, 8), :] = pieces[i]
        leave(t, j).start()

    @pl.when(j == TILES - 1)
    def _():
        leave_tables().wait()
        for t in range(2):
            for tile in range(TILES):
                leave(t, tile).wait()


def split_rows(block, send, source):
    return pl.pallas_call(
        split_kernel,
        grid=(TILES,),
        in_specs=[
            pl.BlockSpec((CX, CY, SIDE), lambda j: (0, 0, j)),
            pl.BlockSpec((1, WIDE), lambda j: (0, 0)),
            pl.BlockSpec((1, PATCH_DEV), lambda j: (0, 0)),
        ],
        out_specs=pl.BlockSpec(memory_space=pl.ANY),
        out_shape=full((WIDE, ROWS + 8, SIDE)),
        scratch_shapes=[
            pltpu.VMEM((WIDE, ROWS + 8, SIDE), F32),
            pltpu.SemaphoreType.DMA((3, TILES)),
        ],
        compiler_params=params(56),
        cost_estimate=pl.CostEstimate(flops=0, bytes_accessed=8 << 20, transcendentals=0),
        name="split_rows",
    )(block, send, source)


def join_kernel(low_ref, high_ref, out_ref):
    for t, in_ref in enumerate((low_ref, high_ref)):
        for x in range(0, CX, 8):
            for y in range(0, WIDE, 8):
                pieces = exchange([in_ref[y + i, x:x + 8, :] for i in range(8)])
                for i in range(8):
                    out_ref[x + i, t * WIDE + y:t * WIDE + y + 8, :] = pieces[i]


def join_rows(parts):
    return pl.pallas_call(
        join_kernel,
        grid=(TILES,),
        in_specs=[
            pl.BlockSpec((WIDE, CX, SIDE), lambda j: (0, j, 0)),
            pl.BlockSpec((WIDE, CX, SIDE), lambda j: (0, TILES + j, 0)),
        ],
        out_specs=pl.BlockSpec((CX, CY, SIDE), lambda j: (0, 0, j)),
        out_shape=full((CX, CY, NZ)),
        compiler_params=params(12),
        cost_estimate=pl.CostEstimate(flops=0, bytes_accessed=8 << 20, transcendentals=0),
        name="join_rows",
    )(parts, parts)


def pair_kernel(in_ref, high_ref, low_ref):
    value = in_ref[...]
    high = value.astype(jnp.bfloat16)
    high_ref[...] = high
    low_ref[...] = (value - high.astype(F32)).astype(jnp.bfloat16)


def bf16_pair(matrix):
    return pl.pallas_call(
        pair_kernel,
        out_shape=[jax.ShapeDtypeStruct((NX, NX), jnp.bfloat16)] * 2,
        compiler_params=params(12),
        cost_estimate=pl.CostEstimate(flops=0, bytes_accessed=2 << 20, transcendentals=0),
        name="bf16_pair",
    )(matrix)


def filter_kernel(high_ref, low_ref, in_ref, parts_ref, first_ref, second_ref):
    lines = jnp.concatenate(
        [in_ref[:, 0:CX, :].reshape(NX, SIDE), in_ref[:, CX:, :].reshape(NX, SIDE)], axis=1
    )
    high = lines.astype(jnp.bfloat16)
    low = (lines - high.astype(F32)).astype(jnp.bfloat16)
    dot = lambda a, b: jnp.dot(a, b, preferred_element_type=F32)
    small = dot(high_ref[...], low) + dot(low_ref[...], high)
    value = jnp.exp(dot(high_ref[...], high) + small)
    sides = [value[:, :SIDE], value[:, SIDE:]]
    for k in range(2):
        parts_ref[:, k * CX:(k + 1) * CX, :] = sides[k].reshape(WIDE, CX, SIDE)

    def plane(ref):
        for k in range(2):
            ref[k] = 0.5 * sides[k]

    pl.when(pl.program_id(0) < 2)(lambda: plane(first_ref))
    pl.when(pl.program_id(0) >= 2)(lambda: plane(second_ref))


def filter_exp(pair, lines):
    whole = pl.BlockSpec((NX, NX), lambda i: (0, 0))
    block = pl.BlockSpec((WIDE, 2 * CX, SIDE), lambda i: (0, i, 0))
    return pl.pallas_call(
        filter_kernel,
        grid=(4,),
        in_specs=[whole, whole, block],
        out_specs=[
            block,
            pl.BlockSpec((2, NX, SIDE), lambda i: (jnp.minimum(i, 1), 0, 0)),
            pl.BlockSpec((2, NX, SIDE), lambda i: (jnp.maximum(i - 2, 0), 0, 0)),
        ],
        out_shape=[full((WIDE, ROWS, SIDE)), full((TILES, NX, SIDE)), full((TILES, NX, SIDE))],
        compiler_params=params(20),
        cost_estimate=pl.CostEstimate(
            flops=12 * NX * NX * NZ, bytes_accessed=8 << 20, transcendentals=2 * NX * NZ
        ),
        name="filter_exp",
    )(*pair, lines)


def window_kernel(slots, table_ref, *refs):
    low_ref, high_ref = refs[:2]
    out_ref, held, sems = refs[-3:]
    step = pl.program_id(0)

    @pl.when(step == 0)
    def _():
        copies = [
            pltpu.make_async_copy(
                src, held.at[t, pl.ds(1, TILES), pl.ds(LAYER, NX), :], sems.at[t]
            )
            for t, src in enumerate((low_ref, high_ref))
        ]
        for copy in copies:
            copy.start()
        side = jnp.zeros((NX + 2 * LAYER, SIDE), F32)
        for t in range(2):
            held[t, 0] = side
            held[t, TILES + 1] = side
            for j in range(TILES):
                held[t, 1 + j, 0:LAYER, :] = side[:LAYER]
                held[t, 1 + j, LAYER + NX:, :] = side[:LAYER]
        for copy in copies:
            copy.wait()

    lane = lax.broadcasted_iota(jnp.int32, (EDGE, SIDE), 1)

    def one_owner(k, _):
        owner = step * OWNERS + k
        places = []
        for p in range(PATCH_DEV):
            source = table_ref[owner, WIDE + p]
            core = jnp.maximum(table_ref[source, owner], 0)
            x_at = source * CX + (core >> 6) * CORE
            z_at = (core & 31) * CORE + (SIDE - LAYER)
            offset = z_at & (SIDE - 1)
            turn = ((p * EDGE) % SIDE - offset) & (SIDE - 1)
            places.append((pl.multiple_of(x_at, CORE), (core >> 5) & 1, z_at >> 7, offset, turn))
        for t in range(slots):
            tiles = [None] * 3
            for p, (x_at, t_at, tile, offset, turn) in enumerate(places):
                plane = t if slots == 2 else t_at
                rows = pl.ds(x_at, EDGE)
                near = held[plane, tile, rows, :]
                far = held[plane, tile + 1, rows, :]
                moved = pltpu.roll(jnp.where(lane >= offset, near, far), turn, 1)
                at = (p * EDGE) % SIDE
                q = (p * EDGE) // SIDE
                tiles[q] = moved if at == 0 else jnp.where(lane >= at, moved, tiles[q])
                if at + EDGE > SIDE:
                    tiles[q + 1] = moved
            for q in range(3):
                out_ref[k, t * EDGE:(t + 1) * EDGE, q * SIDE:(q + 1) * SIDE] = tiles[q]
        return 0

    lax.fori_loop(0, OWNERS, one_owner, 0, unroll=UNROLL)


def windows(table, planes, *others):
    slots = 1 if others else 2
    at = 2 if others else 0
    return pl.pallas_call(
        functools.partial(window_kernel, slots),
        grid_spec=pltpu.PrefetchScalarGridSpec(
            num_scalar_prefetch=1,
            grid=(WIDE // OWNERS,),
            in_specs=[pl.BlockSpec(memory_space=pl.ANY)] * (2 + len(others)),
            out_specs=pl.BlockSpec((OWNERS, slots * EDGE, LANES), lambda d, table: (d, at, 0)),
            scratch_shapes=[
                pltpu.VMEM((2, TILES + 2, NX + 2 * LAYER, SIDE), F32),
                pltpu.SemaphoreType.DMA((2,)),
            ],
        ),
        out_shape=full((WIDE, TAPS * EDGE, LANES)),
        input_output_aliases={3: 0} if others else {},
        compiler_params=params(16),
        cost_estimate=pl.CostEstimate(
            flops=0, bytes_accessed=slots * (6 << 20), transcendentals=0
        ),
        name="patch_windows",
    )(table, *planes, *others)


STRIPS = EDGE // 8
SLABS = 3
GROUPS = EDGE // 8
PIECES = [(i, q) for i in range(STRIPS) for q in range(3)]


def piece(i, q):
    return (pl.ds(8 * i, 8), pl.ds(SIDE * q, SIDE))


def solve_kernel(
    half_ref, later_ref, out_ref, half, first, image, heavy, face_x, face_y, face_z, ready, arrive, leave
):
    arrivals = [
        pltpu.make_async_copy(
            half_ref.at[:, pl.ds(t * EDGE, EDGE), :], (heavy, face_x, face_y)[t].at[pl.ds(0, WIDE)], arrive.at[t]
        )
        for t in range(TAPS)
    ]
    for copy in arrivals:
        copy.start()
    none = jnp.zeros((8, SIDE), F32)
    for at in PIECES:
        half[0, *piece(*at)] = none
        half[EDGE + 1, *piece(*at)] = none
        first[EDGE, *piece(*at)] = none
        image[EDGE, *piece(*at)] = none

    row = lax.broadcasted_iota(jnp.int32, (8, SIDE), 0)
    lane = lax.broadcasted_iota(jnp.int32, (8, SIDE), 1)
    row_low, row_high = row == 0, row == 7
    lane_low, lane_high = lane == 0, lane == SIDE - 1
    depth = []
    for q in range(3):
        place = lane + q * SIDE
        depth.append(place - ((place * 1366) >> 16) * EDGE)
    z_low = [d == 0 for d in depth]
    z_high = [d == EDGE - 1 for d in depth]

    def above_x(slab):
        turned = {at: pltpu.roll(slab[at], 7, 0) for at in PIECES}
        return {
            (i, q): jnp.where(row_high, turned[i + 1, q] if i < STRIPS - 1 else 0.0, turned[i, q])
            for i, q in PIECES
        }

    def below_x(slab):
        turned = {at: pltpu.roll(slab[at], 1, 0) for at in PIECES}
        return {
            (i, q): jnp.where(row_low, turned[i - 1, q] if i else 0.0, turned[i, q])
            for i, q in PIECES
        }

    def above_z(strip):
        turned = [pltpu.roll(v, SIDE - 1, 1) for v in strip]
        return [
            jnp.where(lane_high, turned[1], turned[0]),
            jnp.where(lane_high, turned[2], turned[1]),
            turned[2],
        ]

    def below_z(strip):
        turned = [pltpu.roll(v, 1, 1) for v in strip]
        return [
            jnp.where(lane_low, 0.0, turned[0]),
            jnp.where(lane_low, turned[0], turned[1]),
            jnp.where(lane_low, turned[1], turned[2]),
        ]

    def load(ref, y):
        return {at: ref[y, *piece(*at)] for at in PIECES}

    def strip(slab, i):
        return [slab[i, q] for q in range(3)]

    same = jnp.where(
        ((lax.broadcasted_iota(jnp.int32, (LANES, LANES), 0) * 1366) >> 16)
        == ((lax.broadcasted_iota(jnp.int32, (LANES, LANES), 1) * 1366) >> 16),
        1.0,
        0.0,
    ).astype(jnp.bfloat16)

    def patch_total(parts):
        part = jnp.concatenate(parts, axis=1)
        high = part.astype(jnp.bfloat16).astype(F32)
        middle = (part - high).astype(jnp.bfloat16).astype(F32)
        low = part - high - middle
        stack = jnp.concatenate([high, middle, low, jnp.zeros_like(low)], axis=0)
        spread = jnp.dot(stack.astype(jnp.bfloat16), same, preferred_element_type=F32)
        total = jnp.sum(spread, axis=0, keepdims=True)
        return [
            jnp.broadcast_to(total[:, SIDE * q:SIDE * (q + 1)], (8, SIDE)) for q in range(3)
        ]

    def divide(top, bottom):
        return [t / (b + TINY) for t, b in zip(top, bottom)]

    nothing = (none, none, none)

    for copy in arrivals:
        copy.wait()
    in_order = [
        jnp.broadcast_to(later_ref[:, SIDE * q:SIDE * (q + 1)], (8, SIDE)) != 0 for q in range(3)
    ]

    def arrange(w, _):
        for i, q in PIECES:
            at = piece(i, q)
            a, b, c = heavy[w, *at], face_x[w, *at], face_y[w, *at]
            half[1 + w, *at] = jnp.where(in_order[q], a, c)
            half[1 + WIDE + w, *at] = jnp.where(in_order[q], b, a)
            half[1 + 2 * WIDE + w, *at] = jnp.where(in_order[q], c, b)
        return 0

    lax.fori_loop(0, WIDE, arrange, 0)

    def faces_of(y, rr):
        rr = list(rr)
        h = load(half, y + 1)
        h_up = above_x(h)
        h_down = below_x(h)
        deep_up, deep_down = {}, {}
        for i in range(STRIPS):
            ups, downs = above_z(strip(h, i)), below_z(strip(h, i))
            for q in range(3):
                deep_up[i, q] = jnp.where(z_high[q], 0.0, ups[q])
                deep_down[i, q] = jnp.where(z_low[q], 0.0, downs[q])
        up_up, up_down = above_x(deep_up), below_x(deep_up)
        down_up, down_down = above_x(deep_down), below_x(deep_down)
        for i, q in PIECES:
            here, to = h[i, q], piece(i, q)
            z_up, z_down = deep_up[i, q], deep_down[i, q]
            v = h_up[i, q] - h_down[i, q]
            y_up = half[y + 2, *to]
            y_down = half[y, *to]
            across = here + h_up[i, q]
            if i == STRIPS - 1:
                across = jnp.where(row_high, 0.0, across)
            deep = here + z_up
            heavy[y, *to] = (
                (1.0 + 6.0 * here) + (h_up[i, q] + h_down[i, q])
                + ((y_up + y_down) + (z_up + z_down))
            )
            face_x[y, *to] = across
            face_y[y + 1, *to] = here + y_up
            face_z[y, *to] = jnp.where(z_high[q], 0.0, deep)
            first[y, *to] = v
            image[y, *to] = deep * (up_up[i, q] - up_down[i, q]) + (here + z_down) * (
                down_up[i, q] - down_down[i, q]
            )
            rr[q] = rr[q] + v * v
        return tuple(rr)

    rr = lax.fori_loop(0, EDGE, faces_of, nothing, unroll=3)
    for at in PIECES:
        face_y[0, *piece(*at)] = none
        face_y[EDGE, *piece(*at)] = none
    rr = patch_total(rr)

    def image_of(y, total):
        total = list(total)
        v = load(first, y)
        v_up = above_x(v)
        across = load(face_x, y)
        from_x = below_x({at: across[at] * v[at] for at in PIECES})
        for i, q in PIECES:
            to = piece(i, q)
            couple = across[i, q] * v_up[i, q] + from_x[i, q]
            couple = couple + face_y[y + 1, *to] * first[y + 1, *to]
            couple = couple + face_y[y, *to] * first[jnp.maximum(y - 1, 0), *to]
            result = heavy[y, *to] * v[i, q] - (couple + image[y, *to])
            image[y, *to] = result
            total[q] = total[q] + v[i, q] * result
        return tuple(total)

    alpha = divide(rr, patch_total(lax.fori_loop(0, EDGE, image_of, nothing, unroll=3)))

    def residual_of(y, total):
        total = list(total)
        for i, q in PIECES:
            left = first[y, *piece(i, q)] - alpha[q] * image[y, *piece(i, q)]
            total[q] = total[q] + left * left
        return tuple(total)

    new = patch_total(lax.fori_loop(0, EDGE, residual_of, nothing, unroll=4))
    beta = divide(new, rr)

    def direction(y, i, q):
        v = first[y, *piece(i, q)]
        return (v - alpha[q] * image[y, *piece(i, q)]) + beta[q] * v

    for at in PIECES:
        ready[0, *piece(*at)] = direction(0, *at)

    def energy_of(step, total):
        total = list(total)
        v = load(ready, 0)
        for k in range(SLABS):
            y = step * SLABS + k
            v_up = above_x(v)
            v_next = {at: direction(y + 1, *at) for at in PIECES}
            for i in range(STRIPS):
                ups = above_z(strip(v, i))
                for q in range(3):
                    to = piece(i, q)
                    couple = face_x[y, *to] * v_up[i, q]
                    couple = couple + face_y[y + 1, *to] * v_next[i, q]
                    couple = couple + face_z[y, *to] * ups[q]
                    total[q] = total[q] + v[i, q] * (heavy[y, *to] * v[i, q] - 2.0 * couple)
            v = v_next
        for at in PIECES:
            ready[0, *piece(*at)] = v[at]
        return tuple(total)

    energy = lax.fori_loop(0, EDGE // SLABS, energy_of, nothing)
    alpha_next = divide(new, patch_total(energy))
    on_first = [alpha[q] + alpha_next[q] * (1.0 + beta[q]) for q in range(3)]
    on_image = [-(alpha_next[q] * alpha[q]) for q in range(3)]

    ends = [lane < end for end in (48, 96, 16, 64, 112, 32, 80)]

    def gather(c):
        return (
            jnp.where(ends[0], c[0][0], jnp.where(ends[1], c[1][0], c[2][0])),
            jnp.where(
                ends[2],
                c[2][1],
                jnp.where(ends[3], c[3][1], jnp.where(ends[4], c[4][1], c[5][1])),
            ),
            jnp.where(ends[5], c[5][2], jnp.where(ends[6], c[6][2], c[7][2])),
        )

    departures = []
    for group in range(GROUPS):

        def correct(i, _):
            rows = pl.ds(pl.multiple_of(8 * i, 8), 8)
            lines = []
            for j in range(8):
                y = 8 * group + j
                lines.append([
                    on_first[q] * first[y, rows, pl.ds(SIDE * q, SIDE)]
                    + on_image[q] * image[y, rows, pl.ds(SIDE * q, SIDE)]
                    for q in range(3)
                ])
            turned = []
            for k in range(8):
                a, b, c = gather([lines[(p + k) % 8] for p in range(8)])
                far, near = divmod(EDGE * k, SIDE)
                r = [pltpu.roll(v, near, 1) if near else v for v in (a, b, c)]
                r = [r[(q - far) % 3] for q in range(3)]
                before = [r[2], r[0], r[1]]
                if near:
                    r = [jnp.where(lane < near, before[q], r[q]) for q in range(3)]
                turned.append(r)
            for p in range(PATCH_DEV):
                tiles = gather([turned[(j - p) % 8] for j in range(8)])
                for q in range(3):
                    heavy[8 * group + p, rows, pl.ds(SIDE * q, SIDE)] = tiles[q]
            return 0

        lax.fori_loop(0, STRIPS, correct, 0, unroll=True)
        departures.append(
            pltpu.make_async_copy(
                heavy.at[pl.ds(8 * group, PATCH_DEV)],
                out_ref.at[:, :, pl.ds(group * LANES, LANES)],
                leave.at[group],
            )
        )
        departures[-1].start()
    for copy in departures:
        copy.wait()


def solve(half, later):
    cube = pltpu.VMEM((EDGE, EDGE, LANES), F32)
    longer = pltpu.VMEM((EDGE + 1, EDGE, LANES), F32)
    return pl.pallas_call(
        solve_kernel,
        in_specs=[pl.BlockSpec(memory_space=pl.ANY), pl.BlockSpec(memory_space=pltpu.VMEM)],
        out_specs=pl.BlockSpec(memory_space=pl.ANY),
        out_shape=full((PATCH_DEV, EDGE, EDGE * EDGE)),
        scratch_shapes=[
            pltpu.VMEM((EDGE + 2, EDGE, LANES), F32),
            longer,
            longer,
            cube,
            cube,
            longer,
            cube,
            pltpu.VMEM((1, EDGE, LANES), F32),
            pltpu.SemaphoreType.DMA((TAPS,)),
            pltpu.SemaphoreType.DMA((GROUPS,)),
        ],
        compiler_params=params(40),
        cost_estimate=pl.CostEstimate(
            flops=60 * EDGE**3 * PATCH_DEV, bytes_accessed=32 << 20, transcendentals=0
        ),
        name="solve_patches",
    )(half, later)


def wave_tables():
    index = np.arange(NX, dtype=np.int64)
    angle = (index[:, None] * index[None, :] % NX) * (2.0 * math.pi / NX)
    waves = np.concatenate([np.cos(angle), np.sin(angle)], axis=0)
    return waves.astype(np.float32)


def on_device(noise, spectrum, send_core, recv_source):
    swap = lambda v: lax.all_to_all(v, "wide", split_axis=0, concat_axis=0)
    lines = swap(
        split_rows(noise, send_core.reshape(1, WIDE), recv_source.reshape(1, PATCH_DEV))
    )
    table = jnp.concatenate(
        [lines[:, ROWS, :WIDE], lines[:, ROWS + 1, :PATCH_DEV]], axis=1
    ).astype(jnp.int32)
    waves = jnp.asarray(wave_tables())
    weights = jnp.concatenate([spectrum, spectrum])[:, None] / NX
    matrix = lax.dot_general(
        waves,
        waves * weights,
        (((0,), (0,)), ((), ())),
        precision=lax.Precision.HIGHEST,
        preferred_element_type=F32,
    )
    count = lax.axis_size("mid")
    forward = [(i, i + 1) for i in range(count - 1)]
    backward = [(i + 1, i) for i in range(count - 1)]
    pair = bf16_pair(matrix)
    parts, low, high = filter_exp(pair, lines)
    above = lax.ppermute(low, "mid", backward)
    below = lax.ppermute(high, "mid", forward)
    back = swap(parts)
    outgoing = windows(table, (low, high))
    outgoing = windows(table, (below, above), outgoing)
    outgoing, back = lax.optimization_barrier((outgoing, back))
    incoming = swap(outgoing)
    coefficient = join_rows(back)
    cores = table[recv_source.reshape(-1), lax.axis_index("wide")]
    later = jnp.repeat((cores >> 5) & 1, EDGE).reshape(1, LANES)
    solved = solve(incoming, later)
    return coefficient, solved.reshape(1, 1, PATCH_DEV, EDGE, EDGE * EDGE)


def solution(mesh):
    in_specs = (P("wide", "mid", None), P(), P("wide", "mid", None), P("wide", "mid", None))
    out_specs = (P("wide", "mid", None), P("wide", "mid", None, None, None))
    return jax.shard_map(
        on_device, mesh=mesh, in_specs=in_specs, out_specs=out_specs, check_vma=False
    )
```

```python
import functools
import math

import jax
import jax.numpy as jnp
import numpy as np
from jax import lax
from jax.experimental import pallas as pl
from jax.experimental.pallas import tpu as pltpu
from jax.sharding import PartitionSpec as P

NX = 512
NZ = 512
CY = 32
CX = 32
CORE = 16
LAYER = 16
WIDE = 16
PATCH_DEV = 8
EDGE = 48
TAPS = 3
LANES = PATCH_DEV * EDGE
SIDE = 128
TILES = NZ // SIDE
ROWS = 2 * TILES * CX
OWNERS = 4
UNROLL = 2
TINY = 1e-06
F32 = jnp.float32


def params(mebibytes):
    return pltpu.CompilerParams(vmem_limit_bytes=mebibytes * 1024 * 1024)


def full(shape):
    return jax.ShapeDtypeStruct(shape, F32)


def exchange(pieces):
    row = lax.broadcasted_iota(jnp.int32, pieces[0].shape, 0)
    pieces = list(pieces)
    for bit in (4, 2, 1):
        upper = (row & bit) != 0
        for i in range(8):
            k = i | bit
            if i == k:
                continue
            pieces[i], pieces[k] = (
                jnp.where(upper, pltpu.roll(pieces[k], bit, 0), pieces[i]),
                jnp.where(upper, pieces[k], pltpu.roll(pieces[i], 8 - bit, 0)),
            )
    return pieces


def split_kernel(in_ref, send_ref, source_ref, out_ref, held, sems):
    j = pl.program_id(0)

    def leave(t, tile):
        rows = pl.ds(pl.multiple_of((t * TILES + tile) * CX, CX), CX)
        return pltpu.make_async_copy(held.at[:, rows, :], out_ref.at[:, rows, :], sems.at[t, tile])

    def leave_tables():
        rows = pl.ds(ROWS, 8)
        return pltpu.make_async_copy(held.at[:, rows, :], out_ref.at[:, rows, :], sems.at[2, 0])

    @pl.when(j == 0)
    def _():
        for w in range(WIDE):
            held[w, ROWS:ROWS + 1, 0:WIDE] = send_ref[...].astype(F32)
            held[w, ROWS + 1:ROWS + 2, 0:PATCH_DEV] = source_ref[...].astype(F32)
        leave_tables().start()

    for t in range(2):
        first = pl.multiple_of((t * TILES + j) * CX, CX)
        for x in range(0, CX, 8):
            for y in range(0, WIDE, 8):
                at = t * WIDE + y
                pieces = exchange([in_ref[x + i, at:at + 8, :] for i in range(8)])
                for i in range(8):
                    held[y + i, pl.ds(first + x, 8), :] = pieces[i]
        leave(t, j).start()

    @pl.when(j == TILES - 1)
    def _():
        leave_tables().wait()
        for t in range(2):
            for tile in range(TILES):
                leave(t, tile).wait()


def split_rows(block, send, source):
    return pl.pallas_call(
        split_kernel,
        grid=(TILES,),
        in_specs=[
            pl.BlockSpec((CX, CY, SIDE), lambda j: (0, 0, j)),
            pl.BlockSpec((1, WIDE), lambda j: (0, 0)),
            pl.BlockSpec((1, PATCH_DEV), lambda j: (0, 0)),
        ],
        out_specs=pl.BlockSpec(memory_space=pl.ANY),
        out_shape=full((WIDE, ROWS + 8, SIDE)),
        scratch_shapes=[
            pltpu.VMEM((WIDE, ROWS + 8, SIDE), F32),
            pltpu.SemaphoreType.DMA((3, TILES)),
        ],
        compiler_params=params(56),
        cost_estimate=pl.CostEstimate(flops=0, bytes_accessed=8 << 20, transcendentals=0),
        name="split_rows",
    )(block, send, source)


def join_kernel(low_ref, high_ref, out_ref):
    for t, in_ref in enumerate((low_ref, high_ref)):
        for x in range(0, CX, 8):
            for y in range(0, WIDE, 8):
                pieces = exchange([in_ref[y + i, x:x + 8, :] for i in range(8)])
                for i in range(8):
                    out_ref[x + i, t * WIDE + y:t * WIDE + y + 8, :] = pieces[i]


def join_rows(parts):
    return pl.pallas_call(
        join_kernel,
        grid=(TILES,),
        in_specs=[
            pl.BlockSpec((WIDE, CX, SIDE), lambda j: (0, j, 0)),
            pl.BlockSpec((WIDE, CX, SIDE), lambda j: (0, TILES + j, 0)),
        ],
        out_specs=pl.BlockSpec((CX, CY, SIDE), lambda j: (0, 0, j)),
        out_shape=full((CX, CY, NZ)),
        compiler_params=params(12),
        cost_estimate=pl.CostEstimate(flops=0, bytes_accessed=8 << 20, transcendentals=0),
        name="join_rows",
    )(parts, parts)


def pair_kernel(in_ref, high_ref, low_ref):
    value = in_ref[...]
    high = value.astype(jnp.bfloat16)
    high_ref[...] = high
    low_ref[...] = (value - high.astype(F32)).astype(jnp.bfloat16)


def bf16_pair(matrix):
    return pl.pallas_call(
        pair_kernel,
        out_shape=[jax.ShapeDtypeStruct((NX, NX), jnp.bfloat16)] * 2,
        compiler_params=params(56),
        cost_estimate=pl.CostEstimate(flops=0, bytes_accessed=2 << 20, transcendentals=0),
        name="bf16_pair",
    )(matrix)


def filter_kernel(high_ref, low_ref, in_ref, extra_ref, parts_ref, first_ref, second_ref, table_ref):
    for k in range(2):
        table_ref[k] = extra_ref[:, k, :].astype(jnp.int32)
    lines = jnp.concatenate(
        [in_ref[:, 0:CX, :].reshape(NX, SIDE), in_ref[:, CX:, :].reshape(NX, SIDE)], axis=1
    )
    high = lines.astype(jnp.bfloat16)
    low = (lines - high.astype(F32)).astype(jnp.bfloat16)
    dot = lambda a, b: jnp.dot(a, b, preferred_element_type=F32)
    small = dot(high_ref[...], low) + dot(low_ref[...], high)
    value = jnp.exp(dot(high_ref[...], high) + small)
    sides = [value[:, :SIDE], value[:, SIDE:]]
    for k in range(2):
        parts_ref[:, k * CX:(k + 1) * CX, :] = sides[k].reshape(WIDE, CX, SIDE)

    def plane(ref):
        for k in range(2):
            ref[k] = 0.5 * sides[k]

    pl.when(pl.program_id(0) < 2)(lambda: plane(first_ref))
    pl.when(pl.program_id(0) >= 2)(lambda: plane(second_ref))


def filter_exp(pair, lines):
    whole = pl.BlockSpec((NX, NX), lambda i: (0, 0))
    block = pl.BlockSpec((WIDE, 2 * CX, SIDE), lambda i: (0, i, 0))
    return pl.pallas_call(
        filter_kernel,
        grid=(4,),
        in_specs=[whole, whole, block, pl.BlockSpec((WIDE, 8, SIDE), lambda i: (0, ROWS // 8, 0))],
        out_specs=[
            block,
            pl.BlockSpec((2, NX, SIDE), lambda i: (jnp.minimum(i, 1), 0, 0)),
            pl.BlockSpec((2, NX, SIDE), lambda i: (jnp.maximum(i - 2, 0), 0, 0)),
            pl.BlockSpec((2, WIDE, SIDE), lambda i: (0, 0, 0)),
        ],
        out_shape=[
            full((WIDE, ROWS, SIDE)),
            full((TILES, NX, SIDE)),
            full((TILES, NX, SIDE)),
            jax.ShapeDtypeStruct((2, WIDE, SIDE), jnp.int32),
        ],
        compiler_params=params(56),
        cost_estimate=pl.CostEstimate(
            flops=12 * NX * NX * NZ, bytes_accessed=8 << 20, transcendentals=2 * NX * NZ
        ),
        name="filter_exp",
    )(*pair, lines, lines)


def window_kernel(slots, table_ref, *refs):
    low_ref, high_ref = refs[:2]
    out_ref, held, sems = refs[-3:]
    step = pl.program_id(0)

    @pl.when(step == 0)
    def _():
        copies = [
            pltpu.make_async_copy(
                src, held.at[t, pl.ds(1, TILES), pl.ds(LAYER, NX), :], sems.at[t]
            )
            for t, src in enumerate((low_ref, high_ref))
        ]
        for copy in copies:
            copy.start()
        side = jnp.zeros((NX + 2 * LAYER, SIDE), F32)
        for t in range(2):
            held[t, 0] = side
            held[t, TILES + 1] = side
            for j in range(TILES):
                held[t, 1 + j, 0:LAYER, :] = side[:LAYER]
                held[t, 1 + j, LAYER + NX:, :] = side[:LAYER]
        for copy in copies:
            copy.wait()

    lane = lax.broadcasted_iota(jnp.int32, (EDGE, SIDE), 1)

    def one_owner(k, _):
        owner = step * OWNERS + k
        places = []
        for p in range(PATCH_DEV):
            source = table_ref[1, owner, p]
            core = jnp.maximum(table_ref[0, source, owner], 0)
            x_at = source * CX + (core >> 6) * CORE
            z_at = (core & 31) * CORE + (SIDE - LAYER)
            offset = z_at & (SIDE - 1)
            turn = ((p * EDGE) % SIDE - offset) & (SIDE - 1)
            places.append((pl.multiple_of(x_at, CORE), (core >> 5) & 1, z_at >> 7, offset, turn))
        for t in range(slots):
            tiles = [None] * 3
            for p, (x_at, t_at, tile, offset, turn) in enumerate(places):
                plane = t if slots == 2 else t_at
                rows = pl.ds(x_at, EDGE)
                near = held[plane, tile, rows, :]
                far = held[plane, tile + 1, rows, :]
                moved = pltpu.roll(jnp.where(lane >= offset, near, far), turn, 1)
                at = (p * EDGE) % SIDE
                q = (p * EDGE) // SIDE
                tiles[q] = moved if at == 0 else jnp.where(lane >= at, moved, tiles[q])
                if at + EDGE > SIDE:
                    tiles[q + 1] = moved
            for q in range(3):
                out_ref[k, t * EDGE:(t + 1) * EDGE, q * SIDE:(q + 1) * SIDE] = tiles[q]
        return 0

    lax.fori_loop(0, OWNERS, one_owner, 0, unroll=UNROLL)


def windows(table, planes, *others):
    slots = 1 if others else 2
    at = 2 if others else 0
    return pl.pallas_call(
        functools.partial(window_kernel, slots),
        grid_spec=pltpu.PrefetchScalarGridSpec(
            num_scalar_prefetch=1,
            grid=(WIDE // OWNERS,),
            in_specs=[pl.BlockSpec(memory_space=pl.ANY)] * (2 + len(others)),
            out_specs=pl.BlockSpec((OWNERS, slots * EDGE, LANES), lambda d, table: (d, at, 0)),
            scratch_shapes=[
                pltpu.VMEM((2, TILES + 2, NX + 2 * LAYER, SIDE), F32),
                pltpu.SemaphoreType.DMA((2,)),
            ],
        ),
        out_shape=full((WIDE, TAPS * EDGE, LANES)),
        input_output_aliases={3: 0} if others else {},
        compiler_params=params(16 if others else 56),
        cost_estimate=pl.CostEstimate(
            flops=0, bytes_accessed=slots * (6 << 20), transcendentals=0
        ),
        name="patch_windows",
    )(table, *planes, *others)


STRIPS = EDGE // 8
SLABS = 3
GROUPS = EDGE // 8
PIECES = [(i, q) for i in range(STRIPS) for q in range(3)]


def piece(i, q):
    return (pl.ds(8 * i, 8), pl.ds(SIDE * q, SIDE))


def solve_kernel(
    half_ref, later_ref, out_ref, half, first, image, heavy, face_x, face_y, face_z, ready, arrive, leave
):
    arrivals = [
        [
            pltpu.make_async_copy(
                half_ref.at[pl.ds(4 * g, 4), pl.ds(t * EDGE, EDGE), :],
                (heavy, face_x, face_y)[t].at[pl.ds(4 * g, 4)],
                arrive.at[g, t],
            )
            for t in range(TAPS)
        ]
        for g in range(WIDE // 4)
    ]
    for group in arrivals:
        for copy in group:
            copy.start()
    none = jnp.zeros((8, SIDE), F32)
    for at in PIECES:
        half[0, *piece(*at)] = none
        half[EDGE + 1, *piece(*at)] = none
        first[EDGE, *piece(*at)] = none
        image[EDGE, *piece(*at)] = none

    row = lax.broadcasted_iota(jnp.int32, (8, SIDE), 0)
    lane = lax.broadcasted_iota(jnp.int32, (8, SIDE), 1)
    row_low, row_high = row == 0, row == 7
    lane_low, lane_high = lane == 0, lane == SIDE - 1
    depth = []
    for q in range(3):
        place = lane + q * SIDE
        depth.append(place - ((place * 1366) >> 16) * EDGE)
    z_low = [d == 0 for d in depth]
    z_high = [d == EDGE - 1 for d in depth]

    def above_x(slab):
        turned = {at: pltpu.roll(slab[at], 7, 0) for at in PIECES}
        return {
            (i, q): jnp.where(row_high, turned[i + 1, q] if i < STRIPS - 1 else 0.0, turned[i, q])
            for i, q in PIECES
        }

    def below_x(slab):
        turned = {at: pltpu.roll(slab[at], 1, 0) for at in PIECES}
        return {
            (i, q): jnp.where(row_low, turned[i - 1, q] if i else 0.0, turned[i, q])
            for i, q in PIECES
        }

    def above_z(strip):
        turned = [pltpu.roll(v, SIDE - 1, 1) for v in strip]
        return [
            jnp.where(lane_high, turned[1], turned[0]),
            jnp.where(lane_high, turned[2], turned[1]),
            turned[2],
        ]

    def below_z(strip):
        turned = [pltpu.roll(v, 1, 1) for v in strip]
        return [
            jnp.where(lane_low, 0.0, turned[0]),
            jnp.where(lane_low, turned[0], turned[1]),
            jnp.where(lane_low, turned[1], turned[2]),
        ]

    def load(ref, y):
        return {at: ref[y, *piece(*at)] for at in PIECES}

    def strip(slab, i):
        return [slab[i, q] for q in range(3)]

    same = jnp.where(
        ((lax.broadcasted_iota(jnp.int32, (LANES, LANES), 0) * 1366) >> 16)
        == ((lax.broadcasted_iota(jnp.int32, (LANES, LANES), 1) * 1366) >> 16),
        1.0,
        0.0,
    ).astype(jnp.bfloat16)

    def patch_total(parts):
        part = jnp.concatenate(parts, axis=1)
        high = part.astype(jnp.bfloat16).astype(F32)
        middle = (part - high).astype(jnp.bfloat16).astype(F32)
        low = part - high - middle
        stack = jnp.concatenate([high, middle, low, jnp.zeros_like(low)], axis=0)
        spread = jnp.dot(stack.astype(jnp.bfloat16), same, preferred_element_type=F32)
        total = jnp.sum(spread, axis=0, keepdims=True)
        return [
            jnp.broadcast_to(total[:, SIDE * q:SIDE * (q + 1)], (8, SIDE)) for q in range(3)
        ]

    def divide(top, bottom):
        return [t / (b + TINY) for t, b in zip(top, bottom)]

    nothing = (none, none, none)

    in_order = [
        jnp.broadcast_to(later_ref[:, SIDE * q:SIDE * (q + 1)], (8, SIDE)) != 0 for q in range(3)
    ]

    def arrange(w, _):
        for i, q in PIECES:
            at = piece(i, q)
            a, b, c = heavy[w, *at], face_x[w, *at], face_y[w, *at]
            half[1 + w, *at] = jnp.where(in_order[q], a, c)
            half[1 + WIDE + w, *at] = jnp.where(in_order[q], b, a)
            half[1 + 2 * WIDE + w, *at] = jnp.where(in_order[q], c, b)
        return 0

    for g, group in enumerate(arrivals):
        for copy in group:
            copy.wait()
        lax.fori_loop(4 * g, 4 * g + 4, arrange, 0, unroll=2)

    def faces_of(y, rr):
        rr = list(rr)
        h = load(half, y + 1)
        h_up = above_x(h)
        h_down = below_x(h)
        deep_up, deep_down = {}, {}
        for i in range(STRIPS):
            ups, downs = above_z(strip(h, i)), below_z(strip(h, i))
            for q in range(3):
                deep_up[i, q] = jnp.where(z_high[q], 0.0, ups[q])
                deep_down[i, q] = jnp.where(z_low[q], 0.0, downs[q])
        up_up, up_down = above_x(deep_up), below_x(deep_up)
        down_up, down_down = above_x(deep_down), below_x(deep_down)
        for i, q in PIECES:
            here, to = h[i, q], piece(i, q)
            z_up, z_down = deep_up[i, q], deep_down[i, q]
            v = h_up[i, q] - h_down[i, q]
            y_up = half[y + 2, *to]
            y_down = half[y, *to]
            across = here + h_up[i, q]
            if i == STRIPS - 1:
                across = jnp.where(row_high, 0.0, across)
            deep = here + z_up
            heavy[y, *to] = (
                (1.0 + 6.0 * here) + (h_up[i, q] + h_down[i, q])
                + ((y_up + y_down) + (z_up + z_down))
            )
            face_x[y, *to] = across
            face_y[y + 1, *to] = here + y_up
            face_z[y, *to] = jnp.where(z_high[q], 0.0, deep)
            first[y, *to] = v
            image[y, *to] = deep * (up_up[i, q] - up_down[i, q]) + (here + z_down) * (
                down_up[i, q] - down_down[i, q]
            )
            rr[q] = rr[q] + v * v
        return tuple(rr)

    rr = lax.fori_loop(0, EDGE, faces_of, nothing, unroll=3)
    for at in PIECES:
        face_y[0, *piece(*at)] = none
        face_y[EDGE, *piece(*at)] = none
    rr = patch_total(rr)

    def image_of(y, total):
        total = list(total)
        v = load(first, y)
        v_up = above_x(v)
        across = load(face_x, y)
        from_x = below_x({at: across[at] * v[at] for at in PIECES})
        for i, q in PIECES:
            to = piece(i, q)
            couple = across[i, q] * v_up[i, q] + from_x[i, q]
            couple = couple + face_y[y + 1, *to] * first[y + 1, *to]
            couple = couple + face_y[y, *to] * first[jnp.maximum(y - 1, 0), *to]
            result = heavy[y, *to] * v[i, q] - (couple + image[y, *to])
            image[y, *to] = result
            total[q] = total[q] + v[i, q] * result
        return tuple(total)

    alpha = divide(rr, patch_total(lax.fori_loop(0, EDGE, image_of, nothing, unroll=3)))

    def residual_of(y, total):
        total = list(total)
        for i, q in PIECES:
            left = first[y, *piece(i, q)] - alpha[q] * image[y, *piece(i, q)]
            total[q] = total[q] + left * left
        return tuple(total)

    new = patch_total(lax.fori_loop(0, EDGE, residual_of, nothing, unroll=4))
    beta = divide(new, rr)

    def direction(y, i, q):
        v = first[y, *piece(i, q)]
        return (v - alpha[q] * image[y, *piece(i, q)]) + beta[q] * v

    for at in PIECES:
        ready[0, *piece(*at)] = direction(0, *at)

    def energy_of(step, total):
        total = list(total)
        v = load(ready, 0)
        for k in range(SLABS):
            y = step * SLABS + k
            v_up = above_x(v)
            v_next = {at: direction(y + 1, *at) for at in PIECES}
            for i in range(STRIPS):
                ups = above_z(strip(v, i))
                for q in range(3):
                    to = piece(i, q)
                    couple = face_x[y, *to] * v_up[i, q]
                    couple = couple + face_y[y + 1, *to] * v_next[i, q]
                    couple = couple + face_z[y, *to] * ups[q]
                    total[q] = total[q] + v[i, q] * (heavy[y, *to] * v[i, q] - 2.0 * couple)
            v = v_next
        for at in PIECES:
            ready[0, *piece(*at)] = v[at]
        return tuple(total)

    energy = lax.fori_loop(0, EDGE // SLABS, energy_of, nothing)
    alpha_next = divide(new, patch_total(energy))
    on_first = [alpha[q] + alpha_next[q] * (1.0 + beta[q]) for q in range(3)]
    on_image = [-(alpha_next[q] * alpha[q]) for q in range(3)]

    ends = [lane < end for end in (48, 96, 16, 64, 112, 32, 80)]

    def gather(c):
        return (
            jnp.where(ends[0], c[0][0], jnp.where(ends[1], c[1][0], c[2][0])),
            jnp.where(
                ends[2],
                c[2][1],
                jnp.where(ends[3], c[3][1], jnp.where(ends[4], c[4][1], c[5][1])),
            ),
            jnp.where(ends[5], c[5][2], jnp.where(ends[6], c[6][2], c[7][2])),
        )

    departures = []
    for group in range(GROUPS):

        def correct(i, _):
            rows = pl.ds(pl.multiple_of(8 * i, 8), 8)
            lines = []
            for j in range(8):
                y = 8 * group + j
                lines.append([
                    on_first[q] * first[y, rows, pl.ds(SIDE * q, SIDE)]
                    + on_image[q] * image[y, rows, pl.ds(SIDE * q, SIDE)]
                    for q in range(3)
                ])
            turned = []
            for k in range(8):
                a, b, c = gather([lines[(p + k) % 8] for p in range(8)])
                far, near = divmod(EDGE * k, SIDE)
                r = [pltpu.roll(v, near, 1) if near else v for v in (a, b, c)]
                r = [r[(q - far) % 3] for q in range(3)]
                before = [r[2], r[0], r[1]]
                if near:
                    r = [jnp.where(lane < near, before[q], r[q]) for q in range(3)]
                turned.append(r)
            for p in range(PATCH_DEV):
                tiles = gather([turned[(j - p) % 8] for j in range(8)])
                for q in range(3):
                    heavy[8 * group + p, rows, pl.ds(SIDE * q, SIDE)] = tiles[q]
            return 0

        lax.fori_loop(0, STRIPS, correct, 0, unroll=True)
        departures.append(
            pltpu.make_async_copy(
                heavy.at[pl.ds(8 * group, PATCH_DEV)],
                out_ref.at[:, :, pl.ds(group * LANES, LANES)],
                leave.at[group],
            )
        )
        departures[-1].start()
    for copy in departures:
        copy.wait()


def solve(half, later):
    cube = pltpu.VMEM((EDGE, EDGE, LANES), F32)
    longer = pltpu.VMEM((EDGE + 1, EDGE, LANES), F32)
    return pl.pallas_call(
        solve_kernel,
        in_specs=[pl.BlockSpec(memory_space=pl.ANY), pl.BlockSpec(memory_space=pltpu.VMEM)],
        out_specs=pl.BlockSpec(memory_space=pl.ANY),
        out_shape=full((PATCH_DEV, EDGE, EDGE * EDGE)),
        scratch_shapes=[
            pltpu.VMEM((EDGE + 2, EDGE, LANES), F32),
            longer,
            longer,
            cube,
            cube,
            longer,
            cube,
            pltpu.VMEM((1, EDGE, LANES), F32),
            pltpu.SemaphoreType.DMA((WIDE // 4, TAPS)),
            pltpu.SemaphoreType.DMA((GROUPS,)),
        ],
        compiler_params=params(40),
        cost_estimate=pl.CostEstimate(
            flops=60 * EDGE**3 * PATCH_DEV, bytes_accessed=32 << 20, transcendentals=0
        ),
        name="solve_patches",
    )(half, later)


def wave_tables():
    index = np.arange(NX, dtype=np.int64)
    angle = (index[:, None] * index[None, :] % NX) * (2.0 * math.pi / NX)
    waves = np.concatenate([np.cos(angle), np.sin(angle)], axis=0)
    return waves.astype(np.float32)


def on_device(noise, spectrum, send_core, recv_source):
    swap = lambda v: lax.all_to_all(v, "wide", split_axis=0, concat_axis=0)
    lines = swap(
        split_rows(noise, send_core.reshape(1, WIDE), recv_source.reshape(1, PATCH_DEV))
    )
    waves = jnp.asarray(wave_tables())
    weights = jnp.concatenate([spectrum, spectrum])[:, None] / NX
    matrix = lax.dot_general(
        waves,
        waves * weights,
        (((0,), (0,)), ((), ())),
        precision=lax.Precision.HIGHEST,
        preferred_element_type=F32,
    )
    count = lax.axis_size("mid")
    forward = [(i, i + 1) for i in range(count - 1)]
    backward = [(i + 1, i) for i in range(count - 1)]
    pair = bf16_pair(matrix)
    parts, low, high, table = filter_exp(pair, lines)
    above = lax.ppermute(low, "mid", backward)
    below = lax.ppermute(high, "mid", forward)
    back = swap(parts)
    outgoing = windows(table, (low, high))
    outgoing = windows(table, (below, above), outgoing)
    outgoing, back = lax.optimization_barrier((outgoing, back))
    incoming = swap(outgoing)
    coefficient = join_rows(back)
    cores = table[0, recv_source.reshape(-1), lax.axis_index("wide")]
    later = jnp.repeat((cores >> 5) & 1, EDGE).reshape(1, LANES)
    solved = solve(incoming, later)
    return coefficient, solved.reshape(1, 1, PATCH_DEV, EDGE, EDGE * EDGE)


def solution(mesh):
    in_specs = (P("wide", "mid", None), P(), P("wide", "mid", None), P("wide", "mid", None))
    out_specs = (P("wide", "mid", None), P("wide", "mid", None, None, None))
    return jax.shard_map(
        on_device, mesh=mesh, in_specs=in_specs, out_specs=out_specs, check_vma=False
    )
```

```python
import functools
import math

import jax
import jax.numpy as jnp
import numpy as np
from jax import lax
from jax.experimental import pallas as pl
from jax.experimental.pallas import tpu as pltpu
from jax.sharding import PartitionSpec as P

NX = 512
NZ = 512
CY = 32
CX = 32
CORE = 16
LAYER = 16
WIDE = 16
PATCH_DEV = 8
EDGE = 48
TAPS = 3
LANES = PATCH_DEV * EDGE
SIDE = 128
TILES = NZ // SIDE
ROWS = 2 * TILES * CX
OWNERS = 4
UNROLL = 2
TINY = 1e-06
F32 = jnp.float32


def params(mebibytes):
    return pltpu.CompilerParams(vmem_limit_bytes=mebibytes * 1024 * 1024)


def full(shape):
    return jax.ShapeDtypeStruct(shape, F32)


def exchange(pieces):
    row = lax.broadcasted_iota(jnp.int32, pieces[0].shape, 0)
    pieces = list(pieces)
    for bit in (4, 2, 1):
        upper = (row & bit) != 0
        for i in range(8):
            k = i | bit
            if i == k:
                continue
            pieces[i], pieces[k] = (
                jnp.where(upper, pltpu.roll(pieces[k], bit, 0), pieces[i]),
                jnp.where(upper, pieces[k], pltpu.roll(pieces[i], 8 - bit, 0)),
            )
    return pieces


def split_kernel(in_ref, send_ref, source_ref, out_ref, held, sems):
    j = pl.program_id(0)

    def leave(t, tile):
        rows = pl.ds(pl.multiple_of((t * TILES + tile) * CX, CX), CX)
        return pltpu.make_async_copy(held.at[:, rows, :], out_ref.at[:, rows, :], sems.at[t, tile])

    def leave_tables():
        rows = pl.ds(ROWS, 8)
        return pltpu.make_async_copy(held.at[:, rows, :], out_ref.at[:, rows, :], sems.at[2, 0])

    @pl.when(j == 0)
    def _():
        for w in range(WIDE):
            held[w, ROWS:ROWS + 1, 0:WIDE] = send_ref[...].astype(F32)
            held[w, ROWS + 1:ROWS + 2, 0:PATCH_DEV] = source_ref[...].astype(F32)
        leave_tables().start()

    for t in range(2):
        first = pl.multiple_of((t * TILES + j) * CX, CX)
        for x in range(0, CX, 8):
            for y in range(0, WIDE, 8):
                at = t * WIDE + y
                pieces = exchange([in_ref[x + i, at:at + 8, :] for i in range(8)])
                for i in range(8):
                    held[y + i, pl.ds(first + x, 8), :] = pieces[i]
        leave(t, j).start()

    @pl.when(j == TILES - 1)
    def _():
        leave_tables().wait()
        for t in range(2):
            for tile in range(TILES):
                leave(t, tile).wait()


def split_rows(block, send, source):
    return pl.pallas_call(
        split_kernel,
        grid=(TILES,),
        in_specs=[
            pl.BlockSpec((CX, CY, SIDE), lambda j: (0, 0, j)),
            pl.BlockSpec((1, WIDE), lambda j: (0, 0)),
            pl.BlockSpec((1, PATCH_DEV), lambda j: (0, 0)),
        ],
        out_specs=pl.BlockSpec(memory_space=pl.ANY),
        out_shape=full((WIDE, ROWS + 8, SIDE)),
        scratch_shapes=[
            pltpu.VMEM((WIDE, ROWS + 8, SIDE), F32),
            pltpu.SemaphoreType.DMA((3, TILES)),
        ],
        compiler_params=params(56),
        cost_estimate=pl.CostEstimate(flops=0, bytes_accessed=8 << 20, transcendentals=0),
        name="split_rows",
    )(block, send, source)


def join_kernel(low_ref, high_ref, out_ref):
    for t, in_ref in enumerate((low_ref, high_ref)):
        for x in range(0, CX, 8):
            for y in range(0, WIDE, 8):
                pieces = exchange([in_ref[y + i, x:x + 8, :] for i in range(8)])
                for i in range(8):
                    out_ref[x + i, t * WIDE + y:t * WIDE + y + 8, :] = pieces[i]


def join_rows(parts):
    return pl.pallas_call(
        join_kernel,
        grid=(TILES,),
        in_specs=[
            pl.BlockSpec((WIDE, CX, SIDE), lambda j: (0, j, 0)),
            pl.BlockSpec((WIDE, CX, SIDE), lambda j: (0, TILES + j, 0)),
        ],
        out_specs=pl.BlockSpec((CX, CY, SIDE), lambda j: (0, 0, j)),
        out_shape=full((CX, CY, NZ)),
        compiler_params=params(12),
        cost_estimate=pl.CostEstimate(flops=0, bytes_accessed=8 << 20, transcendentals=0),
        name="join_rows",
    )(parts, parts)


def pair_kernel(in_ref, high_ref, low_ref):
    value = in_ref[...]
    high = value.astype(jnp.bfloat16)
    high_ref[...] = high
    low_ref[...] = (value - high.astype(F32)).astype(jnp.bfloat16)


def bf16_pair(matrix):
    return pl.pallas_call(
        pair_kernel,
        out_shape=[jax.ShapeDtypeStruct((NX, NX), jnp.bfloat16)] * 2,
        compiler_params=params(60),
        cost_estimate=pl.CostEstimate(flops=0, bytes_accessed=2 << 20, transcendentals=0),
        name="bf16_pair",
    )(matrix)


def filter_kernel(high_ref, low_ref, in_ref, extra_ref, parts_ref, first_ref, second_ref, table_ref):
    for k in range(2):
        table_ref[k] = extra_ref[:, k, :].astype(jnp.int32)
    lines = jnp.concatenate(
        [in_ref[:, 0:CX, :].reshape(NX, SIDE), in_ref[:, CX:, :].reshape(NX, SIDE)], axis=1
    )
    high = lines.astype(jnp.bfloat16)
    low = (lines - high.astype(F32)).astype(jnp.bfloat16)
    dot = lambda a, b: jnp.dot(a, b, preferred_element_type=F32)
    small = dot(high_ref[...], low) + dot(low_ref[...], high)
    value = jnp.exp(dot(high_ref[...], high) + small)
    sides = [value[:, :SIDE], value[:, SIDE:]]
    for k in range(2):
        parts_ref[:, k * CX:(k + 1) * CX, :] = sides[k].reshape(WIDE, CX, SIDE)

    def plane(ref):
        for k in range(2):
            ref[k] = 0.5 * sides[k]

    pl.when(pl.program_id(0) < 2)(lambda: plane(first_ref))
    pl.when(pl.program_id(0) >= 2)(lambda: plane(second_ref))


def filter_exp(pair, lines):
    whole = pl.BlockSpec((NX, NX), lambda i: (0, 0))
    block = pl.BlockSpec((WIDE, 2 * CX, SIDE), lambda i: (0, i, 0))
    return pl.pallas_call(
        filter_kernel,
        grid=(4,),
        in_specs=[whole, whole, block, pl.BlockSpec((WIDE, 8, SIDE), lambda i: (0, ROWS // 8, 0))],
        out_specs=[
            block,
            pl.BlockSpec((2, NX, SIDE), lambda i: (jnp.minimum(i, 1), 0, 0)),
            pl.BlockSpec((2, NX, SIDE), lambda i: (jnp.maximum(i - 2, 0), 0, 0)),
            pl.BlockSpec((2, WIDE, SIDE), lambda i: (0, 0, 0)),
        ],
        out_shape=[
            full((WIDE, ROWS, SIDE)),
            full((TILES, NX, SIDE)),
            full((TILES, NX, SIDE)),
            jax.ShapeDtypeStruct((2, WIDE, SIDE), jnp.int32),
        ],
        compiler_params=params(60),
        cost_estimate=pl.CostEstimate(
            flops=12 * NX * NX * NZ, bytes_accessed=8 << 20, transcendentals=2 * NX * NZ
        ),
        name="filter_exp",
    )(*pair, lines, lines)


def window_kernel(slots, table_ref, *refs):
    low_ref, high_ref = refs[:2]
    out_ref, held, sems = refs[-3:]
    step = pl.program_id(0)

    @pl.when(step == 0)
    def _():
        copies = [
            pltpu.make_async_copy(
                src, held.at[t, pl.ds(1, TILES), pl.ds(LAYER, NX), :], sems.at[t]
            )
            for t, src in enumerate((low_ref, high_ref))
        ]
        for copy in copies:
            copy.start()
        side = jnp.zeros((NX + 2 * LAYER, SIDE), F32)
        for t in range(2):
            held[t, 0] = side
            held[t, TILES + 1] = side
            for j in range(TILES):
                held[t, 1 + j, 0:LAYER, :] = side[:LAYER]
                held[t, 1 + j, LAYER + NX:, :] = side[:LAYER]
        for copy in copies:
            copy.wait()

    lane = lax.broadcasted_iota(jnp.int32, (EDGE, SIDE), 1)

    def one_owner(k, _):
        owner = step * OWNERS + k
        places = []
        for p in range(PATCH_DEV):
            source = table_ref[1, owner, p]
            core = jnp.maximum(table_ref[0, source, owner], 0)
            x_at = source * CX + (core >> 6) * CORE
            z_at = (core & 31) * CORE + (SIDE - LAYER)
            offset = z_at & (SIDE - 1)
            turn = ((p * EDGE) % SIDE - offset) & (SIDE - 1)
            places.append((pl.multiple_of(x_at, CORE), (core >> 5) & 1, z_at >> 7, offset, turn))
        for t in range(slots):
            tiles = [None] * 3
            for p, (x_at, t_at, tile, offset, turn) in enumerate(places):
                plane = t if slots == 2 else t_at
                rows = pl.ds(x_at, EDGE)
                near = held[plane, tile, rows, :]
                far = held[plane, tile + 1, rows, :]
                moved = pltpu.roll(jnp.where(lane >= offset, near, far), turn, 1)
                at = (p * EDGE) % SIDE
                q = (p * EDGE) // SIDE
                tiles[q] = moved if at == 0 else jnp.where(lane >= at, moved, tiles[q])
                if at + EDGE > SIDE:
                    tiles[q + 1] = moved
            for q in range(3):
                out_ref[k, t * EDGE:(t + 1) * EDGE, q * SIDE:(q + 1) * SIDE] = tiles[q]
        return 0

    lax.fori_loop(0, OWNERS, one_owner, 0, unroll=UNROLL)


def windows(table, planes, *others):
    slots = 1 if others else 2
    at = 2 if others else 0
    return pl.pallas_call(
        functools.partial(window_kernel, slots),
        grid_spec=pltpu.PrefetchScalarGridSpec(
            num_scalar_prefetch=1,
            grid=(WIDE // OWNERS,),
            in_specs=[pl.BlockSpec(memory_space=pl.ANY)] * (2 + len(others)),
            out_specs=pl.BlockSpec((OWNERS, slots * EDGE, LANES), lambda d, table: (d, at, 0)),
            scratch_shapes=[
                pltpu.VMEM((2, TILES + 2, NX + 2 * LAYER, SIDE), F32),
                pltpu.SemaphoreType.DMA((2,)),
            ],
        ),
        out_shape=full((WIDE, TAPS * EDGE, LANES)),
        input_output_aliases={3: 0} if others else {},
        compiler_params=params(58 if others else 60),
        cost_estimate=pl.CostEstimate(
            flops=0, bytes_accessed=slots * (6 << 20), transcendentals=0
        ),
        name="patch_windows",
    )(table, *planes, *others)


STRIPS = EDGE // 8
SLABS = 3
GROUPS = EDGE // 8
PIECES = [(i, q) for i in range(STRIPS) for q in range(3)]


def piece(i, q):
    return (pl.ds(8 * i, 8), pl.ds(SIDE * q, SIDE))


def solve_kernel(
    half_ref, later_ref, out_ref, half, first, image, heavy, face_x, face_y, face_z, ready, arrive, leave
):
    arrivals = [
        [
            pltpu.make_async_copy(
                half_ref.at[pl.ds(4 * g, 4), pl.ds(t * EDGE, EDGE), :],
                (heavy, face_x, face_y)[t].at[pl.ds(4 * g, 4)],
                arrive.at[g, t],
            )
            for t in range(TAPS)
        ]
        for g in range(WIDE // 4)
    ]
    for group in arrivals:
        for copy in group:
            copy.start()
    none = jnp.zeros((8, SIDE), F32)
    for at in PIECES:
        half[0, *piece(*at)] = none
        half[EDGE + 1, *piece(*at)] = none
        first[EDGE, *piece(*at)] = none
        image[EDGE, *piece(*at)] = none

    row = lax.broadcasted_iota(jnp.int32, (8, SIDE), 0)
    lane = lax.broadcasted_iota(jnp.int32, (8, SIDE), 1)
    row_low, row_high = row == 0, row == 7
    lane_low, lane_high = lane == 0, lane == SIDE - 1
    depth = []
    for q in range(3):
        place = lane + q * SIDE
        depth.append(place - ((place * 1366) >> 16) * EDGE)
    z_low = [d == 0 for d in depth]
    z_high = [d == EDGE - 1 for d in depth]

    def above_x(slab):
        turned = {at: pltpu.roll(slab[at], 7, 0) for at in PIECES}
        return {
            (i, q): jnp.where(row_high, turned[i + 1, q] if i < STRIPS - 1 else 0.0, turned[i, q])
            for i, q in PIECES
        }

    def below_x(slab):
        turned = {at: pltpu.roll(slab[at], 1, 0) for at in PIECES}
        return {
            (i, q): jnp.where(row_low, turned[i - 1, q] if i else 0.0, turned[i, q])
            for i, q in PIECES
        }

    def above_z(strip):
        turned = [pltpu.roll(v, SIDE - 1, 1) for v in strip]
        return [
            jnp.where(lane_high, turned[1], turned[0]),
            jnp.where(lane_high, turned[2], turned[1]),
            turned[2],
        ]

    def below_z(strip):
        turned = [pltpu.roll(v, 1, 1) for v in strip]
        return [
            jnp.where(lane_low, 0.0, turned[0]),
            jnp.where(lane_low, turned[0], turned[1]),
            jnp.where(lane_low, turned[1], turned[2]),
        ]

    def load(ref, y):
        return {at: ref[y, *piece(*at)] for at in PIECES}

    def strip(slab, i):
        return [slab[i, q] for q in range(3)]

    same = jnp.where(
        ((lax.broadcasted_iota(jnp.int32, (LANES, LANES), 0) * 1366) >> 16)
        == ((lax.broadcasted_iota(jnp.int32, (LANES, LANES), 1) * 1366) >> 16),
        1.0,
        0.0,
    ).astype(jnp.bfloat16)

    def patch_total(parts):
        part = jnp.concatenate(parts, axis=1)
        high = part.astype(jnp.bfloat16).astype(F32)
        middle = (part - high).astype(jnp.bfloat16).astype(F32)
        low = part - high - middle
        stack = jnp.concatenate([high, middle, low, jnp.zeros_like(low)], axis=0)
        spread = jnp.dot(stack.astype(jnp.bfloat16), same, preferred_element_type=F32)
        total = jnp.sum(spread, axis=0, keepdims=True)
        return [
            jnp.broadcast_to(total[:, SIDE * q:SIDE * (q + 1)], (8, SIDE)) for q in range(3)
        ]

    def divide(top, bottom):
        return [t / (b + TINY) for t, b in zip(top, bottom)]

    nothing = (none, none, none)

    in_order = [
        jnp.broadcast_to(later_ref[:, SIDE * q:SIDE * (q + 1)], (8, SIDE)) != 0 for q in range(3)
    ]

    def arrange(w, _):
        for i, q in PIECES:
            at = piece(i, q)
            a, b, c = heavy[w, *at], face_x[w, *at], face_y[w, *at]
            half[1 + w, *at] = jnp.where(in_order[q], a, c)
            half[1 + WIDE + w, *at] = jnp.where(in_order[q], b, a)
            half[1 + 2 * WIDE + w, *at] = jnp.where(in_order[q], c, b)
        return 0

    for g, group in enumerate(arrivals):
        for copy in group:
            copy.wait()
        lax.fori_loop(4 * g, 4 * g + 4, arrange, 0, unroll=2)

    def faces_of(y, rr):
        rr = list(rr)
        h = load(half, y + 1)
        h_up = above_x(h)
        h_down = below_x(h)
        deep_up, deep_down = {}, {}
        for i in range(STRIPS):
            ups, downs = above_z(strip(h, i)), below_z(strip(h, i))
            for q in range(3):
                deep_up[i, q] = jnp.where(z_high[q], 0.0, ups[q])
                deep_down[i, q] = jnp.where(z_low[q], 0.0, downs[q])
        up_up, up_down = above_x(deep_up), below_x(deep_up)
        down_up, down_down = above_x(deep_down), below_x(deep_down)
        for i, q in PIECES:
            here, to = h[i, q], piece(i, q)
            z_up, z_down = deep_up[i, q], deep_down[i, q]
            v = h_up[i, q] - h_down[i, q]
            y_up = half[y + 2, *to]
            y_down = half[y, *to]
            across = here + h_up[i, q]
            if i == STRIPS - 1:
                across = jnp.where(row_high, 0.0, across)
            deep = here + z_up
            heavy[y, *to] = (
                (1.0 + 6.0 * here) + (h_up[i, q] + h_down[i, q])
                + ((y_up + y_down) + (z_up + z_down))
            )
            face_x[y, *to] = across
            face_y[y + 1, *to] = here + y_up
            face_z[y, *to] = jnp.where(z_high[q], 0.0, deep)
            first[y, *to] = v
            image[y, *to] = deep * (up_up[i, q] - up_down[i, q]) + (here + z_down) * (
                down_up[i, q] - down_down[i, q]
            )
            rr[q] = rr[q] + v * v
        return tuple(rr)

    rr = lax.fori_loop(0, EDGE, faces_of, nothing, unroll=3)
    for at in PIECES:
        face_y[0, *piece(*at)] = none
        face_y[EDGE, *piece(*at)] = none
    rr = patch_total(rr)

    def image_of(y, total):
        total = list(total)
        v = load(first, y)
        v_up = above_x(v)
        across = load(face_x, y)
        from_x = below_x({at: across[at] * v[at] for at in PIECES})
        for i, q in PIECES:
            to = piece(i, q)
            couple = across[i, q] * v_up[i, q] + from_x[i, q]
            couple = couple + face_y[y + 1, *to] * first[y + 1, *to]
            couple = couple + face_y[y, *to] * first[jnp.maximum(y - 1, 0), *to]
            result = heavy[y, *to] * v[i, q] - (couple + image[y, *to])
            image[y, *to] = result
            total[q] = total[q] + v[i, q] * result
        return tuple(total)

    alpha = divide(rr, patch_total(lax.fori_loop(0, EDGE, image_of, nothing, unroll=3)))

    def residual_of(y, total):
        total = list(total)
        for i, q in PIECES:
            left = first[y, *piece(i, q)] - alpha[q] * image[y, *piece(i, q)]
            total[q] = total[q] + left * left
        return tuple(total)

    new = patch_total(lax.fori_loop(0, EDGE, residual_of, nothing, unroll=4))
    beta = divide(new, rr)

    def direction(y, i, q):
        v = first[y, *piece(i, q)]
        return (v - alpha[q] * image[y, *piece(i, q)]) + beta[q] * v

    for at in PIECES:
        ready[0, *piece(*at)] = direction(0, *at)

    def energy_of(step, total):
        total = list(total)
        v = load(ready, 0)
        for k in range(SLABS):
            y = step * SLABS + k
            v_up = above_x(v)
            v_next = {at: direction(y + 1, *at) for at in PIECES}
            for i in range(STRIPS):
                ups = above_z(strip(v, i))
                for q in range(3):
                    to = piece(i, q)
                    couple = face_x[y, *to] * v_up[i, q]
                    couple = couple + face_y[y + 1, *to] * v_next[i, q]
                    couple = couple + face_z[y, *to] * ups[q]
                    total[q] = total[q] + v[i, q] * (heavy[y, *to] * v[i, q] - 2.0 * couple)
            v = v_next
        for at in PIECES:
            ready[0, *piece(*at)] = v[at]
        return tuple(total)

    energy = lax.fori_loop(0, EDGE // SLABS, energy_of, nothing)
    alpha_next = divide(new, patch_total(energy))
    on_first = [alpha[q] + alpha_next[q] * (1.0 + beta[q]) for q in range(3)]
    on_image = [-(alpha_next[q] * alpha[q]) for q in range(3)]

    ends = [lane < end for end in (48, 96, 16, 64, 112, 32, 80)]

    def gather(c):
        return (
            jnp.where(ends[0], c[0][0], jnp.where(ends[1], c[1][0], c[2][0])),
            jnp.where(
                ends[2],
                c[2][1],
                jnp.where(ends[3], c[3][1], jnp.where(ends[4], c[4][1], c[5][1])),
            ),
            jnp.where(ends[5], c[5][2], jnp.where(ends[6], c[6][2], c[7][2])),
        )

    departures = []
    for group in range(GROUPS):

        def correct(i, _):
            rows = pl.ds(pl.multiple_of(8 * i, 8), 8)
            lines = []
            for j in range(8):
                y = 8 * group + j
                lines.append([
                    on_first[q] * first[y, rows, pl.ds(SIDE * q, SIDE)]
                    + on_image[q] * image[y, rows, pl.ds(SIDE * q, SIDE)]
                    for q in range(3)
                ])
            turned = []
            for k in range(8):
                a, b, c = gather([lines[(p + k) % 8] for p in range(8)])
                far, near = divmod(EDGE * k, SIDE)
                r = [pltpu.roll(v, near, 1) if near else v for v in (a, b, c)]
                r = [r[(q - far) % 3] for q in range(3)]
                before = [r[2], r[0], r[1]]
                if near:
                    r = [jnp.where(lane < near, before[q], r[q]) for q in range(3)]
                turned.append(r)
            for p in range(PATCH_DEV):
                tiles = gather([turned[(j - p) % 8] for j in range(8)])
                for q in range(3):
                    heavy[8 * group + p, rows, pl.ds(SIDE * q, SIDE)] = tiles[q]
            return 0

        lax.fori_loop(0, STRIPS, correct, 0, unroll=True)
        departures.append(
            pltpu.make_async_copy(
                heavy.at[pl.ds(8 * group, PATCH_DEV)],
                out_ref.at[:, :, pl.ds(group * LANES, LANES)],
                leave.at[group],
            )
        )
        departures[-1].start()
    for copy in departures:
        copy.wait()


def solve(half, later):
    cube = pltpu.VMEM((EDGE, EDGE, LANES), F32)
    longer = pltpu.VMEM((EDGE + 1, EDGE, LANES), F32)
    return pl.pallas_call(
        solve_kernel,
        in_specs=[pl.BlockSpec(memory_space=pl.ANY), pl.BlockSpec(memory_space=pltpu.VMEM)],
        out_specs=pl.BlockSpec(memory_space=pl.ANY),
        out_shape=full((PATCH_DEV, EDGE, EDGE * EDGE)),
        scratch_shapes=[
            pltpu.VMEM((EDGE + 2, EDGE, LANES), F32),
            longer,
            longer,
            cube,
            cube,
            longer,
            cube,
            pltpu.VMEM((1, EDGE, LANES), F32),
            pltpu.SemaphoreType.DMA((WIDE // 4, TAPS)),
            pltpu.SemaphoreType.DMA((GROUPS,)),
        ],
        compiler_params=params(40),
        cost_estimate=pl.CostEstimate(
            flops=60 * EDGE**3 * PATCH_DEV, bytes_accessed=32 << 20, transcendentals=0
        ),
        name="solve_patches",
    )(half, later)


def wave_tables():
    index = np.arange(NX, dtype=np.int64)
    angle = (index[:, None] * index[None, :] % NX) * (2.0 * math.pi / NX)
    waves = np.concatenate([np.cos(angle), np.sin(angle)], axis=0)
    return waves.astype(np.float32)


def on_device(noise, spectrum, send_core, recv_source):
    swap = lambda v: lax.all_to_all(v, "wide", split_axis=0, concat_axis=0)
    lines = swap(
        split_rows(noise, send_core.reshape(1, WIDE), recv_source.reshape(1, PATCH_DEV))
    )
    waves = jnp.asarray(wave_tables())
    weights = jnp.concatenate([spectrum, spectrum])[:, None] / NX
    matrix = lax.dot_general(
        waves,
        waves * weights,
        (((0,), (0,)), ((), ())),
        precision=lax.Precision.HIGHEST,
        preferred_element_type=F32,
    )
    count = lax.axis_size("mid")
    forward = [(i, i + 1) for i in range(count - 1)]
    backward = [(i + 1, i) for i in range(count - 1)]
    pair = bf16_pair(matrix)
    parts, low, high, table = filter_exp(pair, lines)
    above = lax.ppermute(low, "mid", backward)
    below = lax.ppermute(high, "mid", forward)
    back = swap(parts)
    outgoing = windows(table, (low, high))
    outgoing = windows(table, (below, above), outgoing)
    outgoing, back = lax.optimization_barrier((outgoing, back))
    incoming = swap(outgoing)
    coefficient = join_rows(back)
    cores = table[0, recv_source.reshape(-1), lax.axis_index("wide")]
    later = jnp.repeat((cores >> 5) & 1, EDGE).reshape(1, LANES)
    solved = solve(incoming, later)
    return coefficient, solved.reshape(1, 1, PATCH_DEV, EDGE, EDGE * EDGE)


def solution(mesh):
    in_specs = (P("wide", "mid", None), P(), P("wide", "mid", None), P("wide", "mid", None))
    out_specs = (P("wide", "mid", None), P("wide", "mid", None, None, None))
    return jax.shard_map(
        on_device, mesh=mesh, in_specs=in_specs, out_specs=out_specs, check_vma=False
    )
```

```python
import functools
import math

import jax
import jax.numpy as jnp
import numpy as np
from jax import lax
from jax.experimental import pallas as pl
from jax.experimental.pallas import tpu as pltpu
from jax.sharding import PartitionSpec as P

NX = 512
NZ = 512
CY = 32
CX = 32
CORE = 16
LAYER = 16
WIDE = 16
PATCH_DEV = 8
EDGE = 48
TAPS = 3
LANES = PATCH_DEV * EDGE
SIDE = 128
TILES = NZ // SIDE
ROWS = 2 * TILES * CX
OWNERS = 4
UNROLL = 2
TINY = 1e-06
F32 = jnp.float32


def params(mebibytes):
    return pltpu.CompilerParams(vmem_limit_bytes=mebibytes * 1024 * 1024)


def full(shape):
    return jax.ShapeDtypeStruct(shape, F32)


def exchange(pieces):
    row = lax.broadcasted_iota(jnp.int32, pieces[0].shape, 0)
    pieces = list(pieces)
    for bit in (4, 2, 1):
        upper = (row & bit) != 0
        for i in range(8):
            k = i | bit
            if i == k:
                continue
            pieces[i], pieces[k] = (
                jnp.where(upper, pltpu.roll(pieces[k], bit, 0), pieces[i]),
                jnp.where(upper, pieces[k], pltpu.roll(pieces[i], 8 - bit, 0)),
            )
    return pieces


def split_kernel(in_ref, send_ref, source_ref, out_ref, held, sems):
    j = pl.program_id(0)

    def leave(t, tile):
        rows = pl.ds(pl.multiple_of((t * TILES + tile) * CX, CX), CX)
        return pltpu.make_async_copy(held.at[:, rows, :], out_ref.at[:, rows, :], sems.at[t, tile])

    def leave_tables():
        rows = pl.ds(ROWS, 8)
        return pltpu.make_async_copy(held.at[:, rows, :], out_ref.at[:, rows, :], sems.at[2, 0])

    @pl.when(j == 0)
    def _():
        for w in range(WIDE):
            held[w, ROWS:ROWS + 1, 0:WIDE] = send_ref[...].astype(F32)
            held[w, ROWS + 1:ROWS + 2, 0:PATCH_DEV] = source_ref[...].astype(F32)
        leave_tables().start()

    for t in range(2):
        first = pl.multiple_of((t * TILES + j) * CX, CX)
        for x in range(0, CX, 8):
            for y in range(0, WIDE, 8):
                at = t * WIDE + y
                pieces = exchange([in_ref[x + i, at:at + 8, :] for i in range(8)])
                for i in range(8):
                    held[y + i, pl.ds(first + x, 8), :] = pieces[i]
        leave(t, j).start()

    @pl.when(j == TILES - 1)
    def _():
        leave_tables().wait()
        for t in range(2):
            for tile in range(TILES):
                leave(t, tile).wait()


def split_rows(block, send, source):
    return pl.pallas_call(
        split_kernel,
        grid=(TILES,),
        in_specs=[
            pl.BlockSpec((CX, CY, SIDE), lambda j: (0, 0, j)),
            pl.BlockSpec((1, WIDE), lambda j: (0, 0)),
            pl.BlockSpec((1, PATCH_DEV), lambda j: (0, 0)),
        ],
        out_specs=pl.BlockSpec(memory_space=pl.ANY),
        out_shape=full((WIDE, ROWS + 8, SIDE)),
        scratch_shapes=[
            pltpu.VMEM((WIDE, ROWS + 8, SIDE), F32),
            pltpu.SemaphoreType.DMA((3, TILES)),
        ],
        compiler_params=params(56),
        cost_estimate=pl.CostEstimate(flops=0, bytes_accessed=8 << 20, transcendentals=0),
        name="split_rows",
    )(block, send, source)


def join_kernel(low_ref, high_ref, out_ref):
    for t, in_ref in enumerate((low_ref, high_ref)):
        for x in range(0, CX, 8):
            for y in range(0, WIDE, 8):
                pieces = exchange([in_ref[y + i, x:x + 8, :] for i in range(8)])
                for i in range(8):
                    out_ref[x + i, t * WIDE + y:t * WIDE + y + 8, :] = pieces[i]


def join_rows(parts):
    return pl.pallas_call(
        join_kernel,
        grid=(TILES,),
        in_specs=[
            pl.BlockSpec((WIDE, CX, SIDE), lambda j: (0, j, 0)),
            pl.BlockSpec((WIDE, CX, SIDE), lambda j: (0, TILES + j, 0)),
        ],
        out_specs=pl.BlockSpec((CX, CY, SIDE), lambda j: (0, 0, j)),
        out_shape=full((CX, CY, NZ)),
        compiler_params=params(12),
        cost_estimate=pl.CostEstimate(flops=0, bytes_accessed=8 << 20, transcendentals=0),
        name="join_rows",
    )(parts, parts)


def pair_kernel(in_ref, high_ref, low_ref):
    value = in_ref[...]
    high = value.astype(jnp.bfloat16)
    high_ref[...] = high
    low_ref[...] = (value - high.astype(F32)).astype(jnp.bfloat16)


def bf16_pair(matrix):
    return pl.pallas_call(
        pair_kernel,
        out_shape=[jax.ShapeDtypeStruct((NX, NX), jnp.bfloat16)] * 2,
        compiler_params=params(60),
        cost_estimate=pl.CostEstimate(flops=0, bytes_accessed=2 << 20, transcendentals=0),
        name="bf16_pair",
    )(matrix)


def filter_kernel(odd_ref, high_ref, low_ref, in_ref, extra_ref, parts_ref, first_ref, second_ref, table_ref):
    for k in range(2):
        table_ref[k] = extra_ref[:, k, :].astype(jnp.int32)
    lines = jnp.concatenate(
        [in_ref[:, 0:CX, :].reshape(NX, SIDE), in_ref[:, CX:, :].reshape(NX, SIDE)], axis=1
    )
    high = lines.astype(jnp.bfloat16)
    low = (lines - high.astype(F32)).astype(jnp.bfloat16)
    dot = lambda a, b: jnp.dot(a, b, preferred_element_type=F32)
    small = dot(high_ref[...], low) + dot(low_ref[...], high)
    value = jnp.exp(dot(high_ref[...], high) + small)
    sides = [value[:, :SIDE], value[:, SIDE:]]
    for k in range(2):
        parts_ref[:, k * CX:(k + 1) * CX, :] = sides[k].reshape(WIDE, CX, SIDE)

    def plane(ref):
        for k in range(2):
            ref[k] = 0.5 * sides[k]

    pl.when(pl.program_id(0) < 2)(lambda: plane(first_ref))
    pl.when(pl.program_id(0) >= 2)(lambda: plane(second_ref))


def filter_exp(odd, pair, lines):
    whole = pl.BlockSpec((NX, NX), lambda i, odd: (0, 0))
    block = pl.BlockSpec(
        (WIDE, 2 * CX, SIDE), lambda i, odd: (0, 2 * ((i >> 1) ^ odd[0]) + (i & 1), 0)
    )
    return pl.pallas_call(
        filter_kernel,
        grid_spec=pltpu.PrefetchScalarGridSpec(
            num_scalar_prefetch=1,
            grid=(4,),
            in_specs=[
                whole,
                whole,
                block,
                pl.BlockSpec((WIDE, 8, SIDE), lambda i, odd: (0, ROWS // 8, 0)),
            ],
            out_specs=[
                block,
                pl.BlockSpec((2, NX, SIDE), lambda i, odd: (jnp.minimum(i, 1), 0, 0)),
                pl.BlockSpec((2, NX, SIDE), lambda i, odd: (jnp.maximum(i - 2, 0), 0, 0)),
                pl.BlockSpec((2, WIDE, SIDE), lambda i, odd: (0, 0, 0)),
            ],
        ),
        out_shape=[
            full((WIDE, ROWS, SIDE)),
            full((TILES, NX, SIDE)),
            full((TILES, NX, SIDE)),
            jax.ShapeDtypeStruct((2, WIDE, SIDE), jnp.int32),
        ],
        compiler_params=params(60),
        cost_estimate=pl.CostEstimate(
            flops=12 * NX * NX * NZ, bytes_accessed=8 << 20, transcendentals=2 * NX * NZ
        ),
        name="filter_exp",
    )(odd, *pair, lines, lines)


def window_kernel(slots, table_ref, odd_ref, *refs):
    low_ref, high_ref = refs[:2]
    out_ref, held, sems = refs[-3:]
    step = pl.program_id(0)

    @pl.when(step == 0)
    def _():
        copies = [
            pltpu.make_async_copy(
                src, held.at[t, pl.ds(1, TILES), pl.ds(LAYER, NX), :], sems.at[t]
            )
            for t, src in enumerate((low_ref, high_ref))
        ]
        for copy in copies:
            copy.start()
        side = jnp.zeros((NX + 2 * LAYER, SIDE), F32)
        for t in range(2):
            held[t, 0] = side
            held[t, TILES + 1] = side
            for j in range(TILES):
                held[t, 1 + j, 0:LAYER, :] = side[:LAYER]
                held[t, 1 + j, LAYER + NX:, :] = side[:LAYER]
        for copy in copies:
            copy.wait()

    lane = lax.broadcasted_iota(jnp.int32, (EDGE, SIDE), 1)

    def one_owner(k, _):
        owner = step * OWNERS + k
        places = []
        for p in range(PATCH_DEV):
            source = table_ref[1, owner, p]
            core = jnp.maximum(table_ref[0, source, owner], 0)
            x_at = source * CX + (core >> 6) * CORE
            z_at = (core & 31) * CORE + (SIDE - LAYER)
            offset = z_at & (SIDE - 1)
            turn = ((p * EDGE) % SIDE - offset) & (SIDE - 1)
            places.append((pl.multiple_of(x_at, CORE), (core >> 5) & 1, z_at >> 7, offset, turn))
        for t in range(slots):
            tiles = [None] * 3
            for p, (x_at, t_at, tile, offset, turn) in enumerate(places):
                plane = (t if slots == 2 else t_at) ^ odd_ref[0]
                rows = pl.ds(x_at, EDGE)
                near = held[plane, tile, rows, :]
                far = held[plane, tile + 1, rows, :]
                moved = pltpu.roll(jnp.where(lane >= offset, near, far), turn, 1)
                at = (p * EDGE) % SIDE
                q = (p * EDGE) // SIDE
                tiles[q] = moved if at == 0 else jnp.where(lane >= at, moved, tiles[q])
                if at + EDGE > SIDE:
                    tiles[q + 1] = moved
            for q in range(3):
                out_ref[k, t * EDGE:(t + 1) * EDGE, q * SIDE:(q + 1) * SIDE] = tiles[q]
        return 0

    lax.fori_loop(0, OWNERS, one_owner, 0, unroll=UNROLL)


def windows(table, odd, planes, *others):
    slots = 1 if others else 2
    at = 2 if others else 0
    return pl.pallas_call(
        functools.partial(window_kernel, slots),
        grid_spec=pltpu.PrefetchScalarGridSpec(
            num_scalar_prefetch=2,
            grid=(WIDE // OWNERS,),
            in_specs=[pl.BlockSpec(memory_space=pl.ANY)] * (2 + len(others)),
            out_specs=pl.BlockSpec((OWNERS, slots * EDGE, LANES), lambda d, table, odd: (d, at, 0)),
            scratch_shapes=[
                pltpu.VMEM((2, TILES + 2, NX + 2 * LAYER, SIDE), F32),
                pltpu.SemaphoreType.DMA((2,)),
            ],
        ),
        out_shape=full((WIDE, TAPS * EDGE, LANES)),
        input_output_aliases={4: 0} if others else {},
        compiler_params=params(58 if others else 60),
        cost_estimate=pl.CostEstimate(
            flops=0, bytes_accessed=slots * (6 << 20), transcendentals=0
        ),
        name="patch_windows",
    )(table, odd, *planes, *others)


STRIPS = EDGE // 8
SLABS = 3
GROUPS = EDGE // 8
PIECES = [(i, q) for i in range(STRIPS) for q in range(3)]


def piece(i, q):
    return (pl.ds(8 * i, 8), pl.ds(SIDE * q, SIDE))


def solve_kernel(
    half_ref, later_ref, out_ref, half, first, image, heavy, face_x, face_y, face_z, ready, arrive, leave
):
    arrivals = [
        [
            pltpu.make_async_copy(
                half_ref.at[pl.ds(4 * g, 4), pl.ds(t * EDGE, EDGE), :],
                (heavy, face_x, face_y)[t].at[pl.ds(4 * g, 4)],
                arrive.at[g, t],
            )
            for t in range(TAPS)
        ]
        for g in range(WIDE // 4)
    ]
    for group in arrivals:
        for copy in group:
            copy.start()
    none = jnp.zeros((8, SIDE), F32)
    for at in PIECES:
        half[0, *piece(*at)] = none
        half[EDGE + 1, *piece(*at)] = none
        first[EDGE, *piece(*at)] = none
        image[EDGE, *piece(*at)] = none

    row = lax.broadcasted_iota(jnp.int32, (8, SIDE), 0)
    lane = lax.broadcasted_iota(jnp.int32, (8, SIDE), 1)
    row_low, row_high = row == 0, row == 7
    lane_low, lane_high = lane == 0, lane == SIDE - 1
    depth = []
    for q in range(3):
        place = lane + q * SIDE
        depth.append(place - ((place * 1366) >> 16) * EDGE)
    z_low = [d == 0 for d in depth]
    z_high = [d == EDGE - 1 for d in depth]

    def above_x(slab):
        turned = {at: pltpu.roll(slab[at], 7, 0) for at in PIECES}
        return {
            (i, q): jnp.where(row_high, turned[i + 1, q] if i < STRIPS - 1 else 0.0, turned[i, q])
            for i, q in PIECES
        }

    def below_x(slab):
        turned = {at: pltpu.roll(slab[at], 1, 0) for at in PIECES}
        return {
            (i, q): jnp.where(row_low, turned[i - 1, q] if i else 0.0, turned[i, q])
            for i, q in PIECES
        }

    def above_z(strip):
        turned = [pltpu.roll(v, SIDE - 1, 1) for v in strip]
        return [
            jnp.where(lane_high, turned[1], turned[0]),
            jnp.where(lane_high, turned[2], turned[1]),
            turned[2],
        ]

    def below_z(strip):
        turned = [pltpu.roll(v, 1, 1) for v in strip]
        return [
            jnp.where(lane_low, 0.0, turned[0]),
            jnp.where(lane_low, turned[0], turned[1]),
            jnp.where(lane_low, turned[1], turned[2]),
        ]

    def load(ref, y):
        return {at: ref[y, *piece(*at)] for at in PIECES}

    def strip(slab, i):
        return [slab[i, q] for q in range(3)]

    same = jnp.where(
        ((lax.broadcasted_iota(jnp.int32, (LANES, LANES), 0) * 1366) >> 16)
        == ((lax.broadcasted_iota(jnp.int32, (LANES, LANES), 1) * 1366) >> 16),
        1.0,
        0.0,
    ).astype(jnp.bfloat16)

    def patch_total(parts):
        part = jnp.concatenate(parts, axis=1)
        high = part.astype(jnp.bfloat16).astype(F32)
        middle = (part - high).astype(jnp.bfloat16).astype(F32)
        low = part - high - middle
        stack = jnp.concatenate([high, middle, low, jnp.zeros_like(low)], axis=0)
        spread = jnp.dot(stack.astype(jnp.bfloat16), same, preferred_element_type=F32)
        total = jnp.sum(spread, axis=0, keepdims=True)
        return [
            jnp.broadcast_to(total[:, SIDE * q:SIDE * (q + 1)], (8, SIDE)) for q in range(3)
        ]

    def divide(top, bottom):
        return [t / (b + TINY) for t, b in zip(top, bottom)]

    nothing = (none, none, none)

    in_order = [
        jnp.broadcast_to(later_ref[:, SIDE * q:SIDE * (q + 1)], (8, SIDE)) != 0 for q in range(3)
    ]

    def arrange(w, _):
        for i, q in PIECES:
            at = piece(i, q)
            a, b, c = heavy[w, *at], face_x[w, *at], face_y[w, *at]
            half[1 + w, *at] = jnp.where(in_order[q], a, c)
            half[1 + WIDE + w, *at] = jnp.where(in_order[q], b, a)
            half[1 + 2 * WIDE + w, *at] = jnp.where(in_order[q], c, b)
        return 0

    for g, group in enumerate(arrivals):
        for copy in group:
            copy.wait()
        lax.fori_loop(4 * g, 4 * g + 4, arrange, 0, unroll=2)

    def faces_of(y, rr):
        rr = list(rr)
        h = load(half, y + 1)
        h_up = above_x(h)
        h_down = below_x(h)
        deep_up, deep_down = {}, {}
        for i in range(STRIPS):
            ups, downs = above_z(strip(h, i)), below_z(strip(h, i))
            for q in range(3):
                deep_up[i, q] = jnp.where(z_high[q], 0.0, ups[q])
                deep_down[i, q] = jnp.where(z_low[q], 0.0, downs[q])
        up_up, up_down = above_x(deep_up), below_x(deep_up)
        down_up, down_down = above_x(deep_down), below_x(deep_down)
        for i, q in PIECES:
            here, to = h[i, q], piece(i, q)
            z_up, z_down = deep_up[i, q], deep_down[i, q]
            v = h_up[i, q] - h_down[i, q]
            y_up = half[y + 2, *to]
            y_down = half[y, *to]
            across = here + h_up[i, q]
            if i == STRIPS - 1:
                across = jnp.where(row_high, 0.0, across)
            deep = here + z_up
            heavy[y, *to] = (
                (1.0 + 6.0 * here) + (h_up[i, q] + h_down[i, q])
                + ((y_up + y_down) + (z_up + z_down))
            )
            face_x[y, *to] = across
            face_y[y + 1, *to] = here + y_up
            face_z[y, *to] = jnp.where(z_high[q], 0.0, deep)
            first[y, *to] = v
            image[y, *to] = deep * (up_up[i, q] - up_down[i, q]) + (here + z_down) * (
                down_up[i, q] - down_down[i, q]
            )
            rr[q] = rr[q] + v * v
        return tuple(rr)

    rr = lax.fori_loop(0, EDGE, faces_of, nothing, unroll=3)
    for at in PIECES:
        face_y[0, *piece(*at)] = none
        face_y[EDGE, *piece(*at)] = none
    rr = patch_total(rr)

    def image_of(y, total):
        total = list(total)
        v = load(first, y)
        v_up = above_x(v)
        across = load(face_x, y)
        from_x = below_x({at: across[at] * v[at] for at in PIECES})
        for i, q in PIECES:
            to = piece(i, q)
            couple = across[i, q] * v_up[i, q] + from_x[i, q]
            couple = couple + face_y[y + 1, *to] * first[y + 1, *to]
            couple = couple + face_y[y, *to] * first[jnp.maximum(y - 1, 0), *to]
            result = heavy[y, *to] * v[i, q] - (couple + image[y, *to])
            image[y, *to] = result
            total[q] = total[q] + v[i, q] * result
        return tuple(total)

    alpha = divide(rr, patch_total(lax.fori_loop(0, EDGE, image_of, nothing, unroll=3)))

    def residual_of(y, total):
        total = list(total)
        for i, q in PIECES:
            left = first[y, *piece(i, q)] - alpha[q] * image[y, *piece(i, q)]
            total[q] = total[q] + left * left
        return tuple(total)

    new = patch_total(lax.fori_loop(0, EDGE, residual_of, nothing, unroll=4))
    beta = divide(new, rr)

    def direction(y, i, q):
        v = first[y, *piece(i, q)]
        return (v - alpha[q] * image[y, *piece(i, q)]) + beta[q] * v

    for at in PIECES:
        ready[0, *piece(*at)] = direction(0, *at)

    def energy_of(step, total):
        total = list(total)
        v = load(ready, 0)
        for k in range(SLABS):
            y = step * SLABS + k
            v_up = above_x(v)
            v_next = {at: direction(y + 1, *at) for at in PIECES}
            for i in range(STRIPS):
                ups = above_z(strip(v, i))
                for q in range(3):
                    to = piece(i, q)
                    couple = face_x[y, *to] * v_up[i, q]
                    couple = couple + face_y[y + 1, *to] * v_next[i, q]
                    couple = couple + face_z[y, *to] * ups[q]
                    total[q] = total[q] + v[i, q] * (heavy[y, *to] * v[i, q] - 2.0 * couple)
            v = v_next
        for at in PIECES:
            ready[0, *piece(*at)] = v[at]
        return tuple(total)

    energy = lax.fori_loop(0, EDGE // SLABS, energy_of, nothing)
    alpha_next = divide(new, patch_total(energy))
    on_first = [alpha[q] + alpha_next[q] * (1.0 + beta[q]) for q in range(3)]
    on_image = [-(alpha_next[q] * alpha[q]) for q in range(3)]

    ends = [lane < end for end in (48, 96, 16, 64, 112, 32, 80)]

    def gather(c):
        return (
            jnp.where(ends[0], c[0][0], jnp.where(ends[1], c[1][0], c[2][0])),
            jnp.where(
                ends[2],
                c[2][1],
                jnp.where(ends[3], c[3][1], jnp.where(ends[4], c[4][1], c[5][1])),
            ),
            jnp.where(ends[5], c[5][2], jnp.where(ends[6], c[6][2], c[7][2])),
        )

    departures = []
    for group in range(GROUPS):

        def correct(i, _):
            rows = pl.ds(pl.multiple_of(8 * i, 8), 8)
            lines = []
            for j in range(8):
                y = 8 * group + j
                lines.append([
                    on_first[q] * first[y, rows, pl.ds(SIDE * q, SIDE)]
                    + on_image[q] * image[y, rows, pl.ds(SIDE * q, SIDE)]
                    for q in range(3)
                ])
            turned = []
            for k in range(8):
                a, b, c = gather([lines[(p + k) % 8] for p in range(8)])
                far, near = divmod(EDGE * k, SIDE)
                r = [pltpu.roll(v, near, 1) if near else v for v in (a, b, c)]
                r = [r[(q - far) % 3] for q in range(3)]
                before = [r[2], r[0], r[1]]
                if near:
                    r = [jnp.where(lane < near, before[q], r[q]) for q in range(3)]
                turned.append(r)
            for p in range(PATCH_DEV):
                tiles = gather([turned[(j - p) % 8] for j in range(8)])
                for q in range(3):
                    heavy[8 * group + p, rows, pl.ds(SIDE * q, SIDE)] = tiles[q]
            return 0

        lax.fori_loop(0, STRIPS, correct, 0, unroll=True)
        departures.append(
            pltpu.make_async_copy(
                heavy.at[pl.ds(8 * group, PATCH_DEV)],
                out_ref.at[:, :, pl.ds(group * LANES, LANES)],
                leave.at[group],
            )
        )
        departures[-1].start()
    for copy in departures:
        copy.wait()


def solve(half, later):
    cube = pltpu.VMEM((EDGE, EDGE, LANES), F32)
    longer = pltpu.VMEM((EDGE + 1, EDGE, LANES), F32)
    return pl.pallas_call(
        solve_kernel,
        in_specs=[pl.BlockSpec(memory_space=pl.ANY), pl.BlockSpec(memory_space=pltpu.VMEM)],
        out_specs=pl.BlockSpec(memory_space=pl.ANY),
        out_shape=full((PATCH_DEV, EDGE, EDGE * EDGE)),
        scratch_shapes=[
            pltpu.VMEM((EDGE + 2, EDGE, LANES), F32),
            longer,
            longer,
            cube,
            cube,
            longer,
            cube,
            pltpu.VMEM((1, EDGE, LANES), F32),
            pltpu.SemaphoreType.DMA((WIDE // 4, TAPS)),
            pltpu.SemaphoreType.DMA((GROUPS,)),
        ],
        compiler_params=params(40),
        cost_estimate=pl.CostEstimate(
            flops=60 * EDGE**3 * PATCH_DEV, bytes_accessed=32 << 20, transcendentals=0
        ),
        name="solve_patches",
    )(half, later)


def wave_tables():
    index = np.arange(NX, dtype=np.int64)
    angle = (index[:, None] * index[None, :] % NX) * (2.0 * math.pi / NX)
    waves = np.concatenate([np.cos(angle), np.sin(angle)], axis=0)
    return waves.astype(np.float32)


def on_device(noise, spectrum, send_core, recv_source):
    swap = lambda v: lax.all_to_all(v, "wide", split_axis=0, concat_axis=0)
    lines = swap(
        split_rows(noise, send_core.reshape(1, WIDE), recv_source.reshape(1, PATCH_DEV))
    )
    waves = jnp.asarray(wave_tables())
    weights = jnp.concatenate([spectrum, spectrum])[:, None] / NX
    matrix = lax.dot_general(
        waves,
        waves * weights,
        (((0,), (0,)), ((), ())),
        precision=lax.Precision.HIGHEST,
        preferred_element_type=F32,
    )
    count = lax.axis_size("mid")
    pairs = lambda start: [
        edge for i in range(start, count - 1, 2) for edge in ((i, i + 1), (i + 1, i))
    ]
    odd = (lax.axis_index("mid") & 1).reshape(1)
    pair = bf16_pair(matrix)
    parts, crossing, staying, table = filter_exp(odd, pair, lines)
    crossed = lax.ppermute(crossing, "mid", pairs(1))
    stayed = lax.ppermute(staying, "mid", pairs(0))
    back = swap(parts)
    outgoing = windows(table, odd, (crossing, staying))
    outgoing = windows(table, odd, (crossed, stayed), outgoing)
    outgoing, back = lax.optimization_barrier((outgoing, back))
    incoming = swap(outgoing)
    coefficient = join_rows(back)
    cores = table[0, recv_source.reshape(-1), lax.axis_index("wide")]
    later = jnp.repeat((cores >> 5) & 1, EDGE).reshape(1, LANES)
    solved = solve(incoming, later)
    return coefficient, solved.reshape(1, 1, PATCH_DEV, EDGE, EDGE * EDGE)


def solution(mesh):
    in_specs = (P("wide", "mid", None), P(), P("wide", "mid", None), P("wide", "mid", None))
    out_specs = (P("wide", "mid", None), P("wide", "mid", None, None, None))
    return jax.shard_map(
        on_device, mesh=mesh, in_specs=in_specs, out_specs=out_specs, check_vma=False
    )
```

```python
import functools
import math

import jax
import jax.numpy as jnp
import numpy as np
from jax import lax
from jax.experimental import pallas as pl
from jax.experimental.pallas import tpu as pltpu
from jax.sharding import PartitionSpec as P

NX = 512
NZ = 512
CY = 32
CX = 32
CORE = 16
LAYER = 16
WIDE = 16
PATCH_DEV = 8
EDGE = 48
TAPS = 3
LANES = PATCH_DEV * EDGE
SIDE = 128
TILES = NZ // SIDE
ROWS = 2 * TILES * CX
OWNERS = 4
UNROLL = 2
TINY = 1e-06
F32 = jnp.float32


def params(mebibytes):
    return pltpu.CompilerParams(vmem_limit_bytes=mebibytes * 1024 * 1024)


def full(shape):
    return jax.ShapeDtypeStruct(shape, F32)


def exchange(pieces):
    row = lax.broadcasted_iota(jnp.int32, pieces[0].shape, 0)
    pieces = list(pieces)
    for bit in (4, 2, 1):
        upper = (row & bit) != 0
        for i in range(8):
            k = i | bit
            if i == k:
                continue
            pieces[i], pieces[k] = (
                jnp.where(upper, pltpu.roll(pieces[k], bit, 0), pieces[i]),
                jnp.where(upper, pieces[k], pltpu.roll(pieces[i], 8 - bit, 0)),
            )
    return pieces


def split_kernel(in_ref, send_ref, source_ref, out_ref, taken, held, arrive, leave):
    arrivals = [
        pltpu.make_async_copy(
            in_ref.at[:, :, pl.ds(j * SIDE, SIDE)], taken.at[j], arrive.at[j]
        )
        for j in range(TILES)
    ]
    for copy in arrivals:
        copy.start()

    def depart(first, count, sem):
        rows = pl.ds(first, count)
        copy = pltpu.make_async_copy(held.at[:, rows, :], out_ref.at[:, rows, :], sem)
        copy.start()
        return copy

    for w in range(WIDE):
        held[w, ROWS:ROWS + 1, 0:WIDE] = send_ref[...].astype(F32)
        held[w, ROWS + 1:ROWS + 2, 0:PATCH_DEV] = source_ref[...].astype(F32)
    departures = [depart(ROWS, 8, leave.at[2, 0])]
    for j in range(TILES):
        arrivals[j].wait()
        for t in range(2):
            first = (t * TILES + j) * CX
            for x in range(0, CX, 8):
                for y in range(0, WIDE, 8):
                    at = t * WIDE + y
                    pieces = exchange([taken[j, x + i, at:at + 8, :] for i in range(8)])
                    for i in range(8):
                        held[y + i, first + x:first + x + 8, :] = pieces[i]
            departures.append(depart(first, CX, leave.at[t, j]))
    for copy in departures:
        copy.wait()


def split_rows(block, send, source):
    return pl.pallas_call(
        split_kernel,
        in_specs=[
            pl.BlockSpec(memory_space=pl.ANY),
            pl.BlockSpec(memory_space=pltpu.VMEM),
            pl.BlockSpec(memory_space=pltpu.VMEM),
        ],
        out_specs=pl.BlockSpec(memory_space=pl.ANY),
        out_shape=full((WIDE, ROWS + 8, SIDE)),
        scratch_shapes=[
            pltpu.VMEM((TILES, CX, CY, SIDE), F32),
            pltpu.VMEM((WIDE, ROWS + 8, SIDE), F32),
            pltpu.SemaphoreType.DMA((TILES,)),
            pltpu.SemaphoreType.DMA((3, TILES)),
        ],
        compiler_params=params(60),
        cost_estimate=pl.CostEstimate(flops=0, bytes_accessed=8 << 20, transcendentals=0),
        name="split_rows",
    )(block, send, source)


def join_kernel(low_ref, high_ref, out_ref):
    for t, in_ref in enumerate((low_ref, high_ref)):
        for x in range(0, CX, 8):
            for y in range(0, WIDE, 8):
                pieces = exchange([in_ref[y + i, x:x + 8, :] for i in range(8)])
                for i in range(8):
                    out_ref[x + i, t * WIDE + y:t * WIDE + y + 8, :] = pieces[i]


def join_rows(parts):
    return pl.pallas_call(
        join_kernel,
        grid=(TILES,),
        in_specs=[
            pl.BlockSpec((WIDE, CX, SIDE), lambda j: (0, j, 0)),
            pl.BlockSpec((WIDE, CX, SIDE), lambda j: (0, TILES + j, 0)),
        ],
        out_specs=pl.BlockSpec((CX, CY, SIDE), lambda j: (0, 0, j)),
        out_shape=full((CX, CY, NZ)),
        compiler_params=params(12),
        cost_estimate=pl.CostEstimate(flops=0, bytes_accessed=8 << 20, transcendentals=0),
        name="join_rows",
    )(parts, parts)


def pair_kernel(in_ref, high_ref, low_ref):
    value = in_ref[...]
    high = value.astype(jnp.bfloat16)
    high_ref[...] = high
    low_ref[...] = (value - high.astype(F32)).astype(jnp.bfloat16)


def bf16_pair(matrix):
    return pl.pallas_call(
        pair_kernel,
        out_shape=[jax.ShapeDtypeStruct((NX, NX), jnp.bfloat16)] * 2,
        compiler_params=params(60),
        cost_estimate=pl.CostEstimate(flops=0, bytes_accessed=2 << 20, transcendentals=0),
        name="bf16_pair",
    )(matrix)


def filter_kernel(odd_ref, high_ref, low_ref, in_ref, extra_ref, parts_ref, first_ref, second_ref, table_ref):
    for k in range(2):
        table_ref[k] = extra_ref[:, k, :].astype(jnp.int32)
    lines = jnp.concatenate(
        [in_ref[:, 0:CX, :].reshape(NX, SIDE), in_ref[:, CX:, :].reshape(NX, SIDE)], axis=1
    )
    high = lines.astype(jnp.bfloat16)
    low = (lines - high.astype(F32)).astype(jnp.bfloat16)
    dot = lambda a, b: jnp.dot(a, b, preferred_element_type=F32)
    small = dot(high_ref[...], low) + dot(low_ref[...], high)
    value = jnp.exp(dot(high_ref[...], high) + small)
    sides = [value[:, :SIDE], value[:, SIDE:]]
    for k in range(2):
        parts_ref[:, k * CX:(k + 1) * CX, :] = sides[k].reshape(WIDE, CX, SIDE)

    def plane(ref):
        for k in range(2):
            ref[k] = 0.5 * sides[k]

    pl.when(pl.program_id(0) < 2)(lambda: plane(first_ref))
    pl.when(pl.program_id(0) >= 2)(lambda: plane(second_ref))


def filter_exp(odd, pair, lines):
    whole = pl.BlockSpec((NX, NX), lambda i, odd: (0, 0))
    block = pl.BlockSpec(
        (WIDE, 2 * CX, SIDE), lambda i, odd: (0, 2 * ((i >> 1) ^ odd[0]) + (i & 1), 0)
    )
    return pl.pallas_call(
        filter_kernel,
        grid_spec=pltpu.PrefetchScalarGridSpec(
            num_scalar_prefetch=1,
            grid=(4,),
            in_specs=[
                whole,
                whole,
                block,
                pl.BlockSpec((WIDE, 8, SIDE), lambda i, odd: (0, ROWS // 8, 0)),
            ],
            out_specs=[
                block,
                pl.BlockSpec((2, NX, SIDE), lambda i, odd: (jnp.minimum(i, 1), 0, 0)),
                pl.BlockSpec((2, NX, SIDE), lambda i, odd: (jnp.maximum(i - 2, 0), 0, 0)),
                pl.BlockSpec((2, WIDE, SIDE), lambda i, odd: (0, 0, 0)),
            ],
        ),
        out_shape=[
            full((WIDE, ROWS, SIDE)),
            full((TILES, NX, SIDE)),
            full((TILES, NX, SIDE)),
            jax.ShapeDtypeStruct((2, WIDE, SIDE), jnp.int32),
        ],
        compiler_params=params(60),
        cost_estimate=pl.CostEstimate(
            flops=12 * NX * NX * NZ, bytes_accessed=8 << 20, transcendentals=2 * NX * NZ
        ),
        name="filter_exp",
    )(odd, *pair, lines, lines)


def window_kernel(slots, table_ref, odd_ref, *refs):
    low_ref, high_ref = refs[:2]
    out_ref, held, sems = refs[-3:]
    step = pl.program_id(0)

    @pl.when(step == 0)
    def _():
        copies = [
            pltpu.make_async_copy(
                src.at[j], held.at[t, 1 + j, pl.ds(LAYER, NX), :], sems.at[t, j]
            )
            for t, src in enumerate((low_ref, high_ref))
            for j in range(TILES)
        ]
        for copy in copies:
            copy.start()
        side = jnp.zeros((NX + 2 * LAYER, SIDE), F32)
        for t in range(2):
            held[t, 0] = side
            held[t, TILES + 1] = side
            for j in range(TILES):
                held[t, 1 + j, 0:LAYER, :] = side[:LAYER]
                held[t, 1 + j, LAYER + NX:, :] = side[:LAYER]
        for copy in copies:
            copy.wait()

    lane = lax.broadcasted_iota(jnp.int32, (EDGE, SIDE), 1)

    def one_owner(k, _):
        owner = step * OWNERS + k
        places = []
        for p in range(PATCH_DEV):
            source = table_ref[1, owner, p]
            core = jnp.maximum(table_ref[0, source, owner], 0)
            x_at = source * CX + (core >> 6) * CORE
            z_at = (core & 31) * CORE + (SIDE - LAYER)
            offset = z_at & (SIDE - 1)
            turn = ((p * EDGE) % SIDE - offset) & (SIDE - 1)
            places.append((pl.multiple_of(x_at, CORE), (core >> 5) & 1, z_at >> 7, offset, turn))
        for t in range(slots):
            tiles = [None] * 3
            for p, (x_at, t_at, tile, offset, turn) in enumerate(places):
                plane = (t if slots == 2 else t_at) ^ odd_ref[0]
                rows = pl.ds(x_at, EDGE)
                near = held[plane, tile, rows, :]
                far = held[plane, tile + 1, rows, :]
                moved = pltpu.roll(jnp.where(lane >= offset, near, far), turn, 1)
                at = (p * EDGE) % SIDE
                q = (p * EDGE) // SIDE
                tiles[q] = moved if at == 0 else jnp.where(lane >= at, moved, tiles[q])
                if at + EDGE > SIDE:
                    tiles[q + 1] = moved
            for q in range(3):
                out_ref[k, t * EDGE:(t + 1) * EDGE, q * SIDE:(q + 1) * SIDE] = tiles[q]
        return 0

    lax.fori_loop(0, OWNERS, one_owner, 0, unroll=UNROLL)


def windows(table, odd, planes, *others):
    slots = 1 if others else 2
    at = 2 if others else 0
    return pl.pallas_call(
        functools.partial(window_kernel, slots),
        grid_spec=pltpu.PrefetchScalarGridSpec(
            num_scalar_prefetch=2,
            grid=(WIDE // OWNERS,),
            in_specs=[pl.BlockSpec(memory_space=pl.ANY)] * (2 + len(others)),
            out_specs=pl.BlockSpec((OWNERS, slots * EDGE, LANES), lambda d, table, odd: (d, at, 0)),
            scratch_shapes=[
                pltpu.VMEM((2, TILES + 2, NX + 2 * LAYER, SIDE), F32),
                pltpu.SemaphoreType.DMA((2, TILES)),
            ],
        ),
        out_shape=full((WIDE, TAPS * EDGE, LANES)),
        input_output_aliases={4: 0} if others else {},
        compiler_params=params(58 if others else 60),
        cost_estimate=pl.CostEstimate(
            flops=0, bytes_accessed=slots * (6 << 20), transcendentals=0
        ),
        name="patch_windows",
    )(table, odd, *planes, *others)


STRIPS = EDGE // 8
SLABS = 4
GROUPS = EDGE // 8
PIECES = [(i, q) for i in range(STRIPS) for q in range(3)]


def piece(i, q):
    return (pl.ds(8 * i, 8), pl.ds(SIDE * q, SIDE))


def solve_kernel(
    half_ref, later_ref, out_ref, half, first, image, heavy, face_x, face_y, face_z, ready, arrive, leave
):
    arrivals = [
        [
            pltpu.make_async_copy(
                half_ref.at[pl.ds(4 * g, 4), pl.ds(t * EDGE, EDGE), :],
                (heavy, face_x, face_y)[t].at[pl.ds(4 * g, 4)],
                arrive.at[g, t],
            )
            for t in range(TAPS)
        ]
        for g in range(WIDE // 4)
    ]
    for group in arrivals:
        for copy in group:
            copy.start()
    none = jnp.zeros((8, SIDE), F32)
    for at in PIECES:
        half[0, *piece(*at)] = none
        half[EDGE + 1, *piece(*at)] = none
        first[EDGE, *piece(*at)] = none
        image[EDGE, *piece(*at)] = none

    row = lax.broadcasted_iota(jnp.int32, (8, SIDE), 0)
    lane = lax.broadcasted_iota(jnp.int32, (8, SIDE), 1)
    row_low, row_high = row == 0, row == 7
    lane_low, lane_high = lane == 0, lane == SIDE - 1
    depth = []
    for q in range(3):
        place = lane + q * SIDE
        depth.append(place - ((place * 1366) >> 16) * EDGE)
    z_low = [d == 0 for d in depth]
    z_high = [d == EDGE - 1 for d in depth]

    def above_x(slab):
        turned = {at: pltpu.roll(slab[at], 7, 0) for at in PIECES}
        return {
            (i, q): jnp.where(row_high, turned[i + 1, q] if i < STRIPS - 1 else 0.0, turned[i, q])
            for i, q in PIECES
        }

    def below_x(slab):
        turned = {at: pltpu.roll(slab[at], 1, 0) for at in PIECES}
        return {
            (i, q): jnp.where(row_low, turned[i - 1, q] if i else 0.0, turned[i, q])
            for i, q in PIECES
        }

    def above_z(strip):
        turned = [pltpu.roll(v, SIDE - 1, 1) for v in strip]
        return [
            jnp.where(lane_high, turned[1], turned[0]),
            jnp.where(lane_high, turned[2], turned[1]),
            turned[2],
        ]

    def below_z(strip):
        turned = [pltpu.roll(v, 1, 1) for v in strip]
        return [
            jnp.where(lane_low, 0.0, turned[0]),
            jnp.where(lane_low, turned[0], turned[1]),
            jnp.where(lane_low, turned[1], turned[2]),
        ]

    def load(ref, y):
        return {at: ref[y, *piece(*at)] for at in PIECES}

    def strip(slab, i):
        return [slab[i, q] for q in range(3)]

    same = jnp.where(
        ((lax.broadcasted_iota(jnp.int32, (LANES, LANES), 0) * 1366) >> 16)
        == ((lax.broadcasted_iota(jnp.int32, (LANES, LANES), 1) * 1366) >> 16),
        1.0,
        0.0,
    ).astype(jnp.bfloat16)

    def patch_total(parts):
        part = jnp.concatenate(parts, axis=1)
        high = part.astype(jnp.bfloat16).astype(F32)
        middle = (part - high).astype(jnp.bfloat16).astype(F32)
        low = part - high - middle
        stack = jnp.concatenate([high, middle, low, jnp.zeros_like(low)], axis=0)
        spread = jnp.dot(stack.astype(jnp.bfloat16), same, preferred_element_type=F32)
        total = jnp.sum(spread, axis=0, keepdims=True)
        return [
            jnp.broadcast_to(total[:, SIDE * q:SIDE * (q + 1)], (8, SIDE)) for q in range(3)
        ]

    def divide(top, bottom):
        return [t / (b + TINY) for t, b in zip(top, bottom)]

    nothing = (none, none, none)

    in_order = [
        jnp.broadcast_to(later_ref[:, SIDE * q:SIDE * (q + 1)], (8, SIDE)) != 0 for q in range(3)
    ]

    def arrange(w, _):
        for i, q in PIECES:
            at = piece(i, q)
            a, b, c = heavy[w, *at], face_x[w, *at], face_y[w, *at]
            half[1 + w, *at] = jnp.where(in_order[q], a, c)
            half[1 + WIDE + w, *at] = jnp.where(in_order[q], b, a)
            half[1 + 2 * WIDE + w, *at] = jnp.where(in_order[q], c, b)
        return 0

    def faces_of(y, rr):
        rr = list(rr)
        h = load(half, y + 1)
        h_up = above_x(h)
        h_down = below_x(h)
        deep_up, deep_down = {}, {}
        for i in range(STRIPS):
            ups, downs = above_z(strip(h, i)), below_z(strip(h, i))
            for q in range(3):
                deep_up[i, q] = jnp.where(z_high[q], 0.0, ups[q])
                deep_down[i, q] = jnp.where(z_low[q], 0.0, downs[q])
        up_up, up_down = above_x(deep_up), below_x(deep_up)
        down_up, down_down = above_x(deep_down), below_x(deep_down)
        for i, q in PIECES:
            here, to = h[i, q], piece(i, q)
            z_up, z_down = deep_up[i, q], deep_down[i, q]
            v = h_up[i, q] - h_down[i, q]
            y_up = half[y + 2, *to]
            y_down = half[y, *to]
            across = here + h_up[i, q]
            if i == STRIPS - 1:
                across = jnp.where(row_high, 0.0, across)
            deep = here + z_up
            heavy[y, *to] = (
                (1.0 + 6.0 * here) + (h_up[i, q] + h_down[i, q])
                + ((y_up + y_down) + (z_up + z_down))
            )
            face_x[y, *to] = across
            face_y[y + 1, *to] = here + y_up
            face_z[y, *to] = jnp.where(z_high[q], 0.0, deep)
            first[y, *to] = v
            image[y, *to] = deep * (up_up[i, q] - up_down[i, q]) + (here + z_down) * (
                down_up[i, q] - down_down[i, q]
            )
            rr[q] = rr[q] + v * v
        return tuple(rr)

    def span(start, count, rr):
        def body(t, rr):
            for k in range(count):
                rr = faces_of(t * WIDE + start + k, rr)
            return rr

        return lax.fori_loop(0, TAPS, body, rr)

    rr = nothing
    for g, group in enumerate(arrivals):
        for copy in group:
            copy.wait()
        lax.fori_loop(4 * g, 4 * g + 4, arrange, 0, unroll=2)
        rr = span(4 * g - 1, 4, rr) if g else span(1, 2, rr)
    for y in (0, 15, 16, 31, 32, 47):
        rr = faces_of(y, rr)
    for at in PIECES:
        face_y[0, *piece(*at)] = none
        face_y[EDGE, *piece(*at)] = none
    rr = patch_total(rr)

    def image_of(y, total):
        total = list(total)
        v = load(first, y)
        v_up = above_x(v)
        across = load(face_x, y)
        from_x = below_x({at: across[at] * v[at] for at in PIECES})
        for i, q in PIECES:
            to = piece(i, q)
            couple = across[i, q] * v_up[i, q] + from_x[i, q]
            couple = couple + face_y[y + 1, *to] * first[y + 1, *to]
            couple = couple + face_y[y, *to] * first[jnp.maximum(y - 1, 0), *to]
            result = heavy[y, *to] * v[i, q] - (couple + image[y, *to])
            image[y, *to] = result
            total[q] = total[q] + v[i, q] * result
        return tuple(total)

    alpha = divide(rr, patch_total(lax.fori_loop(0, EDGE, image_of, nothing, unroll=4)))

    def residual_of(y, total):
        total = list(total)
        for i, q in PIECES:
            left = first[y, *piece(i, q)] - alpha[q] * image[y, *piece(i, q)]
            total[q] = total[q] + left * left
        return tuple(total)

    new = patch_total(lax.fori_loop(0, EDGE, residual_of, nothing, unroll=8))
    beta = divide(new, rr)

    def direction(y, i, q):
        v = first[y, *piece(i, q)]
        return (v - alpha[q] * image[y, *piece(i, q)]) + beta[q] * v

    for at in PIECES:
        ready[0, *piece(*at)] = direction(0, *at)

    def energy_of(step, total):
        total = list(total)
        v = load(ready, 0)
        for k in range(SLABS):
            y = step * SLABS + k
            v_up = above_x(v)
            v_next = {at: direction(y + 1, *at) for at in PIECES}
            for i in range(STRIPS):
                ups = above_z(strip(v, i))
                for q in range(3):
                    to = piece(i, q)
                    couple = face_x[y, *to] * v_up[i, q]
                    couple = couple + face_y[y + 1, *to] * v_next[i, q]
                    couple = couple + face_z[y, *to] * ups[q]
                    total[q] = total[q] + v[i, q] * (heavy[y, *to] * v[i, q] - 2.0 * couple)
            v = v_next
        for at in PIECES:
            ready[0, *piece(*at)] = v[at]
        return tuple(total)

    energy = lax.fori_loop(0, EDGE // SLABS, energy_of, nothing)
    alpha_next = divide(new, patch_total(energy))
    on_first = [alpha[q] + alpha_next[q] * (1.0 + beta[q]) for q in range(3)]
    on_image = [-(alpha_next[q] * alpha[q]) for q in range(3)]

    ends = [lane < end for end in (48, 96, 16, 64, 112, 32, 80)]

    def gather(c):
        return (
            jnp.where(ends[0], c[0][0], jnp.where(ends[1], c[1][0], c[2][0])),
            jnp.where(
                ends[2],
                c[2][1],
                jnp.where(ends[3], c[3][1], jnp.where(ends[4], c[4][1], c[5][1])),
            ),
            jnp.where(ends[5], c[5][2], jnp.where(ends[6], c[6][2], c[7][2])),
        )

    departures = []
    for group in range(GROUPS):

        def correct(i, _):
            rows = pl.ds(pl.multiple_of(8 * i, 8), 8)
            lines = []
            for j in range(8):
                y = 8 * group + j
                lines.append([
                    on_first[q] * first[y, rows, pl.ds(SIDE * q, SIDE)]
                    + on_image[q] * image[y, rows, pl.ds(SIDE * q, SIDE)]
                    for q in range(3)
                ])
            turned = []
            for k in range(8):
                a, b, c = gather([lines[(p + k) % 8] for p in range(8)])
                far, near = divmod(EDGE * k, SIDE)
                r = [pltpu.roll(v, near, 1) if near else v for v in (a, b, c)]
                r = [r[(q - far) % 3] for q in range(3)]
                before = [r[2], r[0], r[1]]
                if near:
                    r = [jnp.where(lane < near, before[q], r[q]) for q in range(3)]
                turned.append(r)
            for p in range(PATCH_DEV):
                tiles = gather([turned[(j - p) % 8] for j in range(8)])
                for q in range(3):
                    heavy[8 * group + p, rows, pl.ds(SIDE * q, SIDE)] = tiles[q]
            return 0

        lax.fori_loop(0, STRIPS, correct, 0, unroll=True)
        departures.append(
            pltpu.make_async_copy(
                heavy.at[pl.ds(8 * group, PATCH_DEV)],
                out_ref.at[:, :, pl.ds(group * LANES, LANES)],
                leave.at[group],
            )
        )
        departures[-1].start()
    for copy in departures:
        copy.wait()


def solve(half, later):
    cube = pltpu.VMEM((EDGE, EDGE, LANES), F32)
    longer = pltpu.VMEM((EDGE + 1, EDGE, LANES), F32)
    return pl.pallas_call(
        solve_kernel,
        in_specs=[pl.BlockSpec(memory_space=pl.ANY), pl.BlockSpec(memory_space=pltpu.VMEM)],
        out_specs=pl.BlockSpec(memory_space=pl.ANY),
        out_shape=full((PATCH_DEV, EDGE, EDGE * EDGE)),
        scratch_shapes=[
            pltpu.VMEM((EDGE + 2, EDGE, LANES), F32),
            longer,
            longer,
            cube,
            cube,
            longer,
            cube,
            pltpu.VMEM((1, EDGE, LANES), F32),
            pltpu.SemaphoreType.DMA((WIDE // 4, TAPS)),
            pltpu.SemaphoreType.DMA((GROUPS,)),
        ],
        compiler_params=params(40),
        cost_estimate=pl.CostEstimate(
            flops=60 * EDGE**3 * PATCH_DEV, bytes_accessed=32 << 20, transcendentals=0
        ),
        name="solve_patches",
    )(half, later)


def wave_tables():
    index = np.arange(NX, dtype=np.int64)
    angle = (index[:, None] * index[None, :] % NX) * (2.0 * math.pi / NX)
    waves = np.concatenate([np.cos(angle), np.sin(angle)], axis=0)
    return waves.astype(np.float32)


def on_device(noise, spectrum, send_core, recv_source):
    swap = lambda v: lax.all_to_all(v, "wide", split_axis=0, concat_axis=0)
    lines = swap(
        split_rows(noise, send_core.reshape(1, WIDE), recv_source.reshape(1, PATCH_DEV))
    )
    waves = jnp.asarray(wave_tables())
    weights = jnp.concatenate([spectrum, spectrum])[:, None] / NX
    matrix = lax.dot_general(
        waves,
        waves * weights,
        (((0,), (0,)), ((), ())),
        precision=lax.Precision.HIGHEST,
        preferred_element_type=F32,
    )
    count = lax.axis_size("mid")
    pairs = lambda start: [
        edge for i in range(start, count - 1, 2) for edge in ((i, i + 1), (i + 1, i))
    ]
    odd = (lax.axis_index("mid") & 1).reshape(1)
    pair = bf16_pair(matrix)
    parts, crossing, staying, table = filter_exp(odd, pair, lines)
    crossed = lax.ppermute(crossing, "mid", pairs(1))
    stayed = lax.ppermute(staying, "mid", pairs(0))
    back = swap(parts)
    outgoing = windows(table, odd, (crossing, staying))
    outgoing = windows(table, odd, (crossed, stayed), outgoing)
    outgoing, back = lax.optimization_barrier((outgoing, back))
    incoming = swap(outgoing)
    coefficient = join_rows(back)
    cores = table[0, recv_source.reshape(-1), lax.axis_index("wide")]
    later = jnp.repeat((cores >> 5) & 1, EDGE).reshape(1, LANES)
    solved = solve(incoming, later)
    return coefficient, solved.reshape(1, 1, PATCH_DEV, EDGE, EDGE * EDGE)


def solution(mesh):
    in_specs = (P("wide", "mid", None), P(), P("wide", "mid", None), P("wide", "mid", None))
    out_specs = (P("wide", "mid", None), P("wide", "mid", None, None, None))
    return jax.shard_map(
        on_device, mesh=mesh, in_specs=in_specs, out_specs=out_specs, check_vma=False
    )
```

```python
import functools
import math

import jax
import jax.numpy as jnp
import numpy as np
from jax import lax
from jax.experimental import pallas as pl
from jax.experimental.pallas import tpu as pltpu
from jax.sharding import PartitionSpec as P

NX = 512
NZ = 512
CY = 32
CX = 32
CORE = 16
LAYER = 16
WIDE = 16
PATCH_DEV = 8
EDGE = 48
TAPS = 3
LANES = PATCH_DEV * EDGE
SIDE = 128
TILES = NZ // SIDE
ROWS = 2 * TILES * CX
OWNERS = 4
UNROLL = 2
TINY = 1e-06
F32 = jnp.float32


def params(mebibytes):
    return pltpu.CompilerParams(vmem_limit_bytes=mebibytes * 1024 * 1024)


def full(shape):
    return jax.ShapeDtypeStruct(shape, F32)


def exchange(pieces):
    row = lax.broadcasted_iota(jnp.int32, pieces[0].shape, 0)
    pieces = list(pieces)
    for bit in (4, 2, 1):
        upper = (row & bit) != 0
        for i in range(8):
            k = i | bit
            if i == k:
                continue
            pieces[i], pieces[k] = (
                jnp.where(upper, pltpu.roll(pieces[k], bit, 0), pieces[i]),
                jnp.where(upper, pieces[k], pltpu.roll(pieces[i], 8 - bit, 0)),
            )
    return pieces


def split_kernel(in_ref, send_ref, source_ref, out_ref, taken, held, arrive, leave):
    arrivals = [
        pltpu.make_async_copy(
            in_ref.at[:, :, pl.ds(j * SIDE, SIDE)], taken.at[j], arrive.at[j]
        )
        for j in range(TILES)
    ]
    for copy in arrivals:
        copy.start()

    def depart(first, count, sem):
        rows = pl.ds(first, count)
        copy = pltpu.make_async_copy(held.at[:, rows, :], out_ref.at[:, rows, :], sem)
        copy.start()
        return copy

    for w in range(WIDE):
        held[w, ROWS:ROWS + 1, 0:WIDE] = send_ref[...].astype(F32)
        held[w, ROWS + 1:ROWS + 2, 0:PATCH_DEV] = source_ref[...].astype(F32)
    departures = [depart(ROWS, 8, leave.at[2, 0])]
    for j in range(TILES):
        arrivals[j].wait()
        for t in range(2):
            first = (t * TILES + j) * CX
            for x in range(0, CX, 8):
                for y in range(0, WIDE, 8):
                    at = t * WIDE + y
                    pieces = exchange([taken[j, x + i, at:at + 8, :] for i in range(8)])
                    for i in range(8):
                        held[y + i, first + x:first + x + 8, :] = pieces[i]
            departures.append(depart(first, CX, leave.at[t, j]))
    for copy in departures:
        copy.wait()


def split_rows(block, send, source):
    return pl.pallas_call(
        split_kernel,
        in_specs=[
            pl.BlockSpec(memory_space=pl.ANY),
            pl.BlockSpec(memory_space=pltpu.VMEM),
            pl.BlockSpec(memory_space=pltpu.VMEM),
        ],
        out_specs=pl.BlockSpec(memory_space=pl.ANY),
        out_shape=full((WIDE, ROWS + 8, SIDE)),
        scratch_shapes=[
            pltpu.VMEM((TILES, CX, CY, SIDE), F32),
            pltpu.VMEM((WIDE, ROWS + 8, SIDE), F32),
            pltpu.SemaphoreType.DMA((TILES,)),
            pltpu.SemaphoreType.DMA((3, TILES)),
        ],
        compiler_params=params(60),
        cost_estimate=pl.CostEstimate(flops=0, bytes_accessed=8 << 20, transcendentals=0),
        name="split_rows",
    )(block, send, source)


def join_kernel(low_ref, high_ref, out_ref):
    for t, in_ref in enumerate((low_ref, high_ref)):
        for x in range(0, CX, 8):
            for y in range(0, WIDE, 8):
                pieces = exchange([in_ref[y + i, x:x + 8, :] for i in range(8)])
                for i in range(8):
                    out_ref[x + i, t * WIDE + y:t * WIDE + y + 8, :] = pieces[i]


def join_rows(parts):
    return pl.pallas_call(
        join_kernel,
        grid=(TILES,),
        in_specs=[
            pl.BlockSpec((WIDE, CX, SIDE), lambda j: (0, j, 0)),
            pl.BlockSpec((WIDE, CX, SIDE), lambda j: (0, TILES + j, 0)),
        ],
        out_specs=pl.BlockSpec((CX, CY, SIDE), lambda j: (0, 0, j)),
        out_shape=full((CX, CY, NZ)),
        compiler_params=params(12),
        cost_estimate=pl.CostEstimate(flops=0, bytes_accessed=8 << 20, transcendentals=0),
        name="join_rows",
    )(parts, parts)


def pair_kernel(in_ref, high_ref, low_ref):
    value = in_ref[...]
    high = value.astype(jnp.bfloat16)
    high_ref[...] = high
    low_ref[...] = (value - high.astype(F32)).astype(jnp.bfloat16)


def bf16_pair(matrix):
    return pl.pallas_call(
        pair_kernel,
        out_shape=[jax.ShapeDtypeStruct((NX, NX), jnp.bfloat16)] * 2,
        compiler_params=params(60),
        cost_estimate=pl.CostEstimate(flops=0, bytes_accessed=2 << 20, transcendentals=0),
        name="bf16_pair",
    )(matrix)


def filter_kernel(odd_ref, high_ref, low_ref, in_ref, extra_ref, parts_ref, first_ref, second_ref, table_ref):
    for k in range(2):
        table_ref[k] = extra_ref[:, k, :].astype(jnp.int32)
    lines = jnp.concatenate(
        [in_ref[:, k * CX:(k + 1) * CX, :].reshape(NX, SIDE) for k in range(TILES)], axis=1
    )
    high = lines.astype(jnp.bfloat16)
    low = (lines - high.astype(F32)).astype(jnp.bfloat16)
    dot = lambda a, b: jnp.dot(a, b, preferred_element_type=F32)
    small = dot(high_ref[...], low) + dot(low_ref[...], high)
    value = jnp.exp(dot(high_ref[...], high) + small)
    sides = [value[:, k * SIDE:(k + 1) * SIDE] for k in range(TILES)]
    for k in range(TILES):
        parts_ref[:, k * CX:(k + 1) * CX, :] = sides[k].reshape(WIDE, CX, SIDE)

    def plane(ref):
        for k in range(TILES):
            ref[k] = 0.5 * sides[k]

    pl.when(pl.program_id(0) == 0)(lambda: plane(first_ref))
    pl.when(pl.program_id(0) == 1)(lambda: plane(second_ref))


def filter_exp(odd, pair, lines):
    whole = pl.BlockSpec((NX, NX), lambda i, odd: (0, 0))
    block = pl.BlockSpec(
        (WIDE, TILES * CX, SIDE), lambda i, odd: (0, i ^ odd[0], 0)
    )
    return pl.pallas_call(
        filter_kernel,
        grid_spec=pltpu.PrefetchScalarGridSpec(
            num_scalar_prefetch=1,
            grid=(2,),
            in_specs=[
                whole,
                whole,
                block,
                pl.BlockSpec((WIDE, 8, SIDE), lambda i, odd: (0, ROWS // 8, 0)),
            ],
            out_specs=[
                block,
                pl.BlockSpec((TILES, NX, SIDE), lambda i, odd: (0, 0, 0)),
                pl.BlockSpec((TILES, NX, SIDE), lambda i, odd: (0, 0, 0)),
                pl.BlockSpec((2, WIDE, SIDE), lambda i, odd: (0, 0, 0)),
            ],
        ),
        out_shape=[
            full((WIDE, ROWS, SIDE)),
            full((TILES, NX, SIDE)),
            full((TILES, NX, SIDE)),
            jax.ShapeDtypeStruct((2, WIDE, SIDE), jnp.int32),
        ],
        compiler_params=params(60),
        cost_estimate=pl.CostEstimate(
            flops=12 * NX * NX * NZ, bytes_accessed=8 << 20, transcendentals=2 * NX * NZ
        ),
        name="filter_exp",
    )(odd, *pair, lines, lines)


def window_kernel(slots, table_ref, odd_ref, *refs):
    low_ref, high_ref = refs[:2]
    out_ref, held, sems = refs[-3:]
    step = pl.program_id(0)

    @pl.when(step == 0)
    def _():
        copies = [
            pltpu.make_async_copy(
                src.at[j], held.at[t, 1 + j, pl.ds(LAYER, NX), :], sems.at[t, j]
            )
            for t, src in enumerate((low_ref, high_ref))
            for j in range(TILES)
        ]
        for copy in copies:
            copy.start()
        side = jnp.zeros((NX + 2 * LAYER, SIDE), F32)
        for t in range(2):
            held[t, 0] = side
            held[t, TILES + 1] = side
            for j in range(TILES):
                held[t, 1 + j, 0:LAYER, :] = side[:LAYER]
                held[t, 1 + j, LAYER + NX:, :] = side[:LAYER]
        for copy in copies:
            copy.wait()

    lane = lax.broadcasted_iota(jnp.int32, (EDGE, SIDE), 1)

    def one_owner(k, _):
        owner = step * OWNERS + k
        places = []
        for p in range(PATCH_DEV):
            source = table_ref[1, owner, p]
            core = jnp.maximum(table_ref[0, source, owner], 0)
            x_at = source * CX + (core >> 6) * CORE
            z_at = (core & 31) * CORE + (SIDE - LAYER)
            offset = z_at & (SIDE - 1)
            turn = ((p * EDGE) % SIDE - offset) & (SIDE - 1)
            places.append((pl.multiple_of(x_at, CORE), (core >> 5) & 1, z_at >> 7, offset, turn))
        for t in range(slots):
            tiles = [None] * 3
            for p, (x_at, t_at, tile, offset, turn) in enumerate(places):
                plane = (t if slots == 2 else t_at) ^ odd_ref[0]
                rows = pl.ds(x_at, EDGE)
                near = held[plane, tile, rows, :]
                far = held[plane, tile + 1, rows, :]
                moved = pltpu.roll(jnp.where(lane >= offset, near, far), turn, 1)
                at = (p * EDGE) % SIDE
                q = (p * EDGE) // SIDE
                tiles[q] = moved if at == 0 else jnp.where(lane >= at, moved, tiles[q])
                if at + EDGE > SIDE:
                    tiles[q + 1] = moved
            for q in range(3):
                out_ref[k, t * EDGE:(t + 1) * EDGE, q * SIDE:(q + 1) * SIDE] = tiles[q]
        return 0

    lax.fori_loop(0, OWNERS, one_owner, 0, unroll=UNROLL)


def windows(table, odd, planes, *others):
    slots = 1 if others else 2
    at = 2 if others else 0
    return pl.pallas_call(
        functools.partial(window_kernel, slots),
        grid_spec=pltpu.PrefetchScalarGridSpec(
            num_scalar_prefetch=2,
            grid=(WIDE // OWNERS,),
            in_specs=[pl.BlockSpec(memory_space=pl.ANY)] * (2 + len(others)),
            out_specs=pl.BlockSpec((OWNERS, slots * EDGE, LANES), lambda d, table, odd: (d, at, 0)),
            scratch_shapes=[
                pltpu.VMEM((2, TILES + 2, NX + 2 * LAYER, SIDE), F32),
                pltpu.SemaphoreType.DMA((2, TILES)),
            ],
        ),
        out_shape=full((WIDE, TAPS * EDGE, LANES)),
        input_output_aliases={4: 0} if others else {},
        compiler_params=params(58 if others else 60),
        cost_estimate=pl.CostEstimate(
            flops=0, bytes_accessed=slots * (6 << 20), transcendentals=0
        ),
        name="patch_windows",
    )(table, odd, *planes, *others)


STRIPS = EDGE // 8
SLABS = 4
GROUPS = EDGE // 8
PIECES = [(i, q) for i in range(STRIPS) for q in range(3)]


def piece(i, q):
    return (pl.ds(8 * i, 8), pl.ds(SIDE * q, SIDE))


def solve_kernel(
    half_ref, later_ref, out_ref, half, first, image, heavy, face_x, face_y, face_z, ready, arrive, leave
):
    arrivals = [
        [
            pltpu.make_async_copy(
                half_ref.at[pl.ds(4 * g, 4), pl.ds(t * EDGE, EDGE), :],
                (heavy, face_x, face_y)[t].at[pl.ds(4 * g, 4)],
                arrive.at[g, t],
            )
            for t in range(TAPS)
        ]
        for g in range(WIDE // 4)
    ]
    for group in arrivals:
        for copy in group:
            copy.start()
    none = jnp.zeros((8, SIDE), F32)
    for at in PIECES:
        half[0, *piece(*at)] = none
        half[EDGE + 1, *piece(*at)] = none
        first[EDGE, *piece(*at)] = none
        image[EDGE, *piece(*at)] = none

    row = lax.broadcasted_iota(jnp.int32, (8, SIDE), 0)
    lane = lax.broadcasted_iota(jnp.int32, (8, SIDE), 1)
    row_low, row_high = row == 0, row == 7
    lane_low, lane_high = lane == 0, lane == SIDE - 1
    depth = []
    for q in range(3):
        place = lane + q * SIDE
        depth.append(place - ((place * 1366) >> 16) * EDGE)
    z_low = [d == 0 for d in depth]
    z_high = [d == EDGE - 1 for d in depth]

    def above_x(slab):
        turned = {at: pltpu.roll(slab[at], 7, 0) for at in PIECES}
        return {
            (i, q): jnp.where(row_high, turned[i + 1, q] if i < STRIPS - 1 else 0.0, turned[i, q])
            for i, q in PIECES
        }

    def below_x(slab):
        turned = {at: pltpu.roll(slab[at], 1, 0) for at in PIECES}
        return {
            (i, q): jnp.where(row_low, turned[i - 1, q] if i else 0.0, turned[i, q])
            for i, q in PIECES
        }

    def above_z(strip):
        turned = [pltpu.roll(v, SIDE - 1, 1) for v in strip]
        return [
            jnp.where(lane_high, turned[1], turned[0]),
            jnp.where(lane_high, turned[2], turned[1]),
            turned[2],
        ]

    def below_z(strip):
        turned = [pltpu.roll(v, 1, 1) for v in strip]
        return [
            jnp.where(lane_low, 0.0, turned[0]),
            jnp.where(lane_low, turned[0], turned[1]),
            jnp.where(lane_low, turned[1], turned[2]),
        ]

    def load(ref, y):
        return {at: ref[y, *piece(*at)] for at in PIECES}

    def strip(slab, i):
        return [slab[i, q] for q in range(3)]

    same = jnp.where(
        ((lax.broadcasted_iota(jnp.int32, (LANES, LANES), 0) * 1366) >> 16)
        == ((lax.broadcasted_iota(jnp.int32, (LANES, LANES), 1) * 1366) >> 16),
        1.0,
        0.0,
    ).astype(jnp.bfloat16)

    def patch_total(parts):
        part = jnp.concatenate(parts, axis=1)
        high = part.astype(jnp.bfloat16).astype(F32)
        middle = (part - high).astype(jnp.bfloat16).astype(F32)
        low = part - high - middle
        stack = jnp.concatenate([high, middle, low, jnp.zeros_like(low)], axis=0)
        spread = jnp.dot(stack.astype(jnp.bfloat16), same, preferred_element_type=F32)
        total = jnp.sum(spread, axis=0, keepdims=True)
        return [
            jnp.broadcast_to(total[:, SIDE * q:SIDE * (q + 1)], (8, SIDE)) for q in range(3)
        ]

    def divide(top, bottom):
        return [t / (b + TINY) for t, b in zip(top, bottom)]

    nothing = (none, none, none)

    in_order = [
        jnp.broadcast_to(later_ref[:, SIDE * q:SIDE * (q + 1)], (8, SIDE)) != 0 for q in range(3)
    ]

    def arrange(w, _):
        for i, q in PIECES:
            at = piece(i, q)
            a, b, c = heavy[w, *at], face_x[w, *at], face_y[w, *at]
            half[1 + w, *at] = jnp.where(in_order[q], a, c)
            half[1 + WIDE + w, *at] = jnp.where(in_order[q], b, a)
            half[1 + 2 * WIDE + w, *at] = jnp.where(in_order[q], c, b)
        return 0

    def faces_of(y, rr):
        rr = list(rr)
        h = load(half, y + 1)
        h_up = above_x(h)
        h_down = below_x(h)
        deep_up, deep_down = {}, {}
        for i in range(STRIPS):
            ups, downs = above_z(strip(h, i)), below_z(strip(h, i))
            for q in range(3):
                deep_up[i, q] = jnp.where(z_high[q], 0.0, ups[q])
                deep_down[i, q] = jnp.where(z_low[q], 0.0, downs[q])
        up_up, up_down = above_x(deep_up), below_x(deep_up)
        down_up, down_down = above_x(deep_down), below_x(deep_down)
        for i, q in PIECES:
            here, to = h[i, q], piece(i, q)
            z_up, z_down = deep_up[i, q], deep_down[i, q]
            v = h_up[i, q] - h_down[i, q]
            y_up = half[y + 2, *to]
            y_down = half[y, *to]
            across = here + h_up[i, q]
            if i == STRIPS - 1:
                across = jnp.where(row_high, 0.0, across)
            deep = here + z_up
            heavy[y, *to] = (
                (1.0 + 6.0 * here) + (h_up[i, q] + h_down[i, q])
                + ((y_up + y_down) + (z_up + z_down))
            )
            face_x[y, *to] = across
            face_y[y + 1, *to] = here + y_up
            face_z[y, *to] = jnp.where(z_high[q], 0.0, deep)
            first[y, *to] = v
            image[y, *to] = deep * (up_up[i, q] - up_down[i, q]) + (here + z_down) * (
                down_up[i, q] - down_down[i, q]
            )
            rr[q] = rr[q] + v * v
        return tuple(rr)

    def span(start, count, rr):
        def body(t, rr):
            for k in range(count):
                rr = faces_of(t * WIDE + start + k, rr)
            return rr

        return lax.fori_loop(0, TAPS, body, rr)

    rr = nothing
    for g, group in enumerate(arrivals):
        for copy in group:
            copy.wait()
        lax.fori_loop(4 * g, 4 * g + 4, arrange, 0, unroll=2)
        rr = span(4 * g - 1, 4, rr) if g else span(1, 2, rr)
    for y in (0, 15, 16, 31, 32, 47):
        rr = faces_of(y, rr)
    for at in PIECES:
        face_y[0, *piece(*at)] = none
        face_y[EDGE, *piece(*at)] = none
    rr = patch_total(rr)

    def image_of(y, total):
        total = list(total)
        v = load(first, y)
        v_up = above_x(v)
        across = load(face_x, y)
        from_x = below_x({at: across[at] * v[at] for at in PIECES})
        for i, q in PIECES:
            to = piece(i, q)
            couple = across[i, q] * v_up[i, q] + from_x[i, q]
            couple = couple + face_y[y + 1, *to] * first[y + 1, *to]
            couple = couple + face_y[y, *to] * first[jnp.maximum(y - 1, 0), *to]
            result = heavy[y, *to] * v[i, q] - (couple + image[y, *to])
            image[y, *to] = result
            total[q] = total[q] + v[i, q] * result
        return tuple(total)

    alpha = divide(rr, patch_total(lax.fori_loop(0, EDGE, image_of, nothing, unroll=4)))

    def residual_of(y, total):
        total = list(total)
        for i, q in PIECES:
            left = first[y, *piece(i, q)] - alpha[q] * image[y, *piece(i, q)]
            total[q] = total[q] + left * left
        return tuple(total)

    new = patch_total(lax.fori_loop(0, EDGE, residual_of, nothing, unroll=8))
    beta = divide(new, rr)

    def direction(y, i, q):
        v = first[y, *piece(i, q)]
        return (v - alpha[q] * image[y, *piece(i, q)]) + beta[q] * v

    for at in PIECES:
        ready[0, *piece(*at)] = direction(0, *at)

    def energy_of(step, total):
        total = list(total)
        v = load(ready, 0)
        for k in range(SLABS):
            y = step * SLABS + k
            v_up = above_x(v)
            v_next = {at: direction(y + 1, *at) for at in PIECES}
            for i in range(STRIPS):
                ups = above_z(strip(v, i))
                for q in range(3):
                    to = piece(i, q)
                    couple = face_x[y, *to] * v_up[i, q]
                    couple = couple + face_y[y + 1, *to] * v_next[i, q]
                    couple = couple + face_z[y, *to] * ups[q]
                    total[q] = total[q] + v[i, q] * (heavy[y, *to] * v[i, q] - 2.0 * couple)
            v = v_next
        for at in PIECES:
            ready[0, *piece(*at)] = v[at]
        return tuple(total)

    energy = lax.fori_loop(0, EDGE // SLABS, energy_of, nothing)
    alpha_next = divide(new, patch_total(energy))
    on_first = [alpha[q] + alpha_next[q] * (1.0 + beta[q]) for q in range(3)]
    on_image = [-(alpha_next[q] * alpha[q]) for q in range(3)]

    ends = [lane < end for end in (48, 96, 16, 64, 112, 32, 80)]

    def gather(c):
        return (
            jnp.where(ends[0], c[0][0], jnp.where(ends[1], c[1][0], c[2][0])),
            jnp.where(
                ends[2],
                c[2][1],
                jnp.where(ends[3], c[3][1], jnp.where(ends[4], c[4][1], c[5][1])),
            ),
            jnp.where(ends[5], c[5][2], jnp.where(ends[6], c[6][2], c[7][2])),
        )

    departures = []
    for group in range(GROUPS):

        def correct(i, _):
            rows = pl.ds(pl.multiple_of(8 * i, 8), 8)
            lines = []
            for j in range(8):
                y = 8 * group + j
                lines.append([
                    on_first[q] * first[y, rows, pl.ds(SIDE * q, SIDE)]
                    + on_image[q] * image[y, rows, pl.ds(SIDE * q, SIDE)]
                    for q in range(3)
                ])
            turned = []
            for k in range(8):
                a, b, c = gather([lines[(p + k) % 8] for p in range(8)])
                far, near = divmod(EDGE * k, SIDE)
                r = [pltpu.roll(v, near, 1) if near else v for v in (a, b, c)]
                r = [r[(q - far) % 3] for q in range(3)]
                before = [r[2], r[0], r[1]]
                if near:
                    r = [jnp.where(lane < near, before[q], r[q]) for q in range(3)]
                turned.append(r)
            for p in range(PATCH_DEV):
                tiles = gather([turned[(j - p) % 8] for j in range(8)])
                for q in range(3):
                    heavy[8 * group + p, rows, pl.ds(SIDE * q, SIDE)] = tiles[q]
            return 0

        lax.fori_loop(0, STRIPS, correct, 0, unroll=True)
        departures.append(
            pltpu.make_async_copy(
                heavy.at[pl.ds(8 * group, PATCH_DEV)],
                out_ref.at[:, :, pl.ds(group * LANES, LANES)],
                leave.at[group],
            )
        )
        departures[-1].start()
    for copy in departures:
        copy.wait()


def solve(half, later):
    cube = pltpu.VMEM((EDGE, EDGE, LANES), F32)
    longer = pltpu.VMEM((EDGE + 1, EDGE, LANES), F32)
    return pl.pallas_call(
        solve_kernel,
        in_specs=[pl.BlockSpec(memory_space=pl.ANY), pl.BlockSpec(memory_space=pltpu.VMEM)],
        out_specs=pl.BlockSpec(memory_space=pl.ANY),
        out_shape=full((PATCH_DEV, EDGE, EDGE * EDGE)),
        scratch_shapes=[
            pltpu.VMEM((EDGE + 2, EDGE, LANES), F32),
            longer,
            longer,
            cube,
            cube,
            longer,
            cube,
            pltpu.VMEM((1, EDGE, LANES), F32),
            pltpu.SemaphoreType.DMA((WIDE // 4, TAPS)),
            pltpu.SemaphoreType.DMA((GROUPS,)),
        ],
        compiler_params=params(40),
        cost_estimate=pl.CostEstimate(
            flops=60 * EDGE**3 * PATCH_DEV, bytes_accessed=32 << 20, transcendentals=0
        ),
        name="solve_patches",
    )(half, later)


def wave_tables():
    index = np.arange(NX, dtype=np.int64)
    angle = (index[:, None] * index[None, :] % NX) * (2.0 * math.pi / NX)
    waves = np.concatenate([np.cos(angle), np.sin(angle)], axis=0)
    return waves.astype(np.float32)


def on_device(noise, spectrum, send_core, recv_source):
    swap = lambda v: lax.all_to_all(v, "wide", split_axis=0, concat_axis=0)
    lines = swap(
        split_rows(noise, send_core.reshape(1, WIDE), recv_source.reshape(1, PATCH_DEV))
    )
    waves = jnp.asarray(wave_tables())
    weights = jnp.concatenate([spectrum, spectrum])[:, None] / NX
    matrix = lax.dot_general(
        waves,
        waves * weights,
        (((0,), (0,)), ((), ())),
        precision=lax.Precision.HIGHEST,
        preferred_element_type=F32,
    )
    count = lax.axis_size("mid")
    pairs = lambda start: [
        edge for i in range(start, count - 1, 2) for edge in ((i, i + 1), (i + 1, i))
    ]
    odd = (lax.axis_index("mid") & 1).reshape(1)
    pair = bf16_pair(matrix)
    parts, crossing, staying, table = filter_exp(odd, pair, lines)
    crossed = lax.ppermute(crossing, "mid", pairs(1))
    stayed = lax.ppermute(staying, "mid", pairs(0))
    back = swap(parts)
    outgoing = windows(table, odd, (crossing, staying))
    outgoing = windows(table, odd, (crossed, stayed), outgoing)
    outgoing, back = lax.optimization_barrier((outgoing, back))
    incoming = swap(outgoing)
    coefficient = join_rows(back)
    cores = table[0, recv_source.reshape(-1), lax.axis_index("wide")]
    later = jnp.repeat((cores >> 5) & 1, EDGE).reshape(1, LANES)
    solved = solve(incoming, later)
    return coefficient, solved.reshape(1, 1, PATCH_DEV, EDGE, EDGE * EDGE)


def solution(mesh):
    in_specs = (P("wide", "mid", None), P(), P("wide", "mid", None), P("wide", "mid", None))
    out_specs = (P("wide", "mid", None), P("wide", "mid", None, None, None))
    return jax.shard_map(
        on_device, mesh=mesh, in_specs=in_specs, out_specs=out_specs, check_vma=False
    )
```

```python
import functools
import math

import jax
import jax.numpy as jnp
import numpy as np
from jax import lax
from jax.experimental import pallas as pl
from jax.experimental.pallas import tpu as pltpu
from jax.sharding import PartitionSpec as P

NX = 512
NZ = 512
CY = 32
CX = 32
CORE = 16
LAYER = 16
WIDE = 16
PATCH_DEV = 8
EDGE = 48
TAPS = 3
LANES = PATCH_DEV * EDGE
SIDE = 128
TILES = NZ // SIDE
ROWS = 2 * TILES * CX
OWNERS = 8
UNROLL = 2
TINY = 1e-06
F32 = jnp.float32


def params(mebibytes):
    return pltpu.CompilerParams(vmem_limit_bytes=mebibytes * 1024 * 1024)


def full(shape):
    return jax.ShapeDtypeStruct(shape, F32)


def exchange(pieces):
    row = lax.broadcasted_iota(jnp.int32, pieces[0].shape, 0)
    pieces = list(pieces)
    for bit in (4, 2, 1):
        upper = (row & bit) != 0
        for i in range(8):
            k = i | bit
            if i == k:
                continue
            pieces[i], pieces[k] = (
                jnp.where(upper, pltpu.roll(pieces[k], bit, 0), pieces[i]),
                jnp.where(upper, pieces[k], pltpu.roll(pieces[i], 8 - bit, 0)),
            )
    return pieces


def split_kernel(in_ref, send_ref, source_ref, out_ref, taken, held, arrive, leave):
    arrivals = [
        pltpu.make_async_copy(
            in_ref.at[:, :, pl.ds(j * SIDE, SIDE)], taken.at[j], arrive.at[j]
        )
        for j in range(TILES)
    ]
    for copy in arrivals:
        copy.start()

    def depart(first, count, sem):
        rows = pl.ds(first, count)
        copy = pltpu.make_async_copy(held.at[:, rows, :], out_ref.at[:, rows, :], sem)
        copy.start()
        return copy

    for w in range(WIDE):
        held[w, ROWS:ROWS + 1, 0:WIDE] = send_ref[...].astype(F32)
        held[w, ROWS + 1:ROWS + 2, 0:PATCH_DEV] = source_ref[...].astype(F32)
    departures = [depart(ROWS, 8, leave.at[2, 0])]
    for j in range(TILES):
        arrivals[j].wait()
        for t in range(2):
            first = (t * TILES + j) * CX
            for x in range(0, CX, 8):
                for y in range(0, WIDE, 8):
                    at = t * WIDE + y
                    pieces = exchange([taken[j, x + i, at:at + 8, :] for i in range(8)])
                    for i in range(8):
                        held[y + i, first + x:first + x + 8, :] = pieces[i]
            departures.append(depart(first, CX, leave.at[t, j]))
    for copy in departures:
        copy.wait()


def split_rows(block, send, source):
    return pl.pallas_call(
        split_kernel,
        in_specs=[
            pl.BlockSpec(memory_space=pl.ANY),
            pl.BlockSpec(memory_space=pltpu.VMEM),
            pl.BlockSpec(memory_space=pltpu.VMEM),
        ],
        out_specs=pl.BlockSpec(memory_space=pl.ANY),
        out_shape=full((WIDE, ROWS + 8, SIDE)),
        scratch_shapes=[
            pltpu.VMEM((TILES, CX, CY, SIDE), F32),
            pltpu.VMEM((WIDE, ROWS + 8, SIDE), F32),
            pltpu.SemaphoreType.DMA((TILES,)),
            pltpu.SemaphoreType.DMA((3, TILES)),
        ],
        compiler_params=params(60),
        cost_estimate=pl.CostEstimate(flops=0, bytes_accessed=8 << 20, transcendentals=0),
        name="split_rows",
    )(block, send, source)


def join_kernel(low_ref, high_ref, out_ref):
    for t, in_ref in enumerate((low_ref, high_ref)):
        for x in range(0, CX, 8):
            for y in range(0, WIDE, 8):
                pieces = exchange([in_ref[y + i, x:x + 8, :] for i in range(8)])
                for i in range(8):
                    out_ref[x + i, t * WIDE + y:t * WIDE + y + 8, :] = pieces[i]


def join_rows(parts):
    return pl.pallas_call(
        join_kernel,
        grid=(TILES,),
        in_specs=[
            pl.BlockSpec((WIDE, CX, SIDE), lambda j: (0, j, 0)),
            pl.BlockSpec((WIDE, CX, SIDE), lambda j: (0, TILES + j, 0)),
        ],
        out_specs=pl.BlockSpec((CX, CY, SIDE), lambda j: (0, 0, j)),
        out_shape=full((CX, CY, NZ)),
        compiler_params=params(12),
        cost_estimate=pl.CostEstimate(flops=0, bytes_accessed=8 << 20, transcendentals=0),
        name="join_rows",
    )(parts, parts)


def pair_kernel(in_ref, high_ref, low_ref):
    value = in_ref[...]
    high = value.astype(jnp.bfloat16)
    high_ref[...] = high
    low_ref[...] = (value - high.astype(F32)).astype(jnp.bfloat16)


def bf16_pair(matrix):
    return pl.pallas_call(
        pair_kernel,
        out_shape=[jax.ShapeDtypeStruct((NX, NX), jnp.bfloat16)] * 2,
        compiler_params=params(60),
        cost_estimate=pl.CostEstimate(flops=0, bytes_accessed=2 << 20, transcendentals=0),
        name="bf16_pair",
    )(matrix)


def filter_kernel(odd_ref, high_ref, low_ref, in_ref, extra_ref, parts_ref, first_ref, second_ref, table_ref):
    for k in range(2):
        table_ref[k] = extra_ref[:, k, :].astype(jnp.int32)
    lines = jnp.concatenate(
        [in_ref[:, k * CX:(k + 1) * CX, :].reshape(NX, SIDE) for k in range(TILES)], axis=1
    )
    high = lines.astype(jnp.bfloat16)
    low = (lines - high.astype(F32)).astype(jnp.bfloat16)
    dot = lambda a, b: jnp.dot(a, b, preferred_element_type=F32)
    small = dot(high_ref[...], low) + dot(low_ref[...], high)
    value = jnp.exp(dot(high_ref[...], high) + small)
    sides = [value[:, k * SIDE:(k + 1) * SIDE] for k in range(TILES)]
    for k in range(TILES):
        parts_ref[:, k * CX:(k + 1) * CX, :] = sides[k].reshape(WIDE, CX, SIDE)

    def plane(ref):
        for k in range(TILES):
            ref[k] = 0.5 * sides[k]

    pl.when(pl.program_id(0) == 0)(lambda: plane(first_ref))
    pl.when(pl.program_id(0) == 1)(lambda: plane(second_ref))


def filter_exp(odd, pair, lines):
    whole = pl.BlockSpec((NX, NX), lambda i, odd: (0, 0))
    block = pl.BlockSpec(
        (WIDE, TILES * CX, SIDE), lambda i, odd: (0, i ^ odd[0], 0)
    )
    return pl.pallas_call(
        filter_kernel,
        grid_spec=pltpu.PrefetchScalarGridSpec(
            num_scalar_prefetch=1,
            grid=(2,),
            in_specs=[
                whole,
                whole,
                block,
                pl.BlockSpec((WIDE, 8, SIDE), lambda i, odd: (0, ROWS // 8, 0)),
            ],
            out_specs=[
                block,
                pl.BlockSpec((TILES, NX, SIDE), lambda i, odd: (0, 0, 0)),
                pl.BlockSpec((TILES, NX, SIDE), lambda i, odd: (0, 0, 0)),
                pl.BlockSpec((2, WIDE, SIDE), lambda i, odd: (0, 0, 0)),
            ],
        ),
        out_shape=[
            full((WIDE, ROWS, SIDE)),
            full((TILES, NX, SIDE)),
            full((TILES, NX, SIDE)),
            jax.ShapeDtypeStruct((2, WIDE, SIDE), jnp.int32),
        ],
        compiler_params=params(60),
        cost_estimate=pl.CostEstimate(
            flops=12 * NX * NX * NZ, bytes_accessed=8 << 20, transcendentals=2 * NX * NZ
        ),
        name="filter_exp",
    )(odd, *pair, lines, lines)


def window_kernel(slots, table_ref, odd_ref, *refs):
    low_ref, high_ref = refs[:2]
    out_ref, held, sems = refs[-3:]
    step = pl.program_id(0)

    @pl.when(step == 0)
    def _():
        copies = [
            pltpu.make_async_copy(
                src.at[j], held.at[t, 1 + j, pl.ds(LAYER, NX), :], sems.at[t, j]
            )
            for t, src in enumerate((low_ref, high_ref))
            for j in range(TILES)
        ]
        for copy in copies:
            copy.start()
        side = jnp.zeros((NX + 2 * LAYER, SIDE), F32)
        for t in range(2):
            held[t, 0] = side
            held[t, TILES + 1] = side
            for j in range(TILES):
                held[t, 1 + j, 0:LAYER, :] = side[:LAYER]
                held[t, 1 + j, LAYER + NX:, :] = side[:LAYER]
        for copy in copies:
            copy.wait()

    lane = lax.broadcasted_iota(jnp.int32, (EDGE, SIDE), 1)

    def one_owner(k, _):
        owner = step * OWNERS + k
        places = []
        for p in range(PATCH_DEV):
            source = table_ref[1, owner, p]
            core = jnp.maximum(table_ref[0, source, owner], 0)
            x_at = source * CX + (core >> 6) * CORE
            z_at = (core & 31) * CORE + (SIDE - LAYER)
            offset = z_at & (SIDE - 1)
            turn = ((p * EDGE) % SIDE - offset) & (SIDE - 1)
            places.append((pl.multiple_of(x_at, CORE), (core >> 5) & 1, z_at >> 7, offset, turn))
        for t in range(slots):
            tiles = [None] * 3
            for p, (x_at, t_at, tile, offset, turn) in enumerate(places):
                plane = (t if slots == 2 else t_at) ^ odd_ref[0]
                rows = pl.ds(x_at, EDGE)
                near = held[plane, tile, rows, :]
                far = held[plane, tile + 1, rows, :]
                moved = pltpu.roll(jnp.where(lane >= offset, near, far), turn, 1)
                at = (p * EDGE) % SIDE
                q = (p * EDGE) // SIDE
                tiles[q] = moved if at == 0 else jnp.where(lane >= at, moved, tiles[q])
                if at + EDGE > SIDE:
                    tiles[q + 1] = moved
            for q in range(3):
                out_ref[k, t * EDGE:(t + 1) * EDGE, q * SIDE:(q + 1) * SIDE] = tiles[q]
        return 0

    lax.fori_loop(0, OWNERS, one_owner, 0, unroll=UNROLL)


def windows(table, odd, planes, *others):
    slots = 1 if others else 2
    at = 2 if others else 0
    return pl.pallas_call(
        functools.partial(window_kernel, slots),
        grid_spec=pltpu.PrefetchScalarGridSpec(
            num_scalar_prefetch=2,
            grid=(WIDE // OWNERS,),
            in_specs=[pl.BlockSpec(memory_space=pl.ANY)] * (2 + len(others)),
            out_specs=pl.BlockSpec((OWNERS, slots * EDGE, LANES), lambda d, table, odd: (d, at, 0)),
            scratch_shapes=[
                pltpu.VMEM((2, TILES + 2, NX + 2 * LAYER, SIDE), F32),
                pltpu.SemaphoreType.DMA((2, TILES)),
            ],
        ),
        out_shape=full((WIDE, TAPS * EDGE, LANES)),
        input_output_aliases={4: 0} if others else {},
        compiler_params=params(58 if others else 60),
        cost_estimate=pl.CostEstimate(
            flops=0, bytes_accessed=slots * (6 << 20), transcendentals=0
        ),
        name="patch_windows",
    )(table, odd, *planes, *others)


STRIPS = EDGE // 8
SLABS = 4
GROUPS = EDGE // 8
PIECES = [(i, q) for i in range(STRIPS) for q in range(3)]


def piece(i, q):
    return (pl.ds(8 * i, 8), pl.ds(SIDE * q, SIDE))


def solve_kernel(
    half_ref, later_ref, out_ref, half, first, image, heavy, face_x, face_y, face_z, ready, arrive, leave
):
    arrivals = [
        [
            pltpu.make_async_copy(
                half_ref.at[pl.ds(4 * g, 4), pl.ds(t * EDGE, EDGE), :],
                (heavy, face_x, face_y)[t].at[pl.ds(4 * g, 4)],
                arrive.at[g, t],
            )
            for t in range(TAPS)
        ]
        for g in range(WIDE // 4)
    ]
    for group in arrivals:
        for copy in group:
            copy.start()
    none = jnp.zeros((8, SIDE), F32)
    for at in PIECES:
        half[0, *piece(*at)] = none
        half[EDGE + 1, *piece(*at)] = none
        first[EDGE, *piece(*at)] = none
        image[EDGE, *piece(*at)] = none

    row = lax.broadcasted_iota(jnp.int32, (8, SIDE), 0)
    lane = lax.broadcasted_iota(jnp.int32, (8, SIDE), 1)
    row_low, row_high = row == 0, row == 7
    lane_low, lane_high = lane == 0, lane == SIDE - 1
    depth = []
    for q in range(3):
        place = lane + q * SIDE
        depth.append(place - ((place * 1366) >> 16) * EDGE)
    z_low = [d == 0 for d in depth]
    z_high = [d == EDGE - 1 for d in depth]

    def above_x(slab):
        turned = {at: pltpu.roll(slab[at], 7, 0) for at in PIECES}
        return {
            (i, q): jnp.where(row_high, turned[i + 1, q] if i < STRIPS - 1 else 0.0, turned[i, q])
            for i, q in PIECES
        }

    def below_x(slab):
        turned = {at: pltpu.roll(slab[at], 1, 0) for at in PIECES}
        return {
            (i, q): jnp.where(row_low, turned[i - 1, q] if i else 0.0, turned[i, q])
            for i, q in PIECES
        }

    def above_z(strip):
        turned = [pltpu.roll(v, SIDE - 1, 1) for v in strip]
        return [
            jnp.where(lane_high, turned[1], turned[0]),
            jnp.where(lane_high, turned[2], turned[1]),
            turned[2],
        ]

    def below_z(strip):
        turned = [pltpu.roll(v, 1, 1) for v in strip]
        return [
            jnp.where(lane_low, 0.0, turned[0]),
            jnp.where(lane_low, turned[0], turned[1]),
            jnp.where(lane_low, turned[1], turned[2]),
        ]

    def load(ref, y):
        return {at: ref[y, *piece(*at)] for at in PIECES}

    def strip(slab, i):
        return [slab[i, q] for q in range(3)]

    same = jnp.where(
        ((lax.broadcasted_iota(jnp.int32, (LANES, LANES), 0) * 1366) >> 16)
        == ((lax.broadcasted_iota(jnp.int32, (LANES, LANES), 1) * 1366) >> 16),
        1.0,
        0.0,
    ).astype(jnp.bfloat16)

    def patch_total(parts):
        part = jnp.concatenate(parts, axis=1)
        high = part.astype(jnp.bfloat16).astype(F32)
        middle = (part - high).astype(jnp.bfloat16).astype(F32)
        low = part - high - middle
        stack = jnp.concatenate([high, middle, low, jnp.zeros_like(low)], axis=0)
        spread = jnp.dot(stack.astype(jnp.bfloat16), same, preferred_element_type=F32)
        total = jnp.sum(spread, axis=0, keepdims=True)
        return [
            jnp.broadcast_to(total[:, SIDE * q:SIDE * (q + 1)], (8, SIDE)) for q in range(3)
        ]

    def divide(top, bottom):
        return [t / (b + TINY) for t, b in zip(top, bottom)]

    nothing = (none, none, none)

    in_order = [
        jnp.broadcast_to(later_ref[:, SIDE * q:SIDE * (q + 1)], (8, SIDE)) != 0 for q in range(3)
    ]

    def arrange(w, _):
        for i, q in PIECES:
            at = piece(i, q)
            a, b, c = heavy[w, *at], face_x[w, *at], face_y[w, *at]
            half[1 + w, *at] = jnp.where(in_order[q], a, c)
            half[1 + WIDE + w, *at] = jnp.where(in_order[q], b, a)
            half[1 + 2 * WIDE + w, *at] = jnp.where(in_order[q], c, b)
        return 0

    def faces_of(y, rr):
        rr = list(rr)
        h = load(half, y + 1)
        h_up = above_x(h)
        h_down = below_x(h)
        deep_up, deep_down = {}, {}
        for i in range(STRIPS):
            ups, downs = above_z(strip(h, i)), below_z(strip(h, i))
            for q in range(3):
                deep_up[i, q] = jnp.where(z_high[q], 0.0, ups[q])
                deep_down[i, q] = jnp.where(z_low[q], 0.0, downs[q])
        up_up, up_down = above_x(deep_up), below_x(deep_up)
        down_up, down_down = above_x(deep_down), below_x(deep_down)
        for i, q in PIECES:
            here, to = h[i, q], piece(i, q)
            z_up, z_down = deep_up[i, q], deep_down[i, q]
            v = h_up[i, q] - h_down[i, q]
            y_up = half[y + 2, *to]
            y_down = half[y, *to]
            across = here + h_up[i, q]
            if i == STRIPS - 1:
                across = jnp.where(row_high, 0.0, across)
            deep = here + z_up
            heavy[y, *to] = (
                (1.0 + 6.0 * here) + (h_up[i, q] + h_down[i, q])
                + ((y_up + y_down) + (z_up + z_down))
            )
            face_x[y, *to] = across
            face_y[y + 1, *to] = here + y_up
            face_z[y, *to] = jnp.where(z_high[q], 0.0, deep)
            first[y, *to] = v
            image[y, *to] = deep * (up_up[i, q] - up_down[i, q]) + (here + z_down) * (
                down_up[i, q] - down_down[i, q]
            )
            rr[q] = rr[q] + v * v
        return tuple(rr)

    def span(start, count, rr):
        def body(t, rr):
            for k in range(count):
                rr = faces_of(t * WIDE + start + k, rr)
            return rr

        return lax.fori_loop(0, TAPS, body, rr)

    rr = nothing
    for g, group in enumerate(arrivals):
        for copy in group:
            copy.wait()
        lax.fori_loop(4 * g, 4 * g + 4, arrange, 0, unroll=2)
        rr = span(4 * g - 1, 4, rr) if g else span(1, 2, rr)
    for y in (0, 15, 16, 31, 32, 47):
        rr = faces_of(y, rr)
    for at in PIECES:
        face_y[0, *piece(*at)] = none
        face_y[EDGE, *piece(*at)] = none
    rr = patch_total(rr)

    def image_of(y, total):
        total = list(total)
        v = load(first, y)
        v_up = above_x(v)
        across = load(face_x, y)
        from_x = below_x({at: across[at] * v[at] for at in PIECES})
        for i, q in PIECES:
            to = piece(i, q)
            couple = across[i, q] * v_up[i, q] + from_x[i, q]
            couple = couple + face_y[y + 1, *to] * first[y + 1, *to]
            couple = couple + face_y[y, *to] * first[jnp.maximum(y - 1, 0), *to]
            result = heavy[y, *to] * v[i, q] - (couple + image[y, *to])
            image[y, *to] = result
            total[q] = total[q] + v[i, q] * result
        return tuple(total)

    alpha = divide(rr, patch_total(lax.fori_loop(0, EDGE, image_of, nothing, unroll=4)))

    def residual_of(y, total):
        total = list(total)
        for i, q in PIECES:
            left = first[y, *piece(i, q)] - alpha[q] * image[y, *piece(i, q)]
            total[q] = total[q] + left * left
        return tuple(total)

    new = patch_total(lax.fori_loop(0, EDGE, residual_of, nothing, unroll=8))
    beta = divide(new, rr)

    def direction(y, i, q):
        v = first[y, *piece(i, q)]
        return (v - alpha[q] * image[y, *piece(i, q)]) + beta[q] * v

    for at in PIECES:
        ready[0, *piece(*at)] = direction(0, *at)

    def energy_of(step, total):
        total = list(total)
        v = load(ready, 0)
        for k in range(SLABS):
            y = step * SLABS + k
            v_up = above_x(v)
            v_next = {at: direction(y + 1, *at) for at in PIECES}
            for i in range(STRIPS):
                ups = above_z(strip(v, i))
                for q in range(3):
                    to = piece(i, q)
                    couple = face_x[y, *to] * v_up[i, q]
                    couple = couple + face_y[y + 1, *to] * v_next[i, q]
                    couple = couple + face_z[y, *to] * ups[q]
                    total[q] = total[q] + v[i, q] * (heavy[y, *to] * v[i, q] - 2.0 * couple)
            v = v_next
        for at in PIECES:
            ready[0, *piece(*at)] = v[at]
        return tuple(total)

    energy = lax.fori_loop(0, EDGE // SLABS, energy_of, nothing)
    alpha_next = divide(new, patch_total(energy))
    on_first = [alpha[q] + alpha_next[q] * (1.0 + beta[q]) for q in range(3)]
    on_image = [-(alpha_next[q] * alpha[q]) for q in range(3)]

    ends = [lane < end for end in (48, 96, 16, 64, 112, 32, 80)]

    def gather(c):
        return (
            jnp.where(ends[0], c[0][0], jnp.where(ends[1], c[1][0], c[2][0])),
            jnp.where(
                ends[2],
                c[2][1],
                jnp.where(ends[3], c[3][1], jnp.where(ends[4], c[4][1], c[5][1])),
            ),
            jnp.where(ends[5], c[5][2], jnp.where(ends[6], c[6][2], c[7][2])),
        )

    departures = []
    for group in range(GROUPS):

        def correct(i, _):
            rows = pl.ds(pl.multiple_of(8 * i, 8), 8)
            lines = []
            for j in range(8):
                y = 8 * group + j
                lines.append([
                    on_first[q] * first[y, rows, pl.ds(SIDE * q, SIDE)]
                    + on_image[q] * image[y, rows, pl.ds(SIDE * q, SIDE)]
                    for q in range(3)
                ])
            turned = []
            for k in range(8):
                a, b, c = gather([lines[(p + k) % 8] for p in range(8)])
                far, near = divmod(EDGE * k, SIDE)
                r = [pltpu.roll(v, near, 1) if near else v for v in (a, b, c)]
                r = [r[(q - far) % 3] for q in range(3)]
                before = [r[2], r[0], r[1]]
                if near:
                    r = [jnp.where(lane < near, before[q], r[q]) for q in range(3)]
                turned.append(r)
            for p in range(PATCH_DEV):
                tiles = gather([turned[(j - p) % 8] for j in range(8)])
                for q in range(3):
                    heavy[8 * group + p, rows, pl.ds(SIDE * q, SIDE)] = tiles[q]
            return 0

        lax.fori_loop(0, STRIPS, correct, 0, unroll=True)
        departures.append(
            pltpu.make_async_copy(
                heavy.at[pl.ds(8 * group, PATCH_DEV)],
                out_ref.at[:, :, pl.ds(group * LANES, LANES)],
                leave.at[group],
            )
        )
        departures[-1].start()
    for copy in departures:
        copy.wait()


def solve(half, later):
    cube = pltpu.VMEM((EDGE, EDGE, LANES), F32)
    longer = pltpu.VMEM((EDGE + 1, EDGE, LANES), F32)
    return pl.pallas_call(
        solve_kernel,
        in_specs=[pl.BlockSpec(memory_space=pl.ANY), pl.BlockSpec(memory_space=pltpu.VMEM)],
        out_specs=pl.BlockSpec(memory_space=pl.ANY),
        out_shape=full((PATCH_DEV, EDGE, EDGE * EDGE)),
        scratch_shapes=[
            pltpu.VMEM((EDGE + 2, EDGE, LANES), F32),
            longer,
            longer,
            cube,
            cube,
            longer,
            cube,
            pltpu.VMEM((1, EDGE, LANES), F32),
            pltpu.SemaphoreType.DMA((WIDE // 4, TAPS)),
            pltpu.SemaphoreType.DMA((GROUPS,)),
        ],
        compiler_params=params(40),
        cost_estimate=pl.CostEstimate(
            flops=60 * EDGE**3 * PATCH_DEV, bytes_accessed=32 << 20, transcendentals=0
        ),
        name="solve_patches",
    )(half, later)


def wave_tables():
    index = np.arange(NX, dtype=np.int64)
    angle = (index[:, None] * index[None, :] % NX) * (2.0 * math.pi / NX)
    waves = np.concatenate([np.cos(angle), np.sin(angle)], axis=0)
    return waves.astype(np.float32)


def on_device(noise, spectrum, send_core, recv_source):
    swap = lambda v: lax.all_to_all(v, "wide", split_axis=0, concat_axis=0)
    lines = swap(
        split_rows(noise, send_core.reshape(1, WIDE), recv_source.reshape(1, PATCH_DEV))
    )
    waves = jnp.asarray(wave_tables())
    weights = jnp.concatenate([spectrum, spectrum])[:, None] / NX
    matrix = lax.dot_general(
        waves,
        waves * weights,
        (((0,), (0,)), ((), ())),
        precision=lax.Precision.HIGHEST,
        preferred_element_type=F32,
    )
    count = lax.axis_size("mid")
    pairs = lambda start: [
        edge for i in range(start, count - 1, 2) for edge in ((i, i + 1), (i + 1, i))
    ]
    odd = (lax.axis_index("mid") & 1).reshape(1)
    pair = bf16_pair(matrix)
    parts, crossing, staying, table = filter_exp(odd, pair, lines)
    crossed = lax.ppermute(crossing, "mid", pairs(1))
    stayed = lax.ppermute(staying, "mid", pairs(0))
    back = swap(parts)
    outgoing = windows(table, odd, (crossing, staying))
    outgoing = windows(table, odd, (crossed, stayed), outgoing)
    outgoing, back = lax.optimization_barrier((outgoing, back))
    incoming = swap(outgoing)
    coefficient = join_rows(back)
    cores = table[0, recv_source.reshape(-1), lax.axis_index("wide")]
    later = jnp.repeat((cores >> 5) & 1, EDGE).reshape(1, LANES)
    solved = solve(incoming, later)
    return coefficient, solved.reshape(1, 1, PATCH_DEV, EDGE, EDGE * EDGE)


def solution(mesh):
    in_specs = (P("wide", "mid", None), P(), P("wide", "mid", None), P("wide", "mid", None))
    out_specs = (P("wide", "mid", None), P("wide", "mid", None, None, None))
    return jax.shard_map(
        on_device, mesh=mesh, in_specs=in_specs, out_specs=out_specs, check_vma=False
    )
```

```python
import functools
import math

import jax
import jax.numpy as jnp
import numpy as np
from jax import lax
from jax.experimental import pallas as pl
from jax.experimental.pallas import tpu as pltpu
from jax.sharding import PartitionSpec as P

NX = 512
NZ = 512
CY = 32
CX = 32
CORE = 16
LAYER = 16
WIDE = 16
PATCH_DEV = 8
EDGE = 48
TAPS = 3
LANES = PATCH_DEV * EDGE
SIDE = 128
TILES = NZ // SIDE
ROWS = 2 * TILES * CX
OWNERS = 8
UNROLL = 4
TINY = 1e-06
F32 = jnp.float32


def params(mebibytes):
    return pltpu.CompilerParams(vmem_limit_bytes=mebibytes * 1024 * 1024)


def full(shape):
    return jax.ShapeDtypeStruct(shape, F32)


def exchange(pieces):
    row = lax.broadcasted_iota(jnp.int32, pieces[0].shape, 0)
    pieces = list(pieces)
    for bit in (4, 2, 1):
        upper = (row & bit) != 0
        for i in range(8):
            k = i | bit
            if i == k:
                continue
            pieces[i], pieces[k] = (
                jnp.where(upper, pltpu.roll(pieces[k], bit, 0), pieces[i]),
                jnp.where(upper, pieces[k], pltpu.roll(pieces[i], 8 - bit, 0)),
            )
    return pieces


def split_kernel(in_ref, send_ref, source_ref, out_ref, taken, held, arrive, leave):
    arrivals = [
        pltpu.make_async_copy(
            in_ref.at[:, :, pl.ds(j * SIDE, SIDE)], taken.at[j], arrive.at[j]
        )
        for j in range(TILES)
    ]
    for copy in arrivals:
        copy.start()

    def depart(first, count, sem):
        rows = pl.ds(first, count)
        copy = pltpu.make_async_copy(held.at[:, rows, :], out_ref.at[:, rows, :], sem)
        copy.start()
        return copy

    for w in range(WIDE):
        held[w, ROWS:ROWS + 1, 0:WIDE] = send_ref[...].astype(F32)
        held[w, ROWS + 1:ROWS + 2, 0:PATCH_DEV] = source_ref[...].astype(F32)
    departures = [depart(ROWS, 8, leave.at[2, 0])]
    for j in range(TILES):
        arrivals[j].wait()
        for t in range(2):
            first = (t * TILES + j) * CX
            for x in range(0, CX, 8):
                for y in range(0, WIDE, 8):
                    at = t * WIDE + y
                    pieces = exchange([taken[j, x + i, at:at + 8, :] for i in range(8)])
                    for i in range(8):
                        held[y + i, first + x:first + x + 8, :] = pieces[i]
            departures.append(depart(first, CX, leave.at[t, j]))
    for copy in departures:
        copy.wait()


def split_rows(block, send, source):
    return pl.pallas_call(
        split_kernel,
        in_specs=[
            pl.BlockSpec(memory_space=pl.ANY),
            pl.BlockSpec(memory_space=pltpu.VMEM),
            pl.BlockSpec(memory_space=pltpu.VMEM),
        ],
        out_specs=pl.BlockSpec(memory_space=pl.ANY),
        out_shape=full((WIDE, ROWS + 8, SIDE)),
        scratch_shapes=[
            pltpu.VMEM((TILES, CX, CY, SIDE), F32),
            pltpu.VMEM((WIDE, ROWS + 8, SIDE), F32),
            pltpu.SemaphoreType.DMA((TILES,)),
            pltpu.SemaphoreType.DMA((3, TILES)),
        ],
        compiler_params=params(60),
        cost_estimate=pl.CostEstimate(flops=0, bytes_accessed=8 << 20, transcendentals=0),
        name="split_rows",
    )(block, send, source)


def join_kernel(low_ref, high_ref, out_ref):
    for t, in_ref in enumerate((low_ref, high_ref)):
        for x in range(0, CX, 8):
            for y in range(0, WIDE, 8):
                pieces = exchange([in_ref[y + i, x:x + 8, :] for i in range(8)])
                for i in range(8):
                    out_ref[x + i, t * WIDE + y:t * WIDE + y + 8, :] = pieces[i]


def join_rows(parts):
    return pl.pallas_call(
        join_kernel,
        grid=(TILES,),
        in_specs=[
            pl.BlockSpec((WIDE, CX, SIDE), lambda j: (0, j, 0)),
            pl.BlockSpec((WIDE, CX, SIDE), lambda j: (0, TILES + j, 0)),
        ],
        out_specs=pl.BlockSpec((CX, CY, SIDE), lambda j: (0, 0, j)),
        out_shape=full((CX, CY, NZ)),
        compiler_params=params(12),
        cost_estimate=pl.CostEstimate(flops=0, bytes_accessed=8 << 20, transcendentals=0),
        name="join_rows",
    )(parts, parts)


def pair_kernel(in_ref, high_ref, low_ref):
    value = in_ref[...]
    high = value.astype(jnp.bfloat16)
    high_ref[...] = high
    low_ref[...] = (value - high.astype(F32)).astype(jnp.bfloat16)


def bf16_pair(matrix):
    return pl.pallas_call(
        pair_kernel,
        out_shape=[jax.ShapeDtypeStruct((NX, NX), jnp.bfloat16)] * 2,
        compiler_params=params(60),
        cost_estimate=pl.CostEstimate(flops=0, bytes_accessed=2 << 20, transcendentals=0),
        name="bf16_pair",
    )(matrix)


def filter_kernel(odd_ref, high_ref, low_ref, in_ref, extra_ref, parts_ref, first_ref, second_ref, table_ref):
    for k in range(2):
        table_ref[k] = extra_ref[:, k, :].astype(jnp.int32)
    lines = jnp.concatenate(
        [in_ref[:, k * CX:(k + 1) * CX, :].reshape(NX, SIDE) for k in range(TILES)], axis=1
    )
    high = lines.astype(jnp.bfloat16)
    low = (lines - high.astype(F32)).astype(jnp.bfloat16)
    dot = lambda a, b: jnp.dot(a, b, preferred_element_type=F32)
    small = dot(high_ref[...], low) + dot(low_ref[...], high)
    value = jnp.exp(dot(high_ref[...], high) + small)
    sides = [value[:, k * SIDE:(k + 1) * SIDE] for k in range(TILES)]
    for k in range(TILES):
        parts_ref[:, k * CX:(k + 1) * CX, :] = sides[k].reshape(WIDE, CX, SIDE)

    def plane(ref):
        for k in range(TILES):
            ref[k] = 0.5 * sides[k]

    pl.when(pl.program_id(0) == 0)(lambda: plane(first_ref))
    pl.when(pl.program_id(0) == 1)(lambda: plane(second_ref))


def filter_exp(odd, pair, lines):
    whole = pl.BlockSpec((NX, NX), lambda i, odd: (0, 0))
    block = pl.BlockSpec(
        (WIDE, TILES * CX, SIDE), lambda i, odd: (0, i ^ odd[0], 0)
    )
    return pl.pallas_call(
        filter_kernel,
        grid_spec=pltpu.PrefetchScalarGridSpec(
            num_scalar_prefetch=1,
            grid=(2,),
            in_specs=[
                whole,
                whole,
                block,
                pl.BlockSpec((WIDE, 8, SIDE), lambda i, odd: (0, ROWS // 8, 0)),
            ],
            out_specs=[
                block,
                pl.BlockSpec((TILES, NX, SIDE), lambda i, odd: (0, 0, 0)),
                pl.BlockSpec((TILES, NX, SIDE), lambda i, odd: (0, 0, 0)),
                pl.BlockSpec((2, WIDE, SIDE), lambda i, odd: (0, 0, 0)),
            ],
        ),
        out_shape=[
            full((WIDE, ROWS, SIDE)),
            full((TILES, NX, SIDE)),
            full((TILES, NX, SIDE)),
            jax.ShapeDtypeStruct((2, WIDE, SIDE), jnp.int32),
        ],
        compiler_params=params(60),
        cost_estimate=pl.CostEstimate(
            flops=12 * NX * NX * NZ, bytes_accessed=8 << 20, transcendentals=2 * NX * NZ
        ),
        name="filter_exp",
    )(odd, *pair, lines, lines)


def window_kernel(slots, table_ref, odd_ref, *refs):
    low_ref, high_ref = refs[:2]
    out_ref, held, sems = refs[-3:]
    step = pl.program_id(0)

    @pl.when(step == 0)
    def _():
        copies = [
            pltpu.make_async_copy(
                src.at[j], held.at[t, 1 + j, pl.ds(LAYER, NX), :], sems.at[t, j]
            )
            for t, src in enumerate((low_ref, high_ref))
            for j in range(TILES)
        ]
        for copy in copies:
            copy.start()
        side = jnp.zeros((NX + 2 * LAYER, SIDE), F32)
        for t in range(2):
            held[t, 0] = side
            held[t, TILES + 1] = side
            for j in range(TILES):
                held[t, 1 + j, 0:LAYER, :] = side[:LAYER]
                held[t, 1 + j, LAYER + NX:, :] = side[:LAYER]
        for copy in copies:
            copy.wait()

    lane = lax.broadcasted_iota(jnp.int32, (EDGE, SIDE), 1)

    def one_owner(k, _):
        owner = step * OWNERS + k
        places = []
        for p in range(PATCH_DEV):
            source = table_ref[1, owner, p]
            core = jnp.maximum(table_ref[0, source, owner], 0)
            x_at = source * CX + (core >> 6) * CORE
            z_at = (core & 31) * CORE + (SIDE - LAYER)
            offset = z_at & (SIDE - 1)
            turn = ((p * EDGE) % SIDE - offset) & (SIDE - 1)
            places.append((pl.multiple_of(x_at, CORE), (core >> 5) & 1, z_at >> 7, offset, turn))
        for t in range(slots):
            tiles = [None] * 3
            for p, (x_at, t_at, tile, offset, turn) in enumerate(places):
                plane = (t if slots == 2 else t_at) ^ odd_ref[0]
                rows = pl.ds(x_at, EDGE)
                near = held[plane, tile, rows, :]
                far = held[plane, tile + 1, rows, :]
                moved = pltpu.roll(jnp.where(lane >= offset, near, far), turn, 1)
                at = (p * EDGE) % SIDE
                q = (p * EDGE) // SIDE
                tiles[q] = moved if at == 0 else jnp.where(lane >= at, moved, tiles[q])
                if at + EDGE > SIDE:
                    tiles[q + 1] = moved
            for q in range(3):
                out_ref[k, t * EDGE:(t + 1) * EDGE, q * SIDE:(q + 1) * SIDE] = tiles[q]
        return 0

    lax.fori_loop(0, OWNERS, one_owner, 0, unroll=UNROLL)


def windows(table, odd, planes, *others):
    slots = 1 if others else 2
    at = 2 if others else 0
    return pl.pallas_call(
        functools.partial(window_kernel, slots),
        grid_spec=pltpu.PrefetchScalarGridSpec(
            num_scalar_prefetch=2,
            grid=(WIDE // OWNERS,),
            in_specs=[pl.BlockSpec(memory_space=pl.ANY)] * (2 + len(others)),
            out_specs=pl.BlockSpec((OWNERS, slots * EDGE, LANES), lambda d, table, odd: (d, at, 0)),
            scratch_shapes=[
                pltpu.VMEM((2, TILES + 2, NX + 2 * LAYER, SIDE), F32),
                pltpu.SemaphoreType.DMA((2, TILES)),
            ],
        ),
        out_shape=full((WIDE, TAPS * EDGE, LANES)),
        input_output_aliases={4: 0} if others else {},
        compiler_params=params(58 if others else 60),
        cost_estimate=pl.CostEstimate(
            flops=0, bytes_accessed=slots * (6 << 20), transcendentals=0
        ),
        name="patch_windows",
    )(table, odd, *planes, *others)


STRIPS = EDGE // 8
SLABS = 4
GROUPS = EDGE // 8
PIECES = [(i, q) for i in range(STRIPS) for q in range(3)]


def piece(i, q):
    return (pl.ds(8 * i, 8), pl.ds(SIDE * q, SIDE))


def solve_kernel(
    half_ref, later_ref, out_ref, half, first, image, heavy, face_x, face_y, face_z, ready, arrive, leave
):
    arrivals = [
        [
            pltpu.make_async_copy(
                half_ref.at[pl.ds(4 * g, 4), pl.ds(t * EDGE, EDGE), :],
                (heavy, face_x, face_y)[t].at[pl.ds(4 * g, 4)],
                arrive.at[g, t],
            )
            for t in range(TAPS)
        ]
        for g in range(WIDE // 4)
    ]
    for group in arrivals:
        for copy in group:
            copy.start()
    none = jnp.zeros((8, SIDE), F32)
    for at in PIECES:
        half[0, *piece(*at)] = none
        half[EDGE + 1, *piece(*at)] = none
        first[EDGE, *piece(*at)] = none
        image[EDGE, *piece(*at)] = none

    row = lax.broadcasted_iota(jnp.int32, (8, SIDE), 0)
    lane = lax.broadcasted_iota(jnp.int32, (8, SIDE), 1)
    row_low, row_high = row == 0, row == 7
    lane_low, lane_high = lane == 0, lane == SIDE - 1
    depth = []
    for q in range(3):
        place = lane + q * SIDE
        depth.append(place - ((place * 1366) >> 16) * EDGE)
    z_low = [d == 0 for d in depth]
    z_high = [d == EDGE - 1 for d in depth]

    def above_x(slab):
        turned = {at: pltpu.roll(slab[at], 7, 0) for at in PIECES}
        return {
            (i, q): jnp.where(row_high, turned[i + 1, q] if i < STRIPS - 1 else 0.0, turned[i, q])
            for i, q in PIECES
        }

    def below_x(slab):
        turned = {at: pltpu.roll(slab[at], 1, 0) for at in PIECES}
        return {
            (i, q): jnp.where(row_low, turned[i - 1, q] if i else 0.0, turned[i, q])
            for i, q in PIECES
        }

    def above_z(strip):
        turned = [pltpu.roll(v, SIDE - 1, 1) for v in strip]
        return [
            jnp.where(lane_high, turned[1], turned[0]),
            jnp.where(lane_high, turned[2], turned[1]),
            turned[2],
        ]

    def below_z(strip):
        turned = [pltpu.roll(v, 1, 1) for v in strip]
        return [
            jnp.where(lane_low, 0.0, turned[0]),
            jnp.where(lane_low, turned[0], turned[1]),
            jnp.where(lane_low, turned[1], turned[2]),
        ]

    def load(ref, y):
        return {at: ref[y, *piece(*at)] for at in PIECES}

    def strip(slab, i):
        return [slab[i, q] for q in range(3)]

    same = jnp.where(
        ((lax.broadcasted_iota(jnp.int32, (LANES, LANES), 0) * 1366) >> 16)
        == ((lax.broadcasted_iota(jnp.int32, (LANES, LANES), 1) * 1366) >> 16),
        1.0,
        0.0,
    ).astype(jnp.bfloat16)

    def patch_total(parts):
        part = jnp.concatenate(parts, axis=1)
        high = part.astype(jnp.bfloat16).astype(F32)
        middle = (part - high).astype(jnp.bfloat16).astype(F32)
        low = part - high - middle
        stack = jnp.concatenate([high, middle, low, jnp.zeros_like(low)], axis=0)
        spread = jnp.dot(stack.astype(jnp.bfloat16), same, preferred_element_type=F32)
        total = jnp.sum(spread, axis=0, keepdims=True)
        return [
            jnp.broadcast_to(total[:, SIDE * q:SIDE * (q + 1)], (8, SIDE)) for q in range(3)
        ]

    def divide(top, bottom):
        return [t / (b + TINY) for t, b in zip(top, bottom)]

    nothing = (none, none, none)

    in_order = [
        jnp.broadcast_to(later_ref[:, SIDE * q:SIDE * (q + 1)], (8, SIDE)) != 0 for q in range(3)
    ]

    def arrange(w, _):
        for i, q in PIECES:
            at = piece(i, q)
            a, b, c = heavy[w, *at], face_x[w, *at], face_y[w, *at]
            half[1 + w, *at] = jnp.where(in_order[q], a, c)
            half[1 + WIDE + w, *at] = jnp.where(in_order[q], b, a)
            half[1 + 2 * WIDE + w, *at] = jnp.where(in_order[q], c, b)
        return 0

    def faces_of(y, rr):
        rr = list(rr)
        h = load(half, y + 1)
        h_up = above_x(h)
        h_down = below_x(h)
        deep_up, deep_down = {}, {}
        for i in range(STRIPS):
            ups, downs = above_z(strip(h, i)), below_z(strip(h, i))
            for q in range(3):
                deep_up[i, q] = jnp.where(z_high[q], 0.0, ups[q])
                deep_down[i, q] = jnp.where(z_low[q], 0.0, downs[q])
        up_up, up_down = above_x(deep_up), below_x(deep_up)
        down_up, down_down = above_x(deep_down), below_x(deep_down)
        for i, q in PIECES:
            here, to = h[i, q], piece(i, q)
            z_up, z_down = deep_up[i, q], deep_down[i, q]
            v = h_up[i, q] - h_down[i, q]
            y_up = half[y + 2, *to]
            y_down = half[y, *to]
            across = here + h_up[i, q]
            if i == STRIPS - 1:
                across = jnp.where(row_high, 0.0, across)
            deep = here + z_up
            heavy[y, *to] = (
                (1.0 + 6.0 * here) + (h_up[i, q] + h_down[i, q])
                + ((y_up + y_down) + (z_up + z_down))
            )
            face_x[y, *to] = across
            face_y[y + 1, *to] = here + y_up
            face_z[y, *to] = jnp.where(z_high[q], 0.0, deep)
            first[y, *to] = v
            image[y, *to] = deep * (up_up[i, q] - up_down[i, q]) + (here + z_down) * (
                down_up[i, q] - down_down[i, q]
            )
            rr[q] = rr[q] + v * v
        return tuple(rr)

    def span(start, count, rr):
        def body(t, rr):
            for k in range(count):
                rr = faces_of(t * WIDE + start + k, rr)
            return rr

        return lax.fori_loop(0, TAPS, body, rr)

    rr = nothing
    for g, group in enumerate(arrivals):
        for copy in group:
            copy.wait()
        lax.fori_loop(4 * g, 4 * g + 4, arrange, 0, unroll=2)
        rr = span(4 * g - 1, 4, rr) if g else span(1, 2, rr)
    for y in (0, 15, 16, 31, 32, 47):
        rr = faces_of(y, rr)
    for at in PIECES:
        face_y[0, *piece(*at)] = none
        face_y[EDGE, *piece(*at)] = none
    rr = patch_total(rr)

    def image_of(y, total):
        total = list(total)
        v = load(first, y)
        v_up = above_x(v)
        across = load(face_x, y)
        from_x = below_x({at: across[at] * v[at] for at in PIECES})
        for i, q in PIECES:
            to = piece(i, q)
            couple = across[i, q] * v_up[i, q] + from_x[i, q]
            couple = couple + face_y[y + 1, *to] * first[y + 1, *to]
            couple = couple + face_y[y, *to] * first[jnp.maximum(y - 1, 0), *to]
            result = heavy[y, *to] * v[i, q] - (couple + image[y, *to])
            image[y, *to] = result
            total[q] = total[q] + v[i, q] * result
        return tuple(total)

    alpha = divide(rr, patch_total(lax.fori_loop(0, EDGE, image_of, nothing, unroll=4)))

    def residual_of(y, total):
        total = list(total)
        for i, q in PIECES:
            left = first[y, *piece(i, q)] - alpha[q] * image[y, *piece(i, q)]
            total[q] = total[q] + left * left
        return tuple(total)

    new = patch_total(lax.fori_loop(0, EDGE, residual_of, nothing, unroll=8))
    beta = divide(new, rr)

    def direction(y, i, q):
        v = first[y, *piece(i, q)]
        return (v - alpha[q] * image[y, *piece(i, q)]) + beta[q] * v

    for at in PIECES:
        ready[0, *piece(*at)] = direction(0, *at)

    def energy_of(step, total):
        total = list(total)
        v = load(ready, 0)
        for k in range(SLABS):
            y = step * SLABS + k
            v_up = above_x(v)
            v_next = {at: direction(y + 1, *at) for at in PIECES}
            for i in range(STRIPS):
                ups = above_z(strip(v, i))
                for q in range(3):
                    to = piece(i, q)
                    couple = face_x[y, *to] * v_up[i, q]
                    couple = couple + face_y[y + 1, *to] * v_next[i, q]
                    couple = couple + face_z[y, *to] * ups[q]
                    total[q] = total[q] + v[i, q] * (heavy[y, *to] * v[i, q] - 2.0 * couple)
            v = v_next
        for at in PIECES:
            ready[0, *piece(*at)] = v[at]
        return tuple(total)

    energy = lax.fori_loop(0, EDGE // SLABS, energy_of, nothing)
    alpha_next = divide(new, patch_total(energy))
    on_first = [alpha[q] + alpha_next[q] * (1.0 + beta[q]) for q in range(3)]
    on_image = [-(alpha_next[q] * alpha[q]) for q in range(3)]

    ends = [lane < end for end in (48, 96, 16, 64, 112, 32, 80)]

    def gather(c):
        return (
            jnp.where(ends[0], c[0][0], jnp.where(ends[1], c[1][0], c[2][0])),
            jnp.where(
                ends[2],
                c[2][1],
                jnp.where(ends[3], c[3][1], jnp.where(ends[4], c[4][1], c[5][1])),
            ),
            jnp.where(ends[5], c[5][2], jnp.where(ends[6], c[6][2], c[7][2])),
        )

    departures = []
    for group in range(GROUPS):

        def correct(i, _):
            rows = pl.ds(pl.multiple_of(8 * i, 8), 8)
            lines = []
            for j in range(8):
                y = 8 * group + j
                lines.append([
                    on_first[q] * first[y, rows, pl.ds(SIDE * q, SIDE)]
                    + on_image[q] * image[y, rows, pl.ds(SIDE * q, SIDE)]
                    for q in range(3)
                ])
            turned = []
            for k in range(8):
                a, b, c = gather([lines[(p + k) % 8] for p in range(8)])
                far, near = divmod(EDGE * k, SIDE)
                r = [pltpu.roll(v, near, 1) if near else v for v in (a, b, c)]
                r = [r[(q - far) % 3] for q in range(3)]
                before = [r[2], r[0], r[1]]
                if near:
                    r = [jnp.where(lane < near, before[q], r[q]) for q in range(3)]
                turned.append(r)
            for p in range(PATCH_DEV):
                tiles = gather([turned[(j - p) % 8] for j in range(8)])
                for q in range(3):
                    heavy[8 * group + p, rows, pl.ds(SIDE * q, SIDE)] = tiles[q]
            return 0

        lax.fori_loop(0, STRIPS, correct, 0, unroll=True)
        departures.append(
            pltpu.make_async_copy(
                heavy.at[pl.ds(8 * group, PATCH_DEV)],
                out_ref.at[:, :, pl.ds(group * LANES, LANES)],
                leave.at[group],
            )
        )
        departures[-1].start()
    for copy in departures:
        copy.wait()


def solve(half, later):
    cube = pltpu.VMEM((EDGE, EDGE, LANES), F32)
    longer = pltpu.VMEM((EDGE + 1, EDGE, LANES), F32)
    return pl.pallas_call(
        solve_kernel,
        in_specs=[pl.BlockSpec(memory_space=pl.ANY), pl.BlockSpec(memory_space=pltpu.VMEM)],
        out_specs=pl.BlockSpec(memory_space=pl.ANY),
        out_shape=full((PATCH_DEV, EDGE, EDGE * EDGE)),
        scratch_shapes=[
            pltpu.VMEM((EDGE + 2, EDGE, LANES), F32),
            longer,
            longer,
            cube,
            cube,
            longer,
            cube,
            pltpu.VMEM((1, EDGE, LANES), F32),
            pltpu.SemaphoreType.DMA((WIDE // 4, TAPS)),
            pltpu.SemaphoreType.DMA((GROUPS,)),
        ],
        compiler_params=params(40),
        cost_estimate=pl.CostEstimate(
            flops=60 * EDGE**3 * PATCH_DEV, bytes_accessed=32 << 20, transcendentals=0
        ),
        name="solve_patches",
    )(half, later)


def wave_tables():
    index = np.arange(NX, dtype=np.int64)
    angle = (index[:, None] * index[None, :] % NX) * (2.0 * math.pi / NX)
    waves = np.concatenate([np.cos(angle), np.sin(angle)], axis=0)
    return waves.astype(np.float32)


def on_device(noise, spectrum, send_core, recv_source):
    swap = lambda v: lax.all_to_all(v, "wide", split_axis=0, concat_axis=0)
    lines = swap(
        split_rows(noise, send_core.reshape(1, WIDE), recv_source.reshape(1, PATCH_DEV))
    )
    waves = jnp.asarray(wave_tables())
    weights = jnp.concatenate([spectrum, spectrum])[:, None] / NX
    matrix = lax.dot_general(
        waves,
        waves * weights,
        (((0,), (0,)), ((), ())),
        precision=lax.Precision.HIGHEST,
        preferred_element_type=F32,
    )
    count = lax.axis_size("mid")
    pairs = lambda start: [
        edge for i in range(start, count - 1, 2) for edge in ((i, i + 1), (i + 1, i))
    ]
    odd = (lax.axis_index("mid") & 1).reshape(1)
    pair = bf16_pair(matrix)
    parts, crossing, staying, table = filter_exp(odd, pair, lines)
    crossed = lax.ppermute(crossing, "mid", pairs(1))
    stayed = lax.ppermute(staying, "mid", pairs(0))
    back = swap(parts)
    outgoing = windows(table, odd, (crossing, staying))
    outgoing = windows(table, odd, (crossed, stayed), outgoing)
    outgoing, back = lax.optimization_barrier((outgoing, back))
    incoming = swap(outgoing)
    coefficient = join_rows(back)
    cores = table[0, recv_source.reshape(-1), lax.axis_index("wide")]
    later = jnp.repeat((cores >> 5) & 1, EDGE).reshape(1, LANES)
    solved = solve(incoming, later)
    return coefficient, solved.reshape(1, 1, PATCH_DEV, EDGE, EDGE * EDGE)


def solution(mesh):
    in_specs = (P("wide", "mid", None), P(), P("wide", "mid", None), P("wide", "mid", None))
    out_specs = (P("wide", "mid", None), P("wide", "mid", None, None, None))
    return jax.shard_map(
        on_device, mesh=mesh, in_specs=in_specs, out_specs=out_specs, check_vma=False
    )
```
